32 devices in a mesh: tp: 4 (over y, x), cp: 4 (over z), dp: 2 (over core).
Axes of the slice: x: 2, y: 2, z: 4, core: 2. Of those that a mesh axis runs over, the one named last changes fastest.
Arguments:
- tokens: bfloat16 [4096, 2, 768], P(('cp', 'tp'), 'dp'), may hold values from -6 to 6
- segment_ids: int32 [4096, 2], P('cp', 'dp'), may hold values from 0 to 2, as said below
- ln1_gain: float32 [768], replicated, may hold values from 0.5 to 1.5
- ln1_bias: float32 [768], replicated, may hold values from -1.75 to 1.75
- w_qkv: bfloat16 [768, 3, 768], P(None, None, 'tp'), may hold values from -0.21875 to 0.21875
- b_qkv: float32 [3, 768], P(None, 'tp'), may hold values from -1.75 to 1.75
- w_feat: bfloat16 [12, 64, 64], P('tp'), may hold values from -1.5 to 1.5
- b_feat: float32 [12, 64], P('tp'), may hold values from -3 to 3
- output_weight: bfloat16 [768, 768], P('tp'), may hold values from -3 to 3
- b_out: float32 [768], replicated, may hold values from -1.75 to 1.75
- ln2_gain: float32 [768], replicated, may hold values from 0.5 to 1.5
- ln2_bias: float32 [768], replicated, may hold values from -1.75 to 1.75
- w_up: bfloat16 [768, 3072], P(None, 'tp'), may hold values from -0.21875 to 0.21875
- b_up: float32 [3072], P('tp'), may hold values from -1.75 to 1.75
- w_down: bfloat16 [3072, 768], P('tp'), may hold values from -0.109375 to 0.109375
- b_down: float32 [768], replicated, may hold values from -1.75 to 1.75
- cotangent: bfloat16 [4096, 2, 768], P(('cp', 'tp'), 'dp'), may hold values from -6 to 6
Outputs:
- out_tokens: bfloat16 [4096, 2, 768], P(('cp', 'tp'), 'dp')
- d_tokens: float32 [4096, 2, 768], P(('cp', 'tp'), 'dp')
- d_ln1_gain: float32 [768], replicated
- d_ln1_bias: float32 [768], replicated
- d_w_qkv: float32 [768, 3, 768], P(None, None, 'tp')
- d_b_qkv: float32 [3, 768], P(None, 'tp')
- d_w_feat: float32 [12, 64, 64], P('tp')
- d_b_feat: float32 [12, 64], P('tp')
- d_w_out: float32 [768, 768], P('tp')
- d_b_out: float32 [768], replicated
- d_ln2_gain: float32 [768], replicated
- d_ln2_bias: float32 [768], replicated
- d_w_up: float32 [768, 3072], P(None, 'tp')
- d_b_up: float32 [3072], P('tp')
- d_w_down: float32 [3072, 768], P('tp')
- d_b_down: float32 [768], replicated
The draws below stay inside these ranges and needn't reach their ends.
Inputs may be any that keep to these rules, and one draw needn't show every extreme that they name: `segment_ids`: in each packed row the ids start at 0 and never fall; they rise by one at one position of 1 to 1023 and again at one position of 3073 to 4095.
All inputs are finite; a program needn't handle non-finite values.
Results may differ from the reference program's by a relative error of at most 0.012.
The reference program's roundings to bfloat16 on the way count: a program that leaves them out, or rounds other values in their place, can miss the bound.
Values may be sent and summed in bfloat16 or wider, within the bound.
No kernel may reach another device: no remote copies, remote signals or barrier semaphores. Data moves between devices by JAX's collectives and lax.ppermute only.
A program may use at most 128 MiB of HBM per device.

```python
import jax
import jax.numpy as jnp
from jax import lax

D = 768
HEADS = 12
HD = 64
FF = 3072
ROW_DEV = 1024
LEN = 4096
BATCH = 2


def draw_segment_ids(key, part):
    key = jax.random.fold_in(key, 7)
    first_key, second_key = jax.random.split(key)
    first_cut = jax.random.randint(first_key, (1, BATCH), 1, ROW_DEV, dtype=jnp.int32)
    second_cut = jax.random.randint(second_key, (1, BATCH), LEN - ROW_DEV + 1, LEN, dtype=jnp.int32)
    positions = jnp.arange(LEN, dtype=jnp.int32)[:, None]
    return (positions >= first_cut).astype(jnp.int32) + (positions >= second_cut).astype(jnp.int32)


def block_scale(stream_key, dims, cuts, smallest, largest):
    factor_of = 1.0
    for axis_at, blocks in cuts:
        steps = jax.random.uniform(jax.random.fold_in(jax.random.fold_in(stream_key, 6), axis_at), (blocks,), jnp.float32, smallest / len(cuts), largest / len(cuts))
        factor_of = factor_of * jnp.repeat(jnp.exp(steps), dims[axis_at] // blocks).reshape((-1,) + (1,) * (len(dims) - 1 - axis_at))
    return factor_of


def bell_draw(stream_key, extent, scale, reach, cuts=(), kind=jnp.bfloat16):
    drawn = scale * jax.random.normal(stream_key, extent, jnp.float32)
    if cuts:
        drawn = drawn * block_scale(stream_key, extent, cuts, -0.22, 0.18)
    return jnp.clip(drawn, -reach, reach).astype(kind)


def setup_inputs(seed: int = 0) -> dict:
    keys = jax.random.split(jax.random.key(seed), 18)
    return {
        "tokens": bell_draw(keys[0], (LEN, BATCH, D), 1.0, 6.0, ((0, 16), (1, 2))),
        "segment_ids": draw_segment_ids(jax.random.fold_in(keys[17], 71), 0),
        "ln1_gain": jnp.clip(1.0 + 0.1 * jax.random.normal(keys[2], (D,), jnp.float32), 0.5, 1.5),
        "ln1_bias": bell_draw(keys[3], (D,), 0.3, 1.75, (), jnp.float32),
        "w_qkv": bell_draw(keys[4], (D, 3, D), D ** -0.5, 0.21875, ((2, 4),)),
        "b_qkv": bell_draw(keys[5], (3, D), 0.3, 1.75, ((1, 4),), jnp.float32),
        "w_feat": bell_draw(keys[6], (HEADS, HD, HD), (HD // 4) ** -0.5, 1.5, ((0, 4),)),
        "b_feat": bell_draw(keys[7], (HEADS, HD), 0.5, 3.0, ((0, 4),), jnp.float32),
        "output_weight": bell_draw(keys[8], (D, D), 4 ** -0.5, 3.0, ((0, 4),)),
        "b_out": bell_draw(keys[9], (D,), 0.3, 1.75, (), jnp.float32),
        "ln2_gain": jnp.clip(1.0 + 0.1 * jax.random.normal(keys[10], (D,), jnp.float32), 0.5, 1.5),
        "ln2_bias": bell_draw(keys[11], (D,), 0.3, 1.75, (), jnp.float32),
        "w_up": bell_draw(keys[12], (D, FF), D ** -0.5, 0.21875, ((1, 4),)),
        "b_up": bell_draw(keys[13], (FF,), 0.3, 1.75, ((0, 4),), jnp.float32),
        "w_down": bell_draw(keys[14], (FF, D), FF ** -0.5, 0.109375, ((0, 4),)),
        "b_down": bell_draw(keys[15], (D,), 0.3, 1.75, (), jnp.float32),
        "cotangent": bell_draw(keys[16], (LEN, BATCH, D), 1.0, 6.0, ((0, 16), (1, 2))),
    }


FULL_PRECISION = lax.Precision.HIGHEST
epsilon = 1e-05

@jax.custom_vjp
def low(v):
    return lax.optimization_barrier(v.astype(jnp.bfloat16)).astype(jnp.float32)

@jax.custom_vjp
def low_back(v):
    return v

def low_keep(v):
    return (low(v), None)

def low_pass(kept, grad):
    return (grad,)

def back_keep(v):
    return (v, None)

def back_low(kept, grad):
    return (low(grad),)
low.defvjp(low_keep, low_pass)
low_back.defvjp(back_keep, back_low)

def norm_rows(values, gain_vec, bias_vec):
    centred = values - lax.optimization_barrier(jnp.mean(values, axis=-1, keepdims=True))
    variance = lax.optimization_barrier(jnp.mean(centred * centred, axis=-1, keepdims=True))
    return centred * lax.rsqrt(variance + epsilon) * gain_vec + bias_vec

def feature_map(inputs, feat_weight, feat_bias):
    logits = jnp.einsum('lhd,hde->lhe', inputs, feat_weight, precision=FULL_PRECISION) + feat_bias
    return jax.nn.softmax(jnp.concatenate([logits, -logits], axis=-1), axis=-1)

def attend(query_feat, key_features_mapped, values, seg_row):
    block_len = min(512, LEN)
    positions = jnp.arange(LEN, dtype=jnp.int32)

    def one_block(row_start):
        query_block = lax.dynamic_slice_in_dim(query_feat, row_start, block_len, 0)
        attention_scores = jnp.einsum('lwa,zwa->wlz', query_block, key_features_mapped, precision=FULL_PRECISION)
        query_pos = row_start + jnp.arange(block_len, dtype=jnp.int32)
        query_seg = lax.dynamic_slice_in_dim(seg_row, row_start, block_len, 0)
        allowed = (positions[None, :] <= query_pos[:, None]) & (seg_row[None, :] == query_seg[:, None])
        weights = jnp.where(allowed[None], attention_scores, 0.0)
        numerator = jnp.einsum('hqk,khd->qhd', weights, values, precision=FULL_PRECISION)
        denominator = lax.optimization_barrier(jnp.sum(weights, axis=-1))
        return numerator / jnp.transpose(denominator)[:, :, None]
    starts = (jnp.arange(LEN // block_len, dtype=jnp.int32) * block_len).astype(jnp.int32)
    blocks = lax.map(jax.checkpoint(one_block), starts)
    return blocks.reshape(LEN, HEADS, HD)

def forward(x_row, seg_row, params):
    ln1_gain, ln1_bias, w_qkv, b_qkv, w_feat, b_feat, output_weight, b_out, ln2_gain, ln2_bias, w_up, b_up, w_down, b_down = params
    normed = low(norm_rows(x_row, ln1_gain, ln1_bias))
    projected = jnp.einsum('ld,dcm->lcm', normed, w_qkv, precision=FULL_PRECISION) + b_qkv
    projected = low(low_back(projected))
    heads_view = projected.reshape(LEN, 3, HEADS, HD)
    query_feat = low(feature_map(heads_view[:, 0], w_feat, b_feat))
    key_features_mapped = low(feature_map(heads_view[:, 1], w_feat, b_feat))
    mixed_heads = low(low_back(attend(query_feat, key_features_mapped, heads_view[:, 2], seg_row)))
    mixed_heads = mixed_heads.reshape(LEN, D)
    branch = low_back(jnp.dot(mixed_heads, output_weight, precision=FULL_PRECISION) + b_out)
    middle = x_row + branch
    normed_two = low(norm_rows(middle, ln2_gain, ln2_bias))
    hidden_pre = low_back(jnp.dot(normed_two, w_up, precision=FULL_PRECISION) + b_up)
    hidden = low(jax.nn.gelu(hidden_pre, approximate=True))
    return middle + jnp.dot(hidden, w_down, precision=FULL_PRECISION) + b_down

def reference(tokens, segment_ids, ln1_gain, ln1_bias, w_qkv, b_qkv, w_feat, b_feat, output_weight, b_out, ln2_gain, ln2_bias, w_up, b_up, w_down, b_down, cotangent):
    params = tuple((member.astype(jnp.float32) for member in (ln1_gain, ln1_bias, w_qkv, b_qkv, w_feat, b_feat, output_weight, b_out, ln2_gain, ln2_bias, w_up, b_up, w_down, b_down)))
    rows_in = jnp.transpose(tokens.astype(jnp.float32), (1, 0, 2))
    cot_in = jnp.transpose(cotangent.astype(jnp.float32), (1, 0, 2))
    seg_in = jnp.transpose(segment_ids)

    def one_row(totals, row_items):
        x_row, seg_row, cot_row = row_items

        def apply_row(row_vals, weight_set):
            return forward(row_vals, seg_row, weight_set)
        outputs, pullback = jax.vjp(apply_row, x_row, params)
        grad_x, grad_params = pullback(cot_row)
        return (jax.tree.map(jnp.add, totals, grad_params), (outputs, grad_x))
    zero_grads = tuple((jnp.zeros_like(member) for member in params))
    totals, (outs_rows, grad_rows) = lax.scan(one_row, zero_grads, (rows_in, seg_in, cot_in))
    out_tokens = jnp.transpose(outs_rows, (1, 0, 2)).astype(jnp.bfloat16)
    d_tokens = jnp.transpose(grad_rows, (1, 0, 2))
    return (out_tokens, d_tokens, totals[0], totals[1], totals[2], totals[3], totals[4], totals[5], totals[6], totals[7], totals[8], totals[9], totals[10], totals[11], totals[12], totals[13])
```

```python
import functools
import math

import jax
import jax.numpy as jnp
from jax import lax
from jax.experimental import pallas as pl
from jax.experimental.pallas import tpu as pltpu
from jax.sharding import PartitionSpec as P

f32 = jnp.float32
bf16 = jnp.bfloat16
EPS = 1e-05
ROOT = math.sqrt(2.0 / math.pi)
VMEM_LIMIT = 48 * 1024 * 1024


def nn(a, b):
    return jnp.dot(a, b, preferred_element_type=f32)


def nt(a, b):
    return lax.dot_general(a, b, (((1,), (1,)), ((), ())), preferred_element_type=f32)


def tn(a, b):
    return lax.dot_general(a, b, (((0,), (0,)), ((), ())), preferred_element_type=f32)


def call(kernel, outs, args, smem=0, scratch=(), flops=1, name=None):
    specs = [pl.BlockSpec(memory_space=pltpu.SMEM)] * smem
    specs += [pl.BlockSpec(memory_space=pltpu.VMEM)] * (len(args) - smem)
    out_shape = [jax.ShapeDtypeStruct(shape, kind) for shape, kind in outs]
    moved = sum(math.prod(o.shape) * o.dtype.itemsize for o in out_shape)
    moved += sum(math.prod(a.shape) * a.dtype.itemsize for a in args)
    return pl.pallas_call(
        kernel,
        out_shape=out_shape,
        in_specs=specs,
        out_specs=[pl.BlockSpec(memory_space=pltpu.VMEM)] * len(outs),
        scratch_shapes=list(scratch),
        compiler_params=pltpu.CompilerParams(vmem_limit_bytes=VMEM_LIMIT),
        cost_estimate=pl.CostEstimate(flops=flops, bytes_accessed=moved, transcendentals=0),
        name=name,
    )(*args)


def lanes():
    return lax.broadcasted_iota(jnp.int32, (1, 128), 1)


def half_turn(v):
    return pltpu.roll(v, 64, 1)


def norm_stats(v):
    centred = v - jnp.mean(v, axis=-1, keepdims=True)
    inv = lax.rsqrt(jnp.mean(centred * centred, axis=-1, keepdims=True) + EPS)
    return centred * inv, inv


def ln_one_kernel(tok, gain, bias, out):
    hat, _ = norm_stats(tok[...].astype(f32))
    out[...] = (hat * gain[...] + bias[...]).astype(bf16)


def encode(pay, tops, norms):
    for g in range(6):
        pay[g * 64 : g * 64 + 64, :] = tops[g].astype(bf16)
    row = lax.broadcasted_iota(jnp.int32, (16, 128), 0)
    for s in range(2):
        block = jnp.zeros((16, 128), f32)
        for h in range(3):
            n = norms[3 * s + h]
            high = n.astype(bf16).astype(f32)
            block = jnp.where(row == h, high, block)
            block = jnp.where(row == 3 + h, n - high, block)
        pay[384 + 16 * s : 400 + 16 * s, :] = block.astype(bf16)


def decode(pay, swap=False):
    tops, norms = [], []
    blocks = [pay[384 + 16 * s : 400 + 16 * s, :].astype(f32) for s in range(2)]
    for s in range(2):
        t = 1 - s if swap else s
        for h in range(3):
            g = 3 * t + h
            tops.append(pay[g * 64 : g * 64 + 64, :].astype(f32))
            norms.append(blocks[t][h : h + 1, :] + blocks[t][3 + h : 4 + h, :])
    return tops, norms


PAY = (416, 128)


def combine(parts):
    tops = [sum(f * p[0][g] for f, p in parts) for g in range(6)]
    norms = [sum(f * p[1][g] for f, p in parts) for g in range(6)]
    return tops, norms


def qkv_kernel(
    idx, seg, n_own, n_oth, w_own, w_oth, bias, wfe, bfe, ln_bias, segc,
    ncat, u, fq, fk, va, arow, pay,
):
    x, y = idx[0], idx[1]
    lane = lanes()
    low = lane < 64
    centre = jnp.broadcast_to(ln_bias[...], (16, 768)).astype(bf16)
    for s, w in ((0, w_own), (1, w_oth)):
        a01 = nt(centre, w[384:512, :])[0:1] + bias[s, :, 384:512]
        a12 = nt(centre, w[448:576, :])[0:1] + bias[s, :, 448:576]
        arow[3 * s] = jnp.where(low, a01, 0.0)
        arow[3 * s + 1] = jnp.where(low, a12, 0.0)
        arow[3 * s + 2] = jnp.where(low, half_turn(jnp.broadcast_to(a12, (8, 128)))[0:1], 0.0)
    for r, n_ref in ((0, n_own), (1, n_oth)):
        start = pl.multiple_of((x if r == 0 else 1 - x) * 256, 256)
        rows = pl.ds(start, 256)
        n = n_ref[...]
        ncat[rows, :] = n
        for s, w in ((0, w_own), (1, w_oth)):
            qk = (nt(n, w[0:384, :]) + bias[s, :, 0:384]).astype(bf16)
            u[rows, 384 * s : 384 * s + 384] = qk
            for p in range(3):
                logits = nn(qk[:, 128 * p : 128 * p + 128], wfe[s, p]) + bfe[s, p]
                for k in range(2):
                    part = logits[:, 128 * k : 128 * k + 128]
                    top = jnp.max(part, axis=1, keepdims=True)
                    e = jnp.exp(part - top)
                    soft = (e * (1.0 / jnp.sum(e, axis=1, keepdims=True))).astype(bf16)
                    m = 2 * p + k
                    if m < 3:
                        fq[3 * s + m, rows, :] = soft
                    else:
                        fk[3 * s + m - 3, rows, :] = soft
            v01 = (nt(n, w[384:512, :]) + bias[s, :, 384:512]).astype(bf16).astype(f32)
            v12 = (nt(n, w[448:576, :]) + bias[s, :, 448:576]).astype(bf16).astype(f32)
            ones = jnp.where((lane == 64) | (lane == 65), 1.0, 0.0)
            for h, v in ((0, v01), (1, v12), (2, half_turn(v12))):
                va[3 * s + h, rows, :] = jnp.where(low, v - arow[3 * s + h], ones).astype(bf16)
    last = seg[y * 512 + 511]
    keep = (segc[...] == last).astype(f32)
    tops, norms = [], []
    for g in range(6):
        st = tn(va[g], (fk[g].astype(f32) * keep).astype(bf16))
        tops.append(st[0:64])
        norms.append(st[64:65])
    encode(pay, tops, norms)


def inner_kernel(segc, segr, fq, fk, va, numden):
    for it in range(2):
        wide = 256 * (it + 1)
        i = lax.broadcasted_iota(jnp.int32, (256, wide), 0) + 256 * it
        j = lax.broadcasted_iota(jnp.int32, (256, wide), 1)
        mask = ((j <= i) & (segc[256 * it : 256 * it + 256, :] == segr[:, 0:wide])).astype(f32)

        def body(g, carry):
            scores = nt(fq[g, 256 * it : 256 * it + 256, :], fk[g, 0:wide, :])
            weights = (scores * mask).astype(bf16)
            numden[g, 256 * it : 256 * it + 256, :] = nn(weights, va[g, 0:wide, :])
            return carry

        lax.fori_loop(0, 6, body, 0)


def flag(test):
    return jnp.where(test, 1.0, 0.0).astype(f32)


def send_state_kernel(forward, idx, seg, mine, theirs, out):
    y = idx[1]
    if forward:
        first_half = flag(seg[511] == seg[1023])
        own = jnp.where(y == 0, first_half, 1.0)
        oth = jnp.where(y == 0, 1.0, first_half)
    else:
        second_half = flag(seg[512] == seg[0])
        own = jnp.where(y == 0, 1.0, second_half)
        oth = jnp.where(y == 0, second_half, 1.0)
    tops, norms = combine([(own, decode(mine)), (oth, decode(theirs, True))])
    encode(out, tops, norms)


def carry_state(forward, idx, seg, theirs, one, two, three):
    y = idx[1]
    near = flag(seg[511] == seg[512])
    if forward:
        near = jnp.where(y == 1, near, 0.0)
        far = jnp.where(y == 1, flag(seg[0] == seg[512]), 1.0)
    else:
        near = jnp.where(y == 0, near, 0.0)
        far = jnp.where(y == 0, flag(seg[511] == seg[1023]), 1.0)
    return combine(
        [(near, decode(theirs, True)), (far, decode(one)), (far, decode(two)), (far, decode(three))]
    )


def augmented(top, norm, third):
    row = lax.broadcasted_iota(jnp.int32, (64, 128), 0)
    high = norm.astype(bf16).astype(f32)
    rest = norm - high
    if third:
        low = jnp.where(row < 2, high, jnp.where(row == 2, rest, 0.0))
    else:
        low = jnp.where(row == 0, high, jnp.where(row == 1, rest, 0.0))
    return jnp.concatenate([top, low], axis=0).astype(bf16)


def out_kernel(
    idx, seg, theirs, one, two, three, numden, fq, arow, segc, w_own, w_oth,
    att, mixed, paug, part_own, part_oth,
):
    x, y = idx[0], idx[1]
    tops, norms = carry_state(True, idx, seg, theirs, one, two, three)
    low = lanes() < 64
    first = seg[y * 512]
    open_rows = (segc[...] == first).astype(f32)
    for s in range(2):
        heads = []
        for h in range(3):
            g = 3 * s + h
            paug[g] = augmented(tops[g], norms[g], True)
            nd = numden[g] + open_rows * nt(fq[g], paug[g])
            inv = 1.0 / (nd[:, 64:65] + nd[:, 66:67])
            a = jnp.where(low, nd * inv, 0.0)
            att[g] = jnp.where(low, a, inv)
            heads.append(a + arow[g])
        mixed[:, 256 * s : 256 * s + 128] = (heads[0] + half_turn(heads[1])).astype(bf16)
        mixed[:, 256 * s + 128 : 256 * s + 256] = half_turn(heads[2]).astype(bf16)

    def term(start):
        rows = pl.ds(pl.multiple_of(start * 256, 256), 256)
        total = nn(mixed[rows, 0:128], w_own[0:128, :]) + nn(mixed[rows, 128:256], w_own[64:192, :])
        total += nn(mixed[rows, 256:384], w_oth[0:128, :])
        return total + nn(mixed[rows, 384:512], w_oth[64:192, :])

    part_oth[...] = term(1 - x).astype(bf16)
    part_own[...] = term(x)


def ln_two_kernel(tok, own, recv, b_out, gain, bias, mid, normed):
    v = tok[...].astype(f32) + (own[...] + recv[...].astype(f32) + b_out[...])
    mid[...] = v
    hat, _ = norm_stats(v)
    normed[...] = (hat * gain[...] + bias[...]).astype(bf16)


def mlp_kernel(n2, cot, up_own, up_oth, down_own, down_oth, b_up, hid, gpre, gn2):
    rows = n2[...]
    cots = cot[...]
    total = jnp.zeros((256, 768), f32)
    for s, up, down in ((0, up_own, down_own), (1, up_oth, down_oth)):
        for t in range(3):
            cols = slice(256 * t, 256 * t + 256)
            at = slice(768 * s + 256 * t, 768 * s + 256 * t + 256)
            pre = nn(rows, up[:, cols]) + b_up[s, :, cols]
            grad = nt(cots, down[cols, :])
            square = pre * pre
            th = jnp.tanh(ROOT * (pre + 0.044715 * (square * pre)))
            half = 0.5 * (1.0 + th)
            hid[:, at] = (pre * half).astype(bf16)
            slope = half + 0.5 * pre * (1.0 - th * th) * (ROOT * (1.0 + 3 * 0.044715 * square))
            g = (grad * slope).astype(bf16)
            gpre[:, at] = g
            total += nt(g, up[:, cols])
    gn2[...] = total.astype(gn2.dtype)


def down_kernel(hid_own, hid_oth, down_own, down_oth, own, oth):
    oth[...] = (nn(hid_oth[:, 0:768], down_own[...]) + nn(hid_oth[:, 768:1536], down_oth[...])).astype(bf16)
    own[...] = nn(hid_own[:, 0:768], down_own[...]) + nn(hid_own[:, 768:1536], down_oth[...])


def final_kernel(mid, own, recv, b_down, out):
    out[...] = (mid[...] + (own[...] + recv[...].astype(f32)) + b_down[...]).astype(bf16)


def norm_grad(v, gain, grad):
    hat, inv = norm_stats(v)
    e = grad * gain
    back = inv * (e - jnp.mean(e, axis=-1, keepdims=True) - hat * jnp.mean(e * hat, axis=-1, keepdims=True))
    return back, jnp.sum(grad * hat, axis=0, keepdims=True), jnp.sum(grad, axis=0, keepdims=True)


def put_vector(ref, row, vec):
    for t in range(vec.shape[1] // 128):
        ref[row + t : row + t + 1, :] = vec[:, 128 * t : 128 * t + 128]


def ln_two_back_kernel(mid, own, recv, gain, cot, gmid, branch, vecs):
    cots = cot[...].astype(f32)
    back, dgain, dbias = norm_grad(mid[...], gain[...], own[...] + recv[...].astype(f32))
    g = cots + back
    gmid[...] = g
    low = g.astype(bf16)
    branch[...] = low
    put_vector(vecs, 0, jnp.sum(low.astype(f32), axis=0, keepdims=True))
    put_vector(vecs, 6, dgain)
    put_vector(vecs, 12, dbias)
    put_vector(vecs, 18, jnp.sum(cots, axis=0, keepdims=True))


def ln_one_back_kernel(tok, own, recv, gain, gmid, out, vecs):
    back, dgain, dbias = norm_grad(tok[...].astype(f32), gain[...], own[...] + recv[...].astype(f32))
    out[...] = gmid[...] + back
    put_vector(vecs, 0, dgain)
    put_vector(vecs, 6, dbias)


def mlp_send_kernel(idx, hid_own, hid_oth, gpre_own, gpre_oth, n2_own, n2_oth, cot_own, cot_oth, send):
    at = pl.ds(pl.multiple_of((1 - idx[3]) * 384, 384), 384)
    for s in range(2):
        units = pl.ds(pl.multiple_of((1 - idx[3]) * 384 + 768 * s, 384), 384)
        cols = slice(768 * s, 768 * s + 768)
        send[s, 0:384, :] = (tn(hid_own[:, units], cot_own[...]) + tn(hid_oth[:, units], cot_oth[...])).astype(bf16)
        send[s, 384:768, :] = (tn(n2_own[:, at], gpre_own[:, cols]) + tn(n2_oth[:, at], gpre_oth[:, cols])).astype(bf16)


def mlp_keep_kernel(idx, hid_own, hid_oth, gpre_own, gpre_oth, n2_own, n2_oth, cot_own, cot_oth, recv, keep, send, sums):
    at = pl.ds(pl.multiple_of(idx[3] * 384, 384), 384)
    for s in (1, 0):
        units = pl.ds(pl.multiple_of(idx[3] * 384 + 768 * s, 384), 384)
        cols = slice(768 * s, 768 * s + 768)
        down = tn(hid_own[:, units], cot_own[...]) + tn(hid_oth[:, units], cot_oth[...])
        down += recv[s, 0:384, :].astype(f32)
        up = tn(n2_own[:, at], gpre_own[:, cols]) + tn(n2_oth[:, at], gpre_oth[:, cols])
        up += recv[s, 384:768, :].astype(f32)
        if s == 1:
            send[0:384, :] = down.astype(bf16)
            send[384:768, :] = up.astype(bf16)
        else:
            keep[0:384, :] = down
            keep[384:768, :] = up
        bias = jnp.sum(gpre_own[:, cols].astype(f32), axis=0, keepdims=True)
        bias += jnp.sum(gpre_oth[:, cols].astype(f32), axis=0, keepdims=True)
        sums[s] = jnp.zeros((8, 128), f32)
        for t in range(6):
            sums[s, t : t + 1, :] = bias[:, 128 * t : 128 * t + 128]


def grad_mixed_kernel(idx, seg, gb_own, gb_oth, w_own, w_oth, att, fq, segc, gbcat, gna, pay):
    x, y = idx[0], idx[1]
    lane = lanes()
    low = lane < 64
    gbcat[pl.ds(pl.multiple_of(x * 256, 256), 256), :] = gb_own[...]
    gbcat[pl.ds(pl.multiple_of((1 - x) * 256, 256), 256), :] = gb_oth[...]
    first = seg[y * 512]
    open_rows = (segc[...] == first).astype(f32)
    tops, norms = [], []
    for s, w in ((0, w_own), (1, w_oth)):
        g01 = nt(gbcat[...], w[0:128, :]).astype(bf16).astype(f32)
        g12 = nt(gbcat[...], w[64:192, :]).astype(bf16).astype(f32)
        for h, gm in ((0, g01), (1, g12), (2, half_turn(g12))):
            g = 3 * s + h
            a = att[g]
            gn = jnp.where(low, gm * a[:, 64:65], 0.0).astype(bf16).astype(f32)
            gd = -jnp.sum(gn * a, axis=1, keepdims=True)
            high = gd.astype(bf16).astype(f32)
            tail = jnp.where((lane == 64) | (lane == 66), high, jnp.where(lane == 65, gd - high, 0.0))
            gna[g] = jnp.where(low, gn, tail).astype(bf16)
            st = tn(gna[g], (fq[g].astype(f32) * open_rows).astype(bf16))
            tops.append(st[0:64])
            norms.append(st[64:65] + st[65:66])
    encode(pay, tops, norms)


def soft_grad(soft, grad):
    s = soft.astype(f32)
    return (s * (grad - jnp.sum(grad * s, axis=1, keepdims=True))).astype(bf16)


def inner_back_kernel(idx, seg, segc, segr, fq, fk, va, gna, paug, gq, gkf, gv):
    y = idx[1]
    first = seg[y * 512]
    i0 = lax.broadcasted_iota(jnp.int32, (256, 256), 0)
    j0 = lax.broadcasted_iota(jnp.int32, (256, 256), 1)
    for it in range(2):
        rows = slice(256 * it, 256 * it + 256)
        wide = 256 * (it + 1)
        i = lax.broadcasted_iota(jnp.int32, (256, wide), 0) + 256 * it
        j = lax.broadcasted_iota(jnp.int32, (256, wide), 1)
        mask = ((j <= i) & (segc[rows, :] == segr[:, 0:wide])).astype(f32)
        open_rows = (segc[rows, :] == first).astype(f32)

        def queries(g, carry):
            gw = (nt(gna[g, rows, :], va[g, 0:wide, :]) * mask).astype(bf16)
            grad = nn(gw, fk[g, 0:wide, :]) + open_rows * nn(gna[g, rows, :], paug[g])
            gq[g, rows, :] = soft_grad(fq[g, rows, :], grad)
            return carry

        lax.fori_loop(0, 6, queries, 0)
        tall = 512 - 256 * it
        kj = lax.broadcasted_iota(jnp.int32, (256, tall), 0)
        ki = lax.broadcasted_iota(jnp.int32, (256, tall), 1)
        kmask = ((kj <= ki) & (segc[rows, :] == segr[:, 256 * it : 512])).astype(f32)

        def keys(g, carry):
            late = slice(256 * it, 512)
            w = (nt(fk[g, rows, :], fq[g, late, :]) * kmask).astype(bf16)
            gv[g, rows, :] = nn(w, gna[g, late, :])
            gw = (nt(va[g, rows, :], gna[g, late, :]) * kmask).astype(bf16)
            gkf[g, rows, :] = nn(gw, fq[g, late, :])
            return carry

        lax.fori_loop(0, 6, keys, 0)


def qkv_back_kernel(
    idx, seg, theirs, one, two, three, segc, fk, va, gkf, gv, gq, wfe, w_own, w_oth,
    gk, gproj, part_own, part_oth,
):
    x, y = idx[0], idx[1]
    tops, norms = carry_state(False, idx, seg, theirs, one, two, three)
    low = lanes() < 64
    last = seg[y * 512 + 511]
    open_rows = (segc[...] == last).astype(f32)
    for s in range(2):
        base = 640 * s
        values = []
        for h in range(3):
            g = 3 * s + h
            aug = augmented(tops[g], norms[g], False)
            grad = gkf[g] + open_rows * nn(va[g], aug)
            gk[g] = soft_grad(fk[g], grad)
            values.append(jnp.where(low, gv[g] + open_rows * nt(fk[g], aug), 0.0))
        gproj[:, base + 384 : base + 512] = (values[0] + half_turn(values[1])).astype(bf16)
        gproj[:, base + 512 : base + 640] = half_turn(values[2]).astype(bf16)
        order = [gq[3 * s], gq[3 * s + 1], gq[3 * s + 2], gk[3 * s], gk[3 * s + 1], gk[3 * s + 2]]
        for p in range(3):
            pair = jnp.concatenate([order[2 * p], order[2 * p + 1]], axis=1)
            gproj[:, base + 128 * p : base + 128 * p + 128] = nt(pair, wfe[s, p]).astype(bf16)

    def term(start):
        rows = pl.ds(pl.multiple_of(start * 256, 256), 256)
        total = nn(gproj[rows, 0:512], w_own[0:512, :]) + nn(gproj[rows, 512:640], w_own[448:576, :])
        total += nn(gproj[rows, 640:1152], w_oth[0:512, :])
        return total + nn(gproj[rows, 1152:1280], w_oth[448:576, :])

    part_oth[...] = term(1 - x).astype(bf16)
    part_own[...] = term(x)


def attn_weights_kernel(idx, n, gproj, mixed, gb, u, gq, gk, send, keep, sums, scr):
    c = idx[3]
    row = lax.broadcasted_iota(jnp.int32, (8, 128), 0)
    for s in range(2):
        base = 640 * s
        scr[0:512, :] = tn(gproj[:, base : base + 512], n[...])
        scr[512:576, :] = tn(gproj[:, base + 512 : base + 640], n[...])[64:128]
        scr[576:704, :] = tn(mixed[:, 256 * s : 256 * s + 128], gb[...])
        scr[704:768, :] = tn(mixed[:, 256 * s + 128 : 256 * s + 256], gb[...])[64:128]
        mine, other = pl.multiple_of(288 * c, 32), pl.multiple_of(288 * (1 - c), 32)
        mine_out, other_out = pl.multiple_of(576 + 96 * c, 32), pl.multiple_of(576 + 96 * (1 - c), 32)
        keep[s, 0:288, :] = scr[pl.ds(mine, 288), :]
        keep[s, 288:384, :] = scr[pl.ds(mine_out, 96), :]
        send[s, 0:288, :] = scr[pl.ds(other, 288), :].astype(bf16)
        send[s, 288:384, :] = scr[pl.ds(other_out, 96), :].astype(bf16)
        order = [gq[3 * s], gq[3 * s + 1], gq[3 * s + 2], gk[3 * s], gk[3 * s + 1], gk[3 * s + 2]]
        feats = [jnp.zeros((64, 128), f32)] * 3
        biases = [jnp.zeros((1, 128), f32)] * 3
        for p in range(3):
            pair = jnp.concatenate([order[2 * p], order[2 * p + 1]], axis=1)
            prod = tn(u[:, 384 * s + 128 * p : 384 * s + 128 * p + 128], pair)
            for k in range(2):
                block = prod[64 * k : 64 * k + 64, 128 * k : 128 * k + 128]
                h = (2 * p + k) % 3
                feats[h] = feats[h] + (block - half_turn(block))
                total = jnp.sum(order[2 * p + k].astype(f32), axis=0, keepdims=True)
                total8 = jnp.broadcast_to(total, (8, 128))
                biases[h] = biases[h] + (total8 - half_turn(total8))[0:1]
        for h in range(3):
            sums[s, 64 * h : 64 * h + 64, :] = feats[h]
        block = jnp.zeros((8, 128), f32)
        for t in range(5):
            total = jnp.sum(gproj[:, base + 128 * t : base + 128 * t + 128].astype(f32), axis=0, keepdims=True)
            block = jnp.where(row == t, total, block)
        for h in range(3):
            block = jnp.where(row == 5 + h, biases[h], block)
        sums[s, 192:200, :] = block


def after(value, *deps):
    return lax.optimization_barrier((value,) + deps)[0]


def swap(value, axis, bit):
    count = lax.axis_size(axis)
    return jax.tree.map(
        lambda v: lax.ppermute(v, axis, [(i, i ^ bit) for i in range(count)]), value
    )


def shift(value, axis, step):
    count = lax.axis_size(axis)
    pairs = [(i, i + step) for i in range(count) if 0 <= i + step < count]
    return lax.ppermute(value, axis, pairs)


def other_shard(half, c):
    fetched = swap(half, "tp", 2)
    sibling = swap(fetched, "dp", 1)
    return jnp.concatenate(
        [jnp.where(c == 0, fetched, sibling), jnp.where(c == 0, sibling, fetched)], axis=0
    )


def my_half(value, c):
    rows = value.shape[0] // 2
    return jnp.where(c == 0, value[:rows], value[rows:])


def rest_of_dp(value):
    bit = 2
    while bit < lax.axis_size("dp"):
        value = jax.tree.map(lambda v: v + swap(v.astype(bf16), "dp", bit).astype(f32), value)
        bit *= 2
    return value


def over_cp(keep, z):
    rows = keep.shape[0] // 2
    low = (z & 1) == 0
    mine = jnp.where(low, keep[:rows], keep[rows:])
    sent = jnp.where(low, keep[rows:], keep[:rows]).astype(bf16)
    half = (mine + swap(sent, "cp", 1).astype(f32)).astype(bf16)
    bit = 2
    while bit < lax.axis_size("cp"):
        half = (half.astype(f32) + swap(half, "cp", bit).astype(f32)).astype(bf16)
        bit *= 2
    return half, swap(half, "cp", 1)


def whole_rows(pieces, c, z):
    half, pair = pieces
    low = (z & 1) == 0
    mine = jnp.concatenate([jnp.where(low, half, pair), jnp.where(low, pair, half)], axis=0)
    sibling = swap(mine, "dp", 1)
    return jnp.where(c == 0, mine, sibling).astype(f32), jnp.where(c == 0, sibling, mine).astype(f32)


def shards(
    tokens, segment_ids, ln1_gain, ln1_bias, w_qkv, b_qkv, w_feat, b_feat, output_weight, b_out,
    ln2_gain, ln2_bias, w_up, b_up, w_down, b_down, cotangent,
):
    t = lax.axis_index("tp")
    z = lax.axis_index("cp")
    c = lax.axis_index("dp") & 1
    x, y = t & 1, t >> 1
    idx = jnp.stack([x, y, z, c, c, c, c, c]).astype(jnp.int32)
    row = lambda v: v.reshape(1, -1)
    tok = tokens.reshape(256, 768)
    cot_own = cotangent.reshape(256, 768)
    seg = segment_ids.reshape(1024)
    seg_block = lax.dynamic_slice_in_dim(seg, y * 512, 512, 0)
    segc = seg_block.reshape(512, 1)
    segr = seg_block.reshape(1, 512)

    wq_own = jnp.transpose(w_qkv, (1, 2, 0)).reshape(576, 768)
    wq_oth = other_shard(my_half(wq_own, c), c)
    flat = jnp.concatenate([b_qkv.reshape(-1), b_feat.reshape(-1), b_up])
    flat_oth = swap(flat, "tp", 2)
    feat_oth = swap(w_feat, "tp", 2)
    biases = jnp.stack([flat, flat_oth])[:, None, :]
    bq = biases[:, :, 0:576]
    bf = biases[:, :, 576:768].reshape(2, 3, 64)
    bup = biases[:, :, 768:1536]
    wf = jnp.stack([w_feat, feat_oth])
    signed = jnp.concatenate([wf, -wf], axis=-1)
    pick_a, pick_b = (0, 2, 1), (1, 0, 2)
    take = lambda v, picks: jnp.stack([v[:, i] for i in picks], axis=1)
    wfe = jnp.pad(take(signed, pick_a), ((0, 0), (0, 0), (0, 64), (0, 128))) + jnp.pad(
        take(signed, pick_b), ((0, 0), (0, 0), (64, 0), (128, 0))
    )
    bsigned = jnp.concatenate([bf, -bf], axis=-1)
    bfe = jnp.concatenate([take(bsigned, pick_a), take(bsigned, pick_b)], axis=-1)[:, :, None, :]

    (n_own,) = call(ln_one_kernel, [((256, 768), bf16)], [tok, row(ln1_gain), row(ln1_bias)], name="ln_one")
    n_oth = swap(n_own, "tp", 1)
    cot_oth = swap(after(cot_own, n_oth), "tp", 1)
    out_half = after(my_half(output_weight, c), wq_oth)
    wo_oth = other_shard(out_half, c)
    up_oth = other_shard(after(my_half(w_up, c), wo_oth), c)
    down_oth = other_shard(after(my_half(w_down, c), up_oth), c)

    head_rows = ((6, 512, 128), bf16)
    head_rows_f32 = ((6, 512, 128), f32)
    ncat, u, fq, fk, va, arow, pay = call(
        qkv_kernel,
        [((512, 768), bf16), ((512, 768), bf16), head_rows, head_rows, head_rows, ((6, 1, 128), f32), (PAY, bf16)],
        [idx, seg, n_own, n_oth, wq_own, wq_oth, bq, wfe, bfe, row(ln1_bias), segc],
        smem=2, flops=2 * 10**9, name="qkv",
    )
    pay_y = swap(pay, "tp", 2)
    (numden,) = call(inner_kernel, [head_rows_f32], [segc, segr, fq, fk, va], flops=10**9, name="inner")
    (state,) = call(
        functools.partial(send_state_kernel, True), [(PAY, bf16)], [idx, seg, pay, pay_y], smem=2, name="state"
    )
    carried = [shift(state, "cp", k) for k in (1, 2, 3)]
    att, mixed, paug, part_own, part_oth = call(
        out_kernel,
        [head_rows_f32, ((512, 512), bf16), ((6, 128, 128), bf16), ((256, 768), f32), ((256, 768), bf16)],
        [idx, seg, pay_y, *carried, numden, fq, arow, segc, output_weight, wo_oth],
        smem=2, flops=10**9, name="out",
    )
    part_in = swap(part_oth, "tp", 1)

    mid, n2_own = call(
        ln_two_kernel, [((256, 768), f32), ((256, 768), bf16)],
        [tok, part_own, part_in, row(b_out), row(ln2_gain), row(ln2_bias)], name="ln_two",
    )
    n2_oth = swap(n2_own, "tp", 1)

    def mlp(n2, cot, kind):
        return call(
            mlp_kernel, [((256, 1536), bf16), ((256, 1536), bf16), ((256, 768), kind)],
            [n2, cot, w_up, up_oth, w_down, down_oth, bup], flops=2 * 10**9, name="mlp",
        )

    hid_own, gpre_own, gn2_own = mlp(n2_own, cot_own, f32)
    hid_oth, gpre_oth, gn2_oth = mlp(n2_oth, cot_oth, bf16)
    gn2_in = swap(gn2_oth, "tp", 1)
    gmid, gb_own, vecs_two = call(
        ln_two_back_kernel, [((256, 768), f32), ((256, 768), bf16), ((24, 128), f32)],
        [mid, gn2_own, gn2_in, row(ln2_gain), cot_own], name="ln_two_back",
    )
    gb_oth = swap(gb_own, "tp", 1)

    mlp_args = [idx, hid_own, hid_oth, gpre_own, gpre_oth, n2_own, n2_oth, cot_own, cot_oth]
    (mlp_send,) = call(mlp_send_kernel, [((2, 768, 768), bf16)], mlp_args, smem=1, flops=2 * 10**9, name="mlp_send")
    mlp_recv = swap(mlp_send, "dp", 1)
    mlp_keep, mlp_y, sums_up = call(
        mlp_keep_kernel, [((768, 768), f32), ((768, 768), bf16), ((2, 8, 128), f32)],
        mlp_args + [mlp_recv], smem=1, flops=2 * 10**9, name="mlp_keep",
    )
    mlp_sum = rest_of_dp(mlp_keep + swap(mlp_y, "tp", 2).astype(f32))
    mlp_pieces = [over_cp(mlp_sum[:384], z), over_cp(mlp_sum[384:], z)]
    down_own, down_part = call(
        down_kernel, [((256, 768), f32), ((256, 768), bf16)],
        [hid_own, hid_oth, w_down, down_oth], flops=10**9, name="down",
    )
    down_in = swap(after(down_part, gb_oth), "tp", 1)
    (out_tokens,) = call(final_kernel, [((256, 768), bf16)], [mid, down_own, down_in, row(b_down)], name="final")

    gbcat, gna, gpay = call(
        grad_mixed_kernel, [((512, 768), bf16), head_rows, (PAY, bf16)],
        [idx, seg, gb_own, gb_oth, output_weight, wo_oth, att, fq, segc], smem=2, flops=10**9, name="grad_mixed",
    )
    gpay_y = swap(gpay, "tp", 2)
    (gstate,) = call(
        functools.partial(send_state_kernel, False), [(PAY, bf16)], [idx, seg, gpay, gpay_y], smem=2, name="gstate"
    )
    coming = [shift(gstate, "cp", -k) for k in (1, 2, 3)]
    gq, gkf, gv = call(
        inner_back_kernel, [head_rows, head_rows_f32, head_rows_f32],
        [idx, seg, segc, segr, fq, fk, va, gna, paug], smem=2, flops=3 * 10**9, name="inner_back",
    )
    gk, gproj, gn1_own, gn1_oth = call(
        qkv_back_kernel, [head_rows, ((512, 1280), bf16), ((256, 768), f32), ((256, 768), bf16)],
        [idx, seg, gpay_y, *coming, segc, fk, va, gkf, gv, gq, wfe, wq_own, wq_oth],
        smem=2, flops=2 * 10**9, name="qkv_back",
    )
    gn1_in = swap(gn1_oth, "tp", 1)
    att_send, att_keep, sums_att = call(
        attn_weights_kernel, [((2, 384, 768), bf16), ((2, 384, 768), f32), ((2, 200, 128), f32)],
        [idx, ncat, gproj, mixed, gbcat, u, gq, gk], smem=1,
        scratch=[pltpu.VMEM((768, 768), f32)], flops=2 * 10**9, name="attn_weights",
    )
    att_both = att_keep + swap(att_send, "dp", 1).astype(f32)
    att_sum = rest_of_dp(att_both[0] + swap(att_both[1].astype(bf16), "tp", 2).astype(f32))
    att_pieces = over_cp(att_sum, z)
    d_tok, vecs_one = call(
        ln_one_back_kernel, [((256, 768), f32), ((12, 128), f32)],
        [tok, gn1_own, gn1_in, row(ln1_gain), gmid], name="ln_one_back",
    )

    own_small = jnp.concatenate([sums_att[0], sums_up[0]], axis=0)
    oth_small = jnp.concatenate([sums_att[1], sums_up[1]], axis=0)
    vecs = jnp.concatenate([vecs_two, vecs_one], axis=0)
    count = own_small.shape[0]
    small = jnp.concatenate([own_small, oth_small, vecs], axis=0)
    bit = 1
    while bit < lax.axis_size("dp"):
        small = small + swap(small, "dp", bit)
        bit *= 2
    crossed = swap(small[count:], "tp", 2)
    small = jnp.concatenate([small[:count] + crossed[:count], small[2 * count :] + crossed[count:]], axis=0)
    bit = 1
    while bit < lax.axis_size("cp"):
        small = small + swap(small, "cp", bit)
        bit *= 2
    vec_rows = small[count:] + swap(small[count:], "tp", 1)
    vec = vec_rows.reshape(6, 768)
    d_feat = small[0:192].reshape(3, 64, 128)[:, :, :64]
    tiles = small[192:197].reshape(640)
    d_b_qkv = jnp.concatenate([tiles[:512], tiles[576:640]]).reshape(3, 192)
    d_b_feat = small[197:200, :64]
    d_b_up = small[200:206].reshape(768)

    first, second = whole_rows(mlp_pieces[0], c, z)
    d_w_down = jnp.concatenate([first, second], axis=0)
    first, second = whole_rows(mlp_pieces[1], c, z)
    d_w_up = jnp.concatenate([first, second], axis=0)
    first, second = whole_rows(att_pieces, c, z)
    d_wq = jnp.concatenate([first[:288], second[:288]], axis=0)
    d_w_qkv = jnp.transpose(d_wq.reshape(3, 192, 768), (2, 0, 1))
    d_w_out = jnp.concatenate([first[288:], second[288:]], axis=0)
    return (
        out_tokens.reshape(tokens.shape),
        d_tok.reshape(tokens.shape),
        vec[4],
        vec[5],
        d_w_qkv,
        d_b_qkv,
        d_feat,
        d_b_feat,
        d_w_out,
        vec[0],
        vec[1],
        vec[2],
        d_w_up,
        d_b_up,
        d_w_down,
        vec[3],
    )


def solution(mesh):
    rows = P(("cp", "tp"), "dp", None)
    placed = (
        rows, P("cp", "dp"), P(), P(), P(None, None, "tp"), P(None, "tp"), P("tp", None, None),
        P("tp", None), P("tp", None), P(), P(), P(), P(None, "tp"), P("tp"), P("tp", None), P(), rows,
    )
    given = (
        rows, rows, P(), P(), P(None, None, "tp"), P(None, "tp"), P("tp", None, None), P("tp", None),
        P("tp", None), P(), P(), P(), P(None, "tp"), P("tp"), P("tp", None), P(),
    )
    return jax.shard_map(shards, mesh=mesh, in_specs=placed, out_specs=given, check_vma=False)
```

```python
import functools
import math

import jax
import jax.numpy as jnp
from jax import lax
from jax.experimental import pallas as pl
from jax.experimental.pallas import tpu as pltpu
from jax.sharding import PartitionSpec as P

f32 = jnp.float32
bf16 = jnp.bfloat16
EPS = 1e-05
ROOT = math.sqrt(2.0 / math.pi)
VMEM_LIMIT = 12 * 1024 * 1024


def nn(a, b):
    return jnp.dot(a, b, preferred_element_type=f32)


def nt(a, b):
    return lax.dot_general(a, b, (((1,), (1,)), ((), ())), preferred_element_type=f32)


def tn(a, b):
    return lax.dot_general(a, b, (((0,), (0,)), ((), ())), preferred_element_type=f32)


def call(kernel, outs, args, smem=0, hbm=0, hbm_out=False, scratch=(), weight=1, name=None):
    args = [
        pltpu.with_memory_space_constraint(a, pltpu.HBM) if smem <= k < smem + hbm else a for k, a in enumerate(args)
    ]
    specs = [pl.BlockSpec(memory_space=pltpu.SMEM)] * smem
    specs += [pl.BlockSpec(memory_space=pltpu.HBM)] * hbm
    specs += [pl.BlockSpec(memory_space=pltpu.VMEM)] * (len(args) - smem - hbm)
    out_shape = [jax.ShapeDtypeStruct(shape, kind) for shape, kind in outs]
    return pl.pallas_call(
        kernel,
        out_shape=out_shape,
        in_specs=specs,
        out_specs=[pl.BlockSpec(memory_space=pltpu.HBM if hbm_out else pltpu.VMEM)] * len(outs),
        scratch_shapes=list(scratch),
        compiler_params=pltpu.CompilerParams(vmem_limit_bytes=VMEM_LIMIT),
        cost_estimate=pl.CostEstimate(flops=max(1, weight * 10**10), bytes_accessed=10**8, transcendentals=0),
        name=name,
    )(*args)


def lanes():
    return lax.broadcasted_iota(jnp.int32, (1, 128), 1)


def half_turn(v):
    return pltpu.roll(v, 64, 1)


def norm_stats(v):
    centred = v - jnp.mean(v, axis=-1, keepdims=True)
    inv = lax.rsqrt(jnp.mean(centred * centred, axis=-1, keepdims=True) + EPS)
    return centred * inv, inv


def encode(pay, tops, norms, scale=None):
    if scale is not None:
        tops, norms = [scale * t for t in tops], [scale * n for n in norms]
    for g in range(6):
        pay[g * 64 : g * 64 + 64, :] = tops[g].astype(bf16)
    row = lax.broadcasted_iota(jnp.int32, (16, 128), 0)
    for s in range(2):
        block = jnp.zeros((16, 128), f32)
        for h in range(3):
            n = norms[3 * s + h]
            high = n.astype(bf16).astype(f32)
            block = jnp.where(row == h, high, block)
            block = jnp.where(row == 3 + h, n - high, block)
        pay[384 + 16 * s : 400 + 16 * s, :] = block.astype(bf16)


def decode(pay, swap=False):
    tops, norms = [], []
    blocks = [pay[384 + 16 * s : 400 + 16 * s, :].astype(f32) for s in range(2)]
    for s in range(2):
        t = 1 - s if swap else s
        for h in range(3):
            g = 3 * t + h
            tops.append(pay[g * 64 : g * 64 + 64, :].astype(f32))
            norms.append(blocks[t][h : h + 1, :] + blocks[t][3 + h : 4 + h, :])
    return tops, norms


PAY = (416, 128)
PAY_OUT = (PAY, bf16)


def combine(parts):
    tops = [sum(f * p[0][g] for f, p in parts) for g in range(6)]
    norms = [sum(f * p[1][g] for f, p in parts) for g in range(6)]
    return tops, norms


def prep_kernel(
    idx, tok, gain, bias, b_out, gain2, bias2, b_down, w_qkv, w_feat, b_qkv, b_feat, b_up, seg, w_out, w_up, w_down,
    out, buf, signed, flat, par, segc, segr, out_half, up_half, down_half,
    tok_v, vecs, feat_v, bq_v, bf_v, seg_v, sems,
):
    half = w_qkv.at[pl.ds(pl.multiple_of(idx[3] * 288, 32), 288), :]
    pairs = [(tok, tok_v), (w_feat, feat_v), (b_qkv, bq_v), (b_feat, bf_v), (seg, seg_v), (half, buf.at[0:288, :])]
    pairs += [(v, vecs[k]) for k, v in enumerate((gain, bias, b_out, gain2, bias2, b_down, b_up))]
    copies = [pltpu.make_async_copy(a, b, sems.at[k]) for k, (a, b) in enumerate(pairs)]
    for copy in copies:
        copy.start()
    halves = []
    for k, (w, part) in enumerate(((w_out, out_half), (w_up, up_half), (w_down, down_half))):
        rows = w.shape[0] // 2
        source = w.at[pl.ds(pl.multiple_of(idx[3] * rows, 32), rows), :]
        halves.append(pltpu.make_async_copy(source, part, sems.at[13 + k]))
        halves[k].start()
    for copy in copies:
        copy.wait()
    hat, _ = norm_stats(tok_v[...].astype(f32))
    rows = [v[...].reshape(1, 768) for v in vecs]
    out[...] = (hat * rows[0] + rows[1]).astype(bf16)
    for k in range(6):
        par[k : k + 1, :] = rows[k]
    par[6:8, :] = jnp.zeros((2, 768), f32)
    block = seg_v[:, pl.ds(pl.multiple_of(idx[1] * 512, 512), 512)].astype(f32)
    segr[...] = block
    segc[...] = jnp.transpose(jnp.broadcast_to(block, (8, 512)))[:, 0:1]
    for h in range(3):
        w = feat_v[h]
        signed[64 * h : 64 * h + 64, :] = jnp.concatenate([w, -w], axis=1)
        b = bf_v[h : h + 1, :]
        flat[6 + h : 7 + h, :] = jnp.concatenate([b, -b], axis=1)
        flat[2 * h : 2 * h + 1, :] = bq_v[h : h + 1, 0:128]
        flat[2 * h + 1 : 2 * h + 2, :] = bq_v[h : h + 1, 64:192]
    for t in range(6):
        flat[9 + t : 10 + t, :] = rows[6][:, 128 * t : 128 * t + 128]
    flat[15:16, :] = jnp.zeros((1, 128), f32)
    for t in range(6):
        buf[288:320, 128 * t : 128 * t + 128] = signed[32 * t : 32 * t + 32, :]
    rest = flat[...]
    for t in range(3):
        limb = rest.astype(bf16)
        buf[320:336, 128 * t : 128 * t + 128] = limb
        rest = rest - limb.astype(f32)
    buf[320:336, 384:768] = jnp.zeros((16, 384), bf16)
    for copy in halves:
        copy.wait()


def join_halves(c, whole, mine, sibling):
    rows = mine.shape[0]
    whole[pl.ds(pl.multiple_of(c * rows, 32), rows), :] = mine[...]
    whole[pl.ds(pl.multiple_of((1 - c) * rows, 32), rows), :] = sibling[...]


def qkv_kernel(
    idx, seg, n_own, n_oth, w_own, buf, buf_sib, signed, flat, par, segc,
    ncat, u, fq, fk, va, arow, pay, pay_far, wx, wfe, bup, w_oth,
):
    x, y, c = idx[0], idx[1], idx[3]
    lane = lanes()
    low = lane < 64
    w_oth[pl.ds(pl.multiple_of(c * 288, 32), 288), :] = buf[0:288, :]
    w_oth[pl.ds(pl.multiple_of((1 - c) * 288, 32), 288), :] = buf_sib[0:288, :]
    flats = [flat[...], sum(buf[320:336, 128 * t : 128 * t + 128].astype(f32) for t in range(3))]
    biases = []
    for s, w in ((0, w_own), (1, w_oth)):
        for k in range(3):
            wx[s, 256 * k : 256 * k + 128, :] = w[192 * k : 192 * k + 128, :]
            wx[s, 256 * k + 128 : 256 * k + 256, :] = w[192 * k + 64 : 192 * k + 192, :]
        if s == 0:
            parts = [signed[64 * h : 64 * h + 64, :] for h in range(3)]
        else:
            tiles = [buf[288:320, 128 * t : 128 * t + 128] for t in range(6)]
            parts = [jnp.concatenate([tiles[2 * h], tiles[2 * h + 1]], axis=0) for h in range(3)]
        none = jnp.zeros((64, 128), bf16)
        wfe[s, 0:64, 0:128] = parts[0]
        wfe[s, 64:128, 0:128] = none
        wfe[s, 0:64, 128:256] = none
        wfe[s, 64:128, 128:256] = parts[1]
        wfe[s, 0:64, 256:384] = none
        wfe[s, 64:128, 256:384] = parts[2]
        f = flats[s]
        bup[s] = f
        biases.append(jnp.concatenate([f[t : t + 1, :] for t in range(6)], axis=1))
        centre = jnp.broadcast_to(par[1:2, :], (16, 768)).astype(bf16)
        a = nt(centre, wx[s, 512:768, :])[0:8] + biases[s][:, 512:768]
        arow[3 * s] = jnp.where(low, a[0:1, 0:128], 0.0)
        arow[3 * s + 1] = jnp.where(low, a[0:1, 128:256], 0.0)
        arow[3 * s + 2] = jnp.where(low, half_turn(a[:, 128:256])[0:1], 0.0)
    ones = jnp.where((lane == 64) | (lane == 65), 1.0, 0.0)
    for r, n_ref in ((0, n_own), (1, n_oth)):
        start = pl.multiple_of((x if r == 0 else 1 - x) * 256, 256)
        rows = pl.ds(start, 256)
        n = n_ref[...]
        ncat[rows, :] = n
        for s in range(2):
            proj = (nt(n, wx[s]) + biases[s]).astype(bf16)
            u[rows, 512 * s : 512 * s + 512] = proj[:, 0:512]
            for k, feats in ((0, fq), (1, fk)):
                both = nn(proj[:, 256 * k : 256 * k + 128], wfe[s, :, 0:256])
                third = nn(proj[:, 256 * k + 128 : 256 * k + 256], wfe[s, :, 256:384])
                for h, part in ((0, both[:, 0:128]), (1, both[:, 128:256]), (2, third)):
                    part = part + flats[s][6 + h : 7 + h, :]
                    top = jnp.max(part, axis=1, keepdims=True)
                    e = jnp.exp(part - top)
                    feats[3 * s + h, rows, :] = (e * (1.0 / jnp.sum(e, axis=1, keepdims=True))).astype(bf16)
            v01 = proj[:, 512:640].astype(f32)
            v12 = proj[:, 640:768].astype(f32)
            for h, v in ((0, v01), (1, v12), (2, half_turn(v12))):
                va[3 * s + h, rows, :] = jnp.where(low, v - arow[3 * s + h], ones).astype(bf16)
    last = seg[y * 512 + 511].astype(f32)
    keep = (segc[...] == last).astype(f32)
    tops, norms = [], []
    for g in range(6):
        st = tn(va[g], (fk[g].astype(f32) * keep).astype(bf16))
        tops.append(st[0:64])
        norms.append(st[64:65])
    encode(pay, tops, norms)
    encode(pay_far, tops, norms, far_scale(True, seg, y))


def inner_kernel(segc, segr, fq, fk, va, numden):
    for it in range(2):
        wide = 256 * (it + 1)
        i = lax.broadcasted_iota(jnp.int32, (256, wide), 0) + 256 * it
        j = lax.broadcasted_iota(jnp.int32, (256, wide), 1)
        mask = ((j <= i) & (segc[256 * it : 256 * it + 256, :] == segr[:, 0:wide])).astype(f32)

        for g in range(6):
            scores = nt(fq[g, 256 * it : 256 * it + 256, :], fk[g, 0:wide, :])
            weights = (scores * mask).astype(bf16)
            numden[g, 256 * it : 256 * it + 256, :] = nn(weights, va[g, 0:wide, :])


def flag(test):
    return jnp.where(test, 1.0, 0.0).astype(f32)


def far_scale(forward, seg, y):
    if forward:
        return jnp.where(y == 0, flag(seg[511] == seg[1023]), 1.0)
    return jnp.where(y == 0, 1.0, flag(seg[512] == seg[0]))


def send_state_kernel(forward, idx, seg, mine, theirs, one, one_theirs, out):
    y = idx[1]
    scale = far_scale(forward, seg, 1 - y)
    parts = [(1.0, decode(mine)), (scale, decode(theirs, True)), (1.0, decode(one)), (1.0, decode(one_theirs, True))]
    encode(out, *combine(parts))


def carry_state(forward, idx, seg, theirs, one, one_theirs, two):
    y, z = idx[1], idx[2]
    near = flag(seg[511] == seg[512])
    if forward:
        near = jnp.where(y == 1, near, 0.0)
        far = jnp.where(y == 1, flag(seg[0] == seg[512]), 1.0)
        within, across = flag((z & 1) == 1), flag(z >= 2)
    else:
        near = jnp.where(y == 0, near, 0.0)
        far = jnp.where(y == 0, flag(seg[511] == seg[1023]), 1.0)
        within, across = flag((z & 1) == 0), flag(z < 2)
    parts = [(near, decode(theirs, True)), (far * within, decode(one)), (far * within, decode(one_theirs, True))]
    return combine(parts + [(far * across, decode(two))])


def augmented(top, norm, third):
    row = lax.broadcasted_iota(jnp.int32, (64, 128), 0)
    high = norm.astype(bf16).astype(f32)
    rest = norm - high
    if third:
        low = jnp.where(row < 2, high, jnp.where(row == 2, rest, 0.0))
    else:
        low = jnp.where(row == 0, high, jnp.where(row == 1, rest, 0.0))
    return jnp.concatenate([top, low], axis=0).astype(bf16)


def out_kernel(
    idx, seg, theirs, one, one_theirs, two, numden, fq, arow, segc, w_own, w_mine, w_sib,
    att, mixed, paug, part_own, part_a, part_b, w_oth,
):
    x, y = idx[0], idx[1]
    join_halves(idx[3], w_oth, w_mine, w_sib)
    tops, norms = carry_state(True, idx, seg, theirs, one, one_theirs, two)
    low = lanes() < 64
    first = seg[y * 512].astype(f32)
    open_rows = (segc[...] == first).astype(f32)
    for s in range(2):
        heads = []
        for h in range(3):
            g = 3 * s + h
            paug[g] = augmented(tops[g], norms[g], True)
            nd = numden[g] + open_rows * nt(fq[g], paug[g])
            inv = 1.0 / (nd[:, 64:65] + nd[:, 66:67])
            a = jnp.where(low, nd * inv, 0.0)
            att[g] = jnp.where(low, a, inv)
            heads.append(a + arow[g])
        mixed[:, 256 * s : 256 * s + 128] = (heads[0] + half_turn(heads[1])).astype(bf16)
        mixed[:, 256 * s + 128 : 256 * s + 256] = half_turn(heads[2]).astype(bf16)

    def term(start):
        rows = pl.ds(pl.multiple_of(start * 256, 256), 256)
        total = nn(mixed[rows, 0:128], w_own[0:128, :]) + nn(mixed[rows, 128:256], w_own[64:192, :])
        total += nn(mixed[rows, 256:384], w_oth[0:128, :])
        return total + nn(mixed[rows, 384:512], w_oth[64:192, :])

    oth = term(1 - x).astype(bf16)
    part_a[...] = oth[0:128]
    part_b[...] = oth[128:256]
    part_own[...] = term(x)


def ln_two_kernel(k, tok, own, recv, par, mid, normed):
    rows = slice(128 * k, 128 * k + 128)
    v = tok[rows, :].astype(f32) + (own[rows, :] + recv[...].astype(f32) + par[2:3, :])
    mid[...] = v
    hat, _ = norm_stats(v)
    normed[...] = (hat * par[3:4, :] + par[4:5, :]).astype(bf16)


def stack(*refs, cols=slice(None)):
    return jnp.concatenate([r[:, cols] for r in refs], axis=0)


def mlp_own_kernel(
    idx, n2_a, n2_b, cot, up_own, up_mine, up_sib, down_own, down_mine, down_sib, b_up, hid, gpre, gn2, up_oth, down_oth
):
    join_halves(idx[3], up_oth, up_mine, up_sib)
    join_halves(idx[3], down_oth, down_mine, down_sib)
    mlp(stack(n2_a, n2_b), cot[...], up_own, up_oth, down_own, down_oth, b_up, hid, gpre, gn2)


def mlp_kernel(k, n2, cot, up_own, up_oth, down_own, down_oth, b_up, hid, gpre, gn2):
    mlp(n2[...], cot[128 * k : 128 * k + 128, :], up_own, up_oth, down_own, down_oth, b_up, hid, gpre, gn2)


def mlp(rows, cots, up_own, up_oth, down_own, down_oth, b_up, hid, gpre, gn2):
    total = jnp.zeros(rows.shape, f32)
    bias = [jnp.concatenate([b_up[s, 9 + t : 10 + t, :] for t in range(6)], axis=1) for s in range(2)]
    for s, up, down in ((0, up_own, down_own), (1, up_oth, down_oth)):
        for t in range(3):
            cols = slice(256 * t, 256 * t + 256)
            at = slice(768 * s + 256 * t, 768 * s + 256 * t + 256)
            pre = nn(rows, up[:, cols]) + bias[s][:, cols]
            grad = nt(cots, down[cols, :])
            square = pre * pre
            th = jnp.tanh(ROOT * (pre + 0.044715 * (square * pre)))
            half = 0.5 * (1.0 + th)
            hid[:, at] = (pre * half).astype(bf16)
            slope = half + 0.5 * pre * (1.0 - th * th) * (ROOT * (1.0 + 3 * 0.044715 * square))
            g = (grad * slope).astype(bf16)
            gpre[:, at] = g
            total += nt(g, up[:, cols])
    gn2[...] = total.astype(gn2.dtype)


def down_kernel(hid_own, hid_a, hid_b, down_own, down_oth, own, oth):
    hid = stack(hid_a, hid_b)
    oth[...] = (nn(hid[:, 0:768], down_own[...]) + nn(hid[:, 768:1536], down_oth[...])).astype(bf16)
    own[...] = nn(hid_own[:, 0:768], down_own[...]) + nn(hid_own[:, 768:1536], down_oth[...])


def final_kernel(mid_a, mid_b, own, recv, par, out):
    for k, mid in enumerate((mid_a, mid_b)):
        rows = slice(128 * k, 128 * k + 128)
        out[rows, :] = (mid[...] + (own[rows, :] + recv[rows, :].astype(f32)) + par[5:6, :]).astype(bf16)


def norm_grad(v, gain, grad):
    hat, inv = norm_stats(v)
    e = grad * gain
    back = inv * (e - jnp.mean(e, axis=-1, keepdims=True) - hat * jnp.mean(e * hat, axis=-1, keepdims=True))
    return back, jnp.sum(grad * hat, axis=0, keepdims=True), jnp.sum(grad, axis=0, keepdims=True)


def put_vector(ref, row, vec):
    for t in range(vec.shape[1] // 128):
        ref[row + t : row + t + 1, :] = vec[:, 128 * t : 128 * t + 128]


def ln_two_back_kernel(k, mid, own, recv, par, cot, *more):
    *before, gmid, branch, vecs = more
    rows = slice(128 * k, 128 * k + 128)
    cots = cot[rows, :].astype(f32)
    back, dgain, dbias = norm_grad(mid[...], par[3:4, :], own[rows, :] + recv[...].astype(f32))
    g = cots + back
    gmid[...] = g
    low = g.astype(bf16)
    branch[...] = low
    put_vector(vecs, 0, jnp.sum(low.astype(f32), axis=0, keepdims=True))
    put_vector(vecs, 6, dgain)
    put_vector(vecs, 12, dbias)
    put_vector(vecs, 18, jnp.sum(cots, axis=0, keepdims=True))
    for earlier in before:
        vecs[...] += earlier[...]


def ln_one_back_kernel(tok, own, recv, par, gmid_a, gmid_b, vecs_two, out, vecs):
    back, dgain, dbias = norm_grad(tok[...].astype(f32), par[0:1, :], own[...] + recv[...].astype(f32))
    out[...] = stack(gmid_a, gmid_b) + back
    vecs[0:24, :] = vecs_two[...]
    put_vector(vecs, 24, dgain)
    put_vector(vecs, 30, dbias)
    vecs[36:40, :] = jnp.zeros((4, 128), f32)


def down_grad(idx, half, s, hid_own, hid_a, hid_b, cot_own, cot_oth):
    at = pl.ds(pl.multiple_of(half * 384 + 768 * s, 384), 384)
    return tn(hid_own[:, at], cot_own[...]) + tn(stack(hid_a, hid_b, cols=at), cot_oth[...])


def up_grad(idx, half, s, own_a, own_b, oth_a, oth_b, gpre_own, gpre_a, gpre_b):
    at = pl.ds(pl.multiple_of(half * 384, 384), 384)
    cols = slice(768 * s, 768 * s + 768)
    total = tn(stack(own_a, own_b, cols=at), gpre_own[:, cols])
    return total + tn(stack(oth_a, oth_b, cols=at), stack(gpre_a, gpre_b, cols=cols))


def mlp_send_kernel(grad, idx, *args):
    *args, send = args
    for s in range(2):
        send[s] = grad(idx, 1 - idx[3], s, *args).astype(bf16)


def mlp_keep_kernel(grad, idx, *args):
    *args, recv, keep, send = args
    send[...] = (grad(idx, idx[3], 1, *args) + recv[1].astype(f32)).astype(bf16)
    keep[...] = grad(idx, idx[3], 0, *args) + recv[0].astype(f32)


def grad_mixed_kernel(idx, seg, own_a, own_b, oth_a, oth_b, w_own, w_oth, att, fq, segc, gbcat, gna, pay, pay_far):
    x, y = idx[0], idx[1]
    lane = lanes()
    low = lane < 64
    for start, a, b in ((x, own_a, own_b), (1 - x, oth_a, oth_b)):
        gbcat[pl.ds(pl.multiple_of(start * 256, 128), 128), :] = a[...]
        gbcat[pl.ds(pl.multiple_of(start * 256 + 128, 128), 128), :] = b[...]
    first = seg[y * 512].astype(f32)
    open_rows = (segc[...] == first).astype(f32)
    tops, norms = [], []
    for s, w in ((0, w_own), (1, w_oth)):
        g01 = nt(gbcat[...], w[0:128, :]).astype(bf16).astype(f32)
        g12 = nt(gbcat[...], w[64:192, :]).astype(bf16).astype(f32)
        for h, gm in ((0, g01), (1, g12), (2, half_turn(g12))):
            g = 3 * s + h
            a = att[g]
            gn = jnp.where(low, gm * a[:, 64:65], 0.0).astype(bf16).astype(f32)
            gd = -jnp.sum(gn * a, axis=1, keepdims=True)
            high = gd.astype(bf16).astype(f32)
            tail = jnp.where((lane == 64) | (lane == 66), high, jnp.where(lane == 65, gd - high, 0.0))
            gna[g] = jnp.where(low, gn, tail).astype(bf16)
            st = tn(gna[g], (fq[g].astype(f32) * open_rows).astype(bf16))
            tops.append(st[0:64])
            norms.append(st[64:65] + st[65:66])
    encode(pay, tops, norms)
    encode(pay_far, tops, norms, far_scale(False, seg, y))


def soft_grad(soft, grad):
    s = soft.astype(f32)
    return (s * (grad - jnp.sum(grad * s, axis=1, keepdims=True))).astype(bf16)


def query_back_kernel(idx, seg, segc, segr, fq, fk, va, gna, paug, wfe, gq, gpq):
    y = idx[1]
    first = seg[y * 512].astype(f32)
    for it in range(2):
        rows = slice(256 * it, 256 * it + 256)
        wide = 256 * (it + 1)
        i = lax.broadcasted_iota(jnp.int32, (256, wide), 0) + 256 * it
        j = lax.broadcasted_iota(jnp.int32, (256, wide), 1)
        mask = ((j <= i) & (segc[rows, :] == segr[:, 0:wide])).astype(f32)
        open_rows = (segc[rows, :] == first).astype(f32)
        for g in range(6):
            gw = (nt(gna[g, rows, :], va[g, 0:wide, :]) * mask).astype(bf16)
            grad = nn(gw, fk[g, 0:wide, :]) + open_rows * nn(gna[g, rows, :], paug[g])
            gq[g, rows, :] = soft_grad(fq[g, rows, :], grad)
        for s in range(2):
            pair = jnp.concatenate([gq[3 * s, rows, :], gq[3 * s + 1, rows, :]], axis=1)
            gpq[rows, 256 * s : 256 * s + 128] = nt(pair, wfe[s, :, 0:256]).astype(bf16)
            gpq[rows, 256 * s + 128 : 256 * s + 256] = nt(gq[3 * s + 2, rows, :], wfe[s, :, 256:384]).astype(bf16)


def key_back_kernel(segc, segr, fq, fk, va, gna, gkf, gv):
    for it in range(2):
        rows = slice(256 * it, 256 * it + 256)
        late = slice(256 * it, 512)
        tall = 512 - 256 * it
        j = lax.broadcasted_iota(jnp.int32, (256, tall), 0)
        i = lax.broadcasted_iota(jnp.int32, (256, tall), 1)
        mask = ((j <= i) & (segc[rows, :] == segr[:, 256 * it : 512])).astype(f32)
        for g in range(6):
            w = (nt(fk[g, rows, :], fq[g, late, :]) * mask).astype(bf16)
            gv[g, rows, :] = nn(w, gna[g, late, :])
            gw = (nt(va[g, rows, :], gna[g, late, :]) * mask).astype(bf16)
            gkf[g, rows, :] = nn(gw, fq[g, late, :])


def qkv_back_kernel(
    idx, seg, theirs, one, one_theirs, two, segc, fk, va, gkf, gv, gpq, wfe, wx,
    gk, gpkv, part_own, part_oth,
):
    x, y = idx[0], idx[1]
    tops, norms = carry_state(False, idx, seg, theirs, one, one_theirs, two)
    low = lanes() < 64
    last = seg[y * 512 + 511].astype(f32)
    open_rows = (segc[...] == last).astype(f32)
    for s in range(2):
        base = 512 * s
        values = []
        for h in range(3):
            g = 3 * s + h
            aug = augmented(tops[g], norms[g], False)
            gk[g] = soft_grad(fk[g], gkf[g] + open_rows * nn(va[g], aug))
            values.append(jnp.where(low, gv[g] + open_rows * nt(fk[g], aug), 0.0))
        gpkv[:, base + 256 : base + 384] = (values[0] + half_turn(values[1])).astype(bf16)
        gpkv[:, base + 384 : base + 512] = half_turn(values[2]).astype(bf16)
        pair = jnp.concatenate([gk[3 * s], gk[3 * s + 1]], axis=1)
        gpkv[:, base : base + 128] = nt(pair, wfe[s, :, 0:256]).astype(bf16)
        gpkv[:, base + 128 : base + 256] = nt(gk[3 * s + 2], wfe[s, :, 256:384]).astype(bf16)

    def term(start):
        rows = pl.ds(pl.multiple_of(start * 256, 256), 256)
        total = nn(gpq[rows, 0:256], wx[0, 0:256, :]) + nn(gpkv[rows, 0:512], wx[0, 256:768, :])
        return total + (nn(gpq[rows, 256:512], wx[1, 0:256, :]) + nn(gpkv[rows, 512:1024], wx[1, 256:768, :]))

    part_oth[...] = term(1 - x).astype(bf16)
    part_own[...] = term(x)


def split_rows(c, scr, base, rows, at, keep, send, s):
    half = rows // 2
    keep[s, at : at + half, :] = scr[pl.ds(pl.multiple_of(base + half * c, 32), half), :]
    send[s, at : at + half, :] = scr[pl.ds(pl.multiple_of(base + half * (1 - c), 32), half), :].astype(bf16)


def early_weights_kernel(idx, n, gpq, mixed, gb, keep, send, scr):
    for s in range(2):
        cols = slice(256 * s, 256 * s + 256)
        for k, (a, b) in enumerate(((gpq, n), (mixed, gb))):
            grad = tn(a[:, cols], b[...])
            scr[192 * k : 192 * k + 128, :] = grad[0:128]
            scr[192 * k + 128 : 192 * k + 192, :] = grad[192:256]
            split_rows(idx[3], scr, 192 * k, 192, 96 * k, keep, send, s)


def late_weights_kernel(idx, n, gpq, gpkv, u, gq, gk, gpre_own, gpre_a, gpre_b, keep, send, scr):
    row = lax.broadcasted_iota(jnp.int32, (16, 128), 0)
    for s in range(2):
        grad = tn(gpkv[:, 512 * s : 512 * s + 512], n[...])
        for k in range(2):
            scr[192 * k : 192 * k + 128, :] = grad[256 * k : 256 * k + 128]
            scr[192 * k + 128 : 192 * k + 192, :] = grad[256 * k + 192 : 256 * k + 256]
        first = jnp.zeros((128, 256), f32)
        third = jnp.zeros((128, 128), f32)
        sums = []
        for k, g in ((0, gq), (1, gk)):
            at = 512 * s + 256 * k
            pair = jnp.concatenate([g[3 * s], g[3 * s + 1]], axis=1)
            first += tn(u[:, at : at + 128], pair)
            third += tn(u[:, at + 128 : at + 256], g[3 * s + 2])
            sums.append([jnp.sum(g[3 * s + h].astype(f32), axis=0, keepdims=True) for h in range(3)])
        low = lanes() < 64
        block = first[0:64, 0:128]
        zero = block - half_turn(block)
        block = first[64:128, 128:256]
        one = block - half_turn(block)
        block = third[64:128]
        two = block - half_turn(block)
        scr[384:448, 0:128] = jnp.where(low, zero, half_turn(one))
        scr[384:448, 128:256] = jnp.where(low, two, 0.0)
        scr[384:448, 256:768] = jnp.zeros((64, 512), f32)
        rows = []
        for t in range(6):
            tile = gpq[:, 256 * s + 128 * t : 256 * s + 128 * t + 128] if t < 2 else (
                gpkv[:, 512 * s + 128 * t - 256 : 512 * s + 128 * t - 128])
            rows.append(jnp.sum(tile.astype(f32), axis=0, keepdims=True))
        for h in range(3):
            total = jnp.broadcast_to(sums[0][h] + sums[1][h], (8, 128))
            rows.append((total - half_turn(total))[0:1])
        block = jnp.zeros((16, 128), f32)
        for t, value in enumerate(rows):
            block = jnp.where(row == t, value, block)
        scr[384:400, 256:384] = block
        cols = slice(768 * s, 768 * s + 768)
        bias = jnp.sum(gpre_own[:, cols].astype(f32), axis=0, keepdims=True)
        for part in (gpre_a, gpre_b):
            bias += jnp.sum(part[:, cols].astype(f32), axis=0, keepdims=True)
        block = jnp.zeros((16, 128), f32)
        for t in range(6):
            block = jnp.where(row == t, bias[:, 128 * t : 128 * t + 128], block)
        scr[384:400, 384:512] = block
        split_rows(idx[3], scr, 0, 192, 0, keep, send, s)
        split_rows(idx[3], scr, 192, 192, 96, keep, send, s)
        split_rows(idx[3], scr, 384, 64, 192, keep, send, s)


def pair_kernel(keep, recv, mine, across):
    mine[...] = keep[0] + recv[0].astype(f32)
    across[...] = (keep[1] + recv[1].astype(f32)).astype(bf16)


def cp_split_kernel(idx, keep, recv, mine, sent):
    rows = mine.shape[0]
    low = pl.multiple_of((idx[2] & 1) * rows, 16)
    high = pl.multiple_of((1 - (idx[2] & 1)) * rows, 16)
    sent[...] = (keep[pl.ds(high, rows), :] + recv[pl.ds(high, rows), :].astype(f32)).astype(bf16)
    mine[...] = keep[pl.ds(low, rows), :] + recv[pl.ds(low, rows), :].astype(f32)


def add_kernel(mine, recv, out):
    out[...] = (mine[...].astype(f32) + recv[...].astype(f32)).astype(out.dtype)


def place(idx, whole, pieces):
    half, pair, sib, sib_pair = pieces
    rows = half.shape[0]
    low, c = idx[2] & 1, idx[3]
    for core, zlow, piece in ((c, low, half), (c, 1 - low, pair), (1 - c, low, sib), (1 - c, 1 - low, sib_pair)):
        whole[pl.ds(pl.multiple_of((core * 2 + zlow) * rows, 16), rows), :] = piece[...].astype(whole.dtype)


def send_out(pairs, sems):
    copies = [pltpu.make_async_copy(a, b, sems.at[k]) for k, (a, b) in enumerate(pairs)]
    for copy in copies:
        copy.start()
    for copy in copies:
        copy.wait()


def join_kernel(idx, half, pair, out):
    join_halves(idx[2] & 1, out, half, pair)


def spread_kernel(idx, mine, sibling, out, whole, sems):
    for core, rows in ((idx[3], mine), (1 - idx[3], sibling)):
        whole[pl.ds(pl.multiple_of(core * 384, 384), 384), :] = rows[...].astype(f32)
    send_out([(whole, out)], sems)


def spread_attention_kernel(idx, *refs):
    early, late = refs[0:4], refs[4:8]
    outs, (first, second, w_qkv, w_out, feat, b_qkv, b_feat, b_up, sems) = refs[8:14], refs[14:]
    place(idx, first, early)
    place(idx, second, late)
    for c in range(2):
        w_qkv[96 * c : 96 * c + 96, :] = first[192 * c : 192 * c + 96, :]
        w_out[96 * c : 96 * c + 96, :] = first[192 * c + 96 : 192 * c + 192, :]
        w_qkv[192 + 96 * c : 288 + 96 * c, :] = second[224 * c : 224 * c + 96, :]
        w_qkv[384 + 96 * c : 480 + 96 * c, :] = second[224 * c + 96 : 224 * c + 192, :]
    more = jnp.concatenate([second[192:224, :], second[416:448, :]], axis=0)
    feat[0] = more[:, 0:64]
    feat[1] = half_turn(more[:, 0:128])[:, 0:64]
    feat[2] = more[:, 128:192]
    sums = more[0:16, 256:384]
    turned = half_turn(sums)
    for k in range(3):
        b_qkv[k : k + 1, 0:128] = sums[2 * k : 2 * k + 1]
        b_qkv[k : k + 1, 128:192] = turned[2 * k + 1 : 2 * k + 2, 0:64]
    b_feat[...] = sums[6:9, 0:64]
    b_up[...] = more[0:8, 384:512]
    send_out(list(zip((w_qkv, w_out, feat, b_qkv, b_feat, b_up), outs)), sems)


def after(value, *deps):
    return lax.optimization_barrier((value,) + deps)[0]


def swap(value, axis, bit):
    count = lax.axis_size(axis)
    return jax.tree.map(
        lambda v: lax.ppermute(v, axis, [(i, i ^ bit) for i in range(count)]), value
    )


def diagonal(value):
    tp, cp = lax.axis_size("tp"), lax.axis_size("cp")
    pairs = [(t * cp + z, (t ^ 2) * cp + (z ^ 1)) for t in range(tp) for z in range(cp)]
    return lax.ppermute(value, ("tp", "cp"), pairs)


def rest_of_dp(value):
    bit = 2
    while bit < lax.axis_size("dp"):
        value = value + swap(value.astype(bf16), "dp", bit).astype(f32)
        bit *= 2
    return value


def shards(
    tokens, segment_ids, ln1_gain, ln1_bias, w_qkv, b_qkv, w_feat, b_feat, output_weight, b_out,
    ln2_gain, ln2_bias, w_up, b_up, w_down, b_down, cotangent,
):
    t = lax.axis_index("tp")
    z = lax.axis_index("cp")
    c = lax.axis_index("dp") & 1
    x, y = t & 1, t >> 1
    idx = jnp.stack([x, y, z, c, c, c, c, c]).astype(jnp.int32)
    tok = tokens.reshape(256, 768)
    cot_own = cotangent.reshape(256, 768)
    seg = segment_ids.reshape(1024)

    wq = jnp.transpose(w_qkv, (1, 2, 0)).reshape(576, 768)
    done = []

    def run(kernel, outs, args, needs=(), **options):
        args = list(args)
        args[-1] = after(args[-1], *needs, *done)
        result = call(kernel, outs, args, **options)
        done[:] = [result[0]]
        return result

    def array(*shape, kind=bf16):
        return (shape, kind)

    rows_b, rows_f = array(256, 768), array(256, 768, kind=f32)
    part_b, part_f = array(128, 768), array(128, 768, kind=f32)
    head_rows, head_rows_f = array(6, 512, 128), array(6, 512, 128, kind=f32)

    n_own, buf, signed, flat, par, segc, segr, wo_half, up_half, down_half = run(
        prep_kernel,
        [
            rows_b, array(336, 768), array(192, 128), array(16, 128, kind=f32), array(8, 768, kind=f32),
            array(512, 1, kind=f32), array(1, 512, kind=f32), array(96, 768), array(384, 768), array(384, 768),
        ],
        [
            idx, tok, ln1_gain, ln1_bias, b_out, ln2_gain, ln2_bias, b_down, wq, w_feat, b_qkv, b_feat, b_up,
            segment_ids.reshape(1, 1024), output_weight, w_up, w_down,
        ],
        smem=1, hbm=16, name="prep",
        scratch=[
            pltpu.VMEM((256, 768), bf16), [pltpu.VMEM((768,), f32)] * 7, pltpu.VMEM((3, 64, 64), bf16),
            pltpu.VMEM((3, 192), f32), pltpu.VMEM((3, 64), f32), pltpu.VMEM((1, 1024), jnp.int32),
            pltpu.SemaphoreType.DMA((16,)),
        ],
    )
    n_oth = swap(n_own, "tp", 1)
    buf_y = swap(buf, "tp", 2)
    buf_sib = swap(after(buf_y, n_oth), "dp", 1)
    wo_mine = swap(after(wo_half, buf_y), "tp", 2)
    ncat, u, fq, fk, va, arow, pay, pay_far, wx, wfe, bup = run(
        qkv_kernel,
        [
            array(512, 768), array(512, 1024), head_rows, head_rows, head_rows, array(6, 1, 128, kind=f32),
            PAY_OUT, PAY_OUT, array(2, 768, 768), array(2, 128, 384), array(2, 16, 128, kind=f32),
        ],
        [idx, seg, n_own, n_oth, wq, buf_y, buf_sib, signed, flat, par, segc],
        smem=2, scratch=[pltpu.VMEM((576, 768), bf16)], name="qkv",
    )
    around = [swap(pay, "tp", 2), swap(pay_far, "cp", 1), diagonal(pay_far)]
    up_mine = swap(after(up_half, around[0]), "tp", 2)
    wo_pair = (wo_mine, swap(after(wo_mine, pay), "dp", 1))
    cot_oth = swap(after(cot_own, pay), "tp", 1)
    (numden,) = run(inner_kernel, [head_rows_f], [segc, segr, fq, fk, va], name="inner")
    (state,) = run(
        functools.partial(send_state_kernel, True), [PAY_OUT], [idx, seg, pay_far, *around], smem=2, weight=4, name="state"
    )
    down_mine = swap(after(down_half, up_mine), "tp", 2)
    carried = [*around, swap(state, "cp", 2)]
    att, mixed, paug, part_own, send_a, send_b, wo_oth = run(
        out_kernel,
        [head_rows_f, array(512, 512), array(6, 128, 128), rows_f, part_b, part_b, array(192, 768)],
        [idx, seg, *carried, numden, fq, arow, segc, output_weight, *wo_pair],
        needs=(cot_oth, up_mine), smem=2, name="out",
    )
    part_in = [swap(send_a, "tp", 1), swap(send_b, "tp", 1)]
    up_pair = (up_mine, swap(after(up_mine, send_a), "dp", 1))

    mid, n2_own = [None, None], [None, None]
    for k in range(2):
        mid[k], n2_own[k] = run(
            functools.partial(ln_two_kernel, k), [part_f, part_b], [tok, part_own, part_in[k], par], weight=4, name="ln_two"
        )
    n2_oth = [swap(v, "tp", 1) for v in n2_own]
    down_pair = (down_mine, swap(after(down_mine, n2_own[0]), "dp", 1))
    hid_own, gpre_own, gn2_own, up_oth, down_oth = run(
        mlp_own_kernel, [array(256, 1536), array(256, 1536), rows_f, array(768, 768), array(768, 768)],
        [idx, *n2_own, cot_own, w_up, *up_pair, w_down, *down_pair, bup], smem=1, name="mlp_own",
    )
    hid, gpre, gn2 = [None, None], [None, None], [None, None]
    for k in range(2):
        hid[k], gpre[k], gn2[k] = run(
            functools.partial(mlp_kernel, k), [array(128, 1536), array(128, 1536), part_b],
            [n2_oth[k], cot_oth, w_up, up_oth, w_down, down_oth, bup], name="mlp",
        )
    gn2_in = [swap(v, "tp", 1) for v in gn2]
    gmid, branch = [None, None], [None, None]

    def ln_two_back(k, *before):
        gmid[k], branch[k], vecs = run(
            functools.partial(ln_two_back_kernel, k), [part_f, part_b, array(24, 128, kind=f32)],
            [mid[k], gn2_own, gn2_in[k], par, cot_own, *before], weight=4, name="ln_two_back",
        )
        return vecs

    def grad_send(grad, args, name):
        (send,) = run(
            functools.partial(mlp_send_kernel, grad), [array(2, 384, 768)], args,
            smem=1, weight=0, name=name,
        )
        return swap(send, "dp", 1)

    def grad_keep(grad, args, name):
        return run(
            functools.partial(mlp_keep_kernel, grad), [array(384, 768, kind=f32), array(384, 768)], args,
            smem=1, name=name,
        )

    def cp_split(keep, recv, name):
        rows = keep.shape[0] // 2
        if lax.axis_size("dp") > 2:
            keep, recv = rest_of_dp(keep + recv.astype(f32)), jnp.zeros_like(recv)
        mine, sent = run(
            cp_split_kernel, [array(rows, 768, kind=f32), array(rows, 768)], [idx, keep, recv], smem=1, weight=4, name=name
        )
        return mine, swap(sent, "cp", 1)

    def add_across(mine, recv, name):
        (half,) = run(add_kernel, [(mine.shape, bf16)], [mine, recv], weight=4, name=name)
        return half, swap(half, "cp", 2)

    def add_last(mine, recv, name):
        (half,) = run(add_kernel, [(mine.shape, bf16)], [mine, recv], weight=4, name=name)
        return half, swap(half, "cp", 1)

    def pieces(last):
        half, pair = last
        return half, pair, swap(half, "dp", 1), swap(pair, "dp", 1)

    def join(last, name):
        rows = last[0].shape[0] * 2
        (mine,) = run(join_kernel, [array(rows, 768)], [idx, *last], smem=1, weight=4, name=name)
        return mine, swap(mine, "dp", 1)

    def spread(both, name):
        return run(
            spread_kernel, [array(768, 768, kind=f32)], [idx, *both], smem=1, hbm_out=True, name=name,
            scratch=[pltpu.VMEM((768, 768), f32), pltpu.SemaphoreType.DMA((1,))],
        )[0]

    down_args = [idx, hid_own, *hid, cot_own, cot_oth]
    up_args = [idx, *n2_own, *n2_oth, gpre_own, *gpre]
    down_recv = grad_send(down_grad, down_args, "down_send")
    vecs_two = ln_two_back(0)
    gb_oth = [swap(branch[0], "tp", 1)]
    down_keep, down_across = grad_keep(down_grad, down_args + [down_recv], "down_keep")
    down_sum = (down_keep, swap(down_across, "tp", 2))
    up_recv = grad_send(up_grad, up_args, "up_send")
    vecs_two = ln_two_back(1, vecs_two)
    gb_oth.append(swap(branch[1], "tp", 1))
    up_sum = grad_keep(up_grad, up_args + [up_recv], "up_keep")
    gbcat, gna, gpay, gpay_far = run(
        grad_mixed_kernel, [array(512, 768), head_rows, PAY_OUT, PAY_OUT],
        [idx, seg, *branch, *gb_oth, output_weight, wo_oth, att, fq, segc],
        smem=2, name="grad_mixed",
    )
    around = [swap(gpay, "tp", 2), swap(gpay_far, "cp", 1), diagonal(gpay_far)]
    down_sum = cp_split(*down_sum, "down_split")
    up_sum = (up_sum[0], swap(after(up_sum[1], down_sum[0]), "tp", 2))
    gkf, gv = run(
        key_back_kernel, [head_rows_f, head_rows_f], [segc, segr, fq, fk, va, gna], name="key_back",
    )
    (gstate,) = run(
        functools.partial(send_state_kernel, False), [PAY_OUT], [idx, seg, gpay_far, *around], smem=2, weight=4, name="gstate"
    )
    coming = [*around, swap(gstate, "cp", 2)]
    gq, gpq = run(
        query_back_kernel, [head_rows, array(512, 512)],
        [idx, seg, segc, segr, fq, fk, va, gna, paug, wfe], smem=2, name="query_back",
    )
    early_keep, early_send = run(
        early_weights_kernel, [array(2, 192, 768, kind=f32), array(2, 192, 768)], [idx, ncat, gpq, mixed, gbcat],
        smem=1, scratch=[pltpu.VMEM((384, 768), f32)], name="early_weights",
    )
    early_recv = swap(early_send, "dp", 1)
    def pair_sum(keep, recv, name):
        rows = keep.shape[1]
        mine, across = run(pair_kernel, [array(rows, 768, kind=f32), array(rows, 768)], [keep, recv], weight=4, name=name)
        return mine, swap(across, "tp", 2)

    down_sum = add_across(after(down_sum[0], coming[-1]), down_sum[1], "down_add")
    gk, gpkv, gn1_own, gn1_oth = run(
        qkv_back_kernel, [head_rows, array(512, 1024), rows_f, rows_b],
        [idx, seg, *coming, segc, fk, va, gkf, gv, gpq, wfe, wx],
        smem=2, name="qkv_back",
    )
    gn1_in = swap(gn1_oth, "tp", 1)
    late_keep, late_send = run(
        late_weights_kernel, [array(2, 224, 768, kind=f32), array(2, 224, 768)],
        [idx, ncat, gpq, gpkv, u, gq, gk, gpre_own, *gpre],
        smem=1, scratch=[pltpu.VMEM((448, 768), f32)], name="late_weights",
    )
    late_recv = swap(late_send, "dp", 1)
    early_sum = pair_sum(early_keep, early_recv, "early_pair")
    up_sum = cp_split(*up_sum, "up_split")
    late_sum = pair_sum(late_keep, late_recv, "late_pair")
    down_own, down_part = run(
        down_kernel, [rows_f, rows_b], [hid_own, *hid, w_down, down_oth], name="down",
    )

    down_last = add_last(*down_sum, "down_last")
    up_sum = add_across(*up_sum, "up_add")
    d_tok, vecs = run(
        ln_one_back_kernel, [rows_f, array(40, 128, kind=f32)], [tok, gn1_own, gn1_in, par, *gmid, vecs_two],
        weight=4, name="ln_one_back",
    )
    down_in = swap(after(down_part, gn1_in), "tp", 1)
    hops = [(axis, 1 << k) for axis in ("tp", "dp", "cp") for k in range(lax.axis_size(axis).bit_length() - 1)]

    def vec_hop():
        if hops:
            pending = swap(vecs, *hops.pop(0))
            return run(add_kernel, [array(40, 128, kind=f32)], [vecs, pending], weight=4, name="vecs")[0]
        return vecs

    early_sum = cp_split(*early_sum, "early_split")
    vecs = vec_hop()
    down_rows = join(down_last, "down_join")
    late_sum = cp_split(*late_sum, "late_split")
    vecs = vec_hop()
    early_sum = add_across(*early_sum, "early_add")
    vecs = vec_hop()
    (out_tokens,) = run(final_kernel, [rows_b], [*mid, down_own, down_in, par], weight=4, name="final")
    late_sum = add_across(*late_sum, "late_add")
    up_last = add_last(*up_sum, "up_last")
    vecs = vec_hop()
    early_last = add_last(*early_sum, "early_last")
    d_w_down = spread(down_rows, "spread_down")
    late_last = add_last(*late_sum, "late_last")
    up_rows = join(up_last, "up_join")
    while hops:
        vecs = vec_hop()
    early_pieces = pieces(early_last)
    late_pieces = pieces(late_last)
    d_w_up = spread(up_rows, "spread_up")
    given = [(576, 768), (192, 768), (3, 64, 64), (3, 192), (3, 64), (8, 128)]
    d_wq, d_w_out, d_feat, d_b_qkv, d_b_feat, d_b_up = run(
        spread_attention_kernel, [array(*shape, kind=f32) for shape in given], [idx, *early_pieces, *late_pieces],
        smem=1, hbm_out=True, name="spread_attention",
        scratch=[pltpu.VMEM((384, 768), f32), pltpu.VMEM((448, 768), f32)]
        + [pltpu.VMEM(shape, f32) for shape in given] + [pltpu.SemaphoreType.DMA((6,))],
    )
    vec = vecs[:36].reshape(6, 768)
    return (
        out_tokens.reshape(tokens.shape),
        d_tok.reshape(tokens.shape),
        vec[4],
        vec[5],
        jnp.transpose(d_wq.reshape(3, 192, 768), (2, 0, 1)),
        d_b_qkv,
        d_feat,
        d_b_feat,
        d_w_out,
        vec[0],
        vec[1],
        vec[2],
        d_w_up,
        d_b_up[:6].reshape(768),
        d_w_down,
        vec[3],
    )


def solution(mesh):
    rows = P(("cp", "tp"), "dp", None)
    placed = (
        rows, P("cp", "dp"), P(), P(), P(None, None, "tp"), P(None, "tp"), P("tp", None, None),
        P("tp", None), P("tp", None), P(), P(), P(), P(None, "tp"), P("tp"), P("tp", None), P(), rows,
    )
    given = (
        rows, rows, P(), P(), P(None, None, "tp"), P(None, "tp"), P("tp", None, None), P("tp", None),
        P("tp", None), P(), P(), P(), P(None, "tp"), P("tp"), P("tp", None), P(),
    )
    return jax.shard_map(shards, mesh=mesh, in_specs=placed, out_specs=given, check_vma=False)
```

```python
import functools
import math

import jax
import jax.numpy as jnp
from jax import lax
from jax.experimental import pallas as pl
from jax.experimental.pallas import tpu as pltpu
from jax.sharding import PartitionSpec as P

f32 = jnp.float32
bf16 = jnp.bfloat16
EPS = 1e-05
ROOT = math.sqrt(2.0 / math.pi)
VMEM_LIMIT = 12 * 1024 * 1024

ORDER = (
    "mlp_own", "mlp_0", "mlp_1", "down_send", "ln_two_back_0", "down_keep", "up_send", "ln_two_back_1",
    "up_keep", "grad_mixed", "down_split", "key_back", "gstate", "query_back", "down_add", "up_split",
    "qkv_back", "early_weights", "late_weights", "early_pair", "late_pair", "down_last", "up_add",
    "ln_one_back", "early_split", "down", "vec", "down_join", "late_split", "vec", "early_add", "late_add",
    "vec", "up_last", "down_spread", "vec", "early_last", "final", "up_join", "late_last", "up_spread",
    "attention",
)
WEIGHTS = {"down_send": 0, "gstate": 4, "late_pair": 0, "ln_two_back_0": 4, "ln_two_back_1": 4, "up_send": 0}


def nn(a, b):
    return jnp.dot(a, b, preferred_element_type=f32)


def nt(a, b):
    return lax.dot_general(a, b, (((1,), (1,)), ((), ())), preferred_element_type=f32)


def tn(a, b):
    return lax.dot_general(a, b, (((0,), (0,)), ((), ())), preferred_element_type=f32)


def call(kernel, outs, args, smem=0, hbm=0, hbm_out=False, scratch=(), weight=1, name=None):
    args = [
        pltpu.with_memory_space_constraint(a, pltpu.HBM) if smem <= k < smem + hbm else a for k, a in enumerate(args)
    ]
    specs = [pl.BlockSpec(memory_space=pltpu.SMEM)] * smem
    specs += [pl.BlockSpec(memory_space=pltpu.HBM)] * hbm
    specs += [pl.BlockSpec(memory_space=pltpu.VMEM)] * (len(args) - smem - hbm)
    out_shape = [jax.ShapeDtypeStruct(shape, kind) for shape, kind in outs]
    return pl.pallas_call(
        kernel,
        out_shape=out_shape,
        in_specs=specs,
        out_specs=[pl.BlockSpec(memory_space=pltpu.HBM if hbm_out else pltpu.VMEM)] * len(outs),
        scratch_shapes=list(scratch),
        compiler_params=pltpu.CompilerParams(vmem_limit_bytes=VMEM_LIMIT),
        cost_estimate=pl.CostEstimate(flops=max(1, weight * 10**10), bytes_accessed=10**8, transcendentals=0),
        name=name,
    )(*args)


def lanes():
    return lax.broadcasted_iota(jnp.int32, (1, 128), 1)


def half_turn(v):
    return pltpu.roll(v, 64, 1)


def norm_stats(v):
    centred = v - jnp.mean(v, axis=-1, keepdims=True)
    inv = lax.rsqrt(jnp.mean(centred * centred, axis=-1, keepdims=True) + EPS)
    return centred * inv, inv


def encode(pay, tops, norms, scale=None):
    if scale is not None:
        tops, norms = [scale * t for t in tops], [scale * n for n in norms]
    for g in range(6):
        pay[g * 64 : g * 64 + 64, :] = tops[g].astype(bf16)
    row = lax.broadcasted_iota(jnp.int32, (16, 128), 0)
    for s in range(2):
        block = jnp.zeros((16, 128), f32)
        for h in range(3):
            n = norms[3 * s + h]
            high = n.astype(bf16).astype(f32)
            block = jnp.where(row == h, high, block)
            block = jnp.where(row == 3 + h, n - high, block)
        pay[384 + 16 * s : 400 + 16 * s, :] = block.astype(bf16)


def decode(pay, swap=False):
    tops, norms = [], []
    blocks = [pay[384 + 16 * s : 400 + 16 * s, :].astype(f32) for s in range(2)]
    for s in range(2):
        t = 1 - s if swap else s
        for h in range(3):
            g = 3 * t + h
            tops.append(pay[g * 64 : g * 64 + 64, :].astype(f32))
            norms.append(blocks[t][h : h + 1, :] + blocks[t][3 + h : 4 + h, :])
    return tops, norms


PAY = (416, 128)
PAY_OUT = (PAY, bf16)


def combine(parts):
    tops = [sum(f * p[0][g] for f, p in parts) for g in range(6)]
    norms = [sum(f * p[1][g] for f, p in parts) for g in range(6)]
    return tops, norms


def prep_kernel(
    idx, tok, gain, bias, b_out, gain2, bias2, b_down, w_qkv, w_feat, b_qkv, b_feat, b_up, seg, w_out, w_up, w_down,
    out, buf, signed, flat, par, segc, segr, first_part, second_part,
    tok_v, vecs, feat_v, bq_v, bf_v, seg_v, sems,
):
    half = w_qkv.at[pl.ds(pl.multiple_of(idx[3] * 288, 32), 288), :]
    pairs = [(tok, tok_v), (w_feat, feat_v), (b_qkv, bq_v), (b_feat, bf_v), (seg, seg_v), (half, buf.at[0:288, :])]
    pairs += [(v, vecs[k]) for k, v in enumerate((gain, bias, b_out, gain2, bias2, b_down, b_up))]
    copies = [pltpu.make_async_copy(a, b, sems.at[k]) for k, (a, b) in enumerate(pairs)]
    for copy in copies:
        copy.start()
    halves = []
    for k, (w, skip, part) in enumerate(
        (
            (w_out, 0, first_part.at[0:96, :]),
            (w_up, 0, first_part.at[96:224, :]),
            (w_up, 128, second_part.at[0:256, :]),
            (w_down, 0, second_part.at[256:640, :]),
        )
    ):
        start = pl.multiple_of(idx[3] * (w.shape[0] // 2) + skip, 32)
        source = w.at[pl.ds(start, part.shape[0]), :]
        halves.append(pltpu.make_async_copy(source, part, sems.at[13 + k]))
        halves[k].start()
    for copy in copies:
        copy.wait()
    hat, _ = norm_stats(tok_v[...].astype(f32))
    rows = [v[...].reshape(1, 768) for v in vecs]
    out[...] = (hat * rows[0] + rows[1]).astype(bf16)
    for k in range(6):
        par[k : k + 1, :] = rows[k]
    par[6:8, :] = jnp.zeros((2, 768), f32)
    block = seg_v[:, pl.ds(pl.multiple_of(idx[1] * 512, 512), 512)].astype(f32)
    segr[...] = block
    segc[...] = jnp.transpose(jnp.broadcast_to(block, (8, 512)))[:, 0:1]
    for h in range(3):
        w = feat_v[h]
        signed[64 * h : 64 * h + 64, :] = jnp.concatenate([w, -w], axis=1)
        b = bf_v[h : h + 1, :]
        flat[6 + h : 7 + h, :] = jnp.concatenate([b, -b], axis=1)
        flat[2 * h : 2 * h + 1, :] = bq_v[h : h + 1, 0:128]
        flat[2 * h + 1 : 2 * h + 2, :] = bq_v[h : h + 1, 64:192]
    for t in range(6):
        flat[9 + t : 10 + t, :] = rows[6][:, 128 * t : 128 * t + 128]
    flat[15:16, :] = jnp.zeros((1, 128), f32)
    for t in range(6):
        buf[288:320, 128 * t : 128 * t + 128] = signed[32 * t : 32 * t + 32, :]
    rest = flat[...]
    for t in range(3):
        limb = rest.astype(bf16)
        buf[320:336, 128 * t : 128 * t + 128] = limb
        rest = rest - limb.astype(f32)
    buf[320:336, 384:768] = jnp.zeros((16, 384), bf16)
    for copy in halves:
        copy.wait()


def join_halves(c, whole, mine, sibling):
    rows = mine.shape[0]
    whole[pl.ds(pl.multiple_of(c * rows, 32), rows), :] = mine[...]
    whole[pl.ds(pl.multiple_of((1 - c) * rows, 32), rows), :] = sibling[...]


def qkv_kernel(
    idx, seg, n_own, n_oth, w_own, buf, buf_sib, signed, flat, par, segc,
    ncat, u, fq, fk, va, arow, pay, pay_far, wx, wfe, bup, w_oth,
):
    x, y, c = idx[0], idx[1], idx[3]
    lane = lanes()
    low = lane < 64
    w_oth[pl.ds(pl.multiple_of(c * 288, 32), 288), :] = buf[0:288, :]
    w_oth[pl.ds(pl.multiple_of((1 - c) * 288, 32), 288), :] = buf_sib[0:288, :]
    flats = [flat[...], sum(buf[320:336, 128 * t : 128 * t + 128].astype(f32) for t in range(3))]
    biases = []
    for s, w in ((0, w_own), (1, w_oth)):
        for k in range(3):
            wx[s, 256 * k : 256 * k + 128, :] = w[192 * k : 192 * k + 128, :]
            wx[s, 256 * k + 128 : 256 * k + 256, :] = w[192 * k + 64 : 192 * k + 192, :]
        if s == 0:
            parts = [signed[64 * h : 64 * h + 64, :] for h in range(3)]
        else:
            tiles = [buf[288:320, 128 * t : 128 * t + 128] for t in range(6)]
            parts = [jnp.concatenate([tiles[2 * h], tiles[2 * h + 1]], axis=0) for h in range(3)]
        none = jnp.zeros((64, 128), bf16)
        wfe[s, 0:64, 0:128] = parts[0]
        wfe[s, 64:128, 0:128] = none
        wfe[s, 0:64, 128:256] = none
        wfe[s, 64:128, 128:256] = parts[1]
        wfe[s, 0:64, 256:384] = none
        wfe[s, 64:128, 256:384] = parts[2]
        f = flats[s]
        bup[s] = f
        biases.append(jnp.concatenate([f[t : t + 1, :] for t in range(6)], axis=1))
        centre = jnp.broadcast_to(par[1:2, :], (16, 768)).astype(bf16)
        a = nt(centre, wx[s, 512:768, :])[0:8] + biases[s][:, 512:768]
        arow[3 * s] = jnp.where(low, a[0:1, 0:128], 0.0)
        arow[3 * s + 1] = jnp.where(low, a[0:1, 128:256], 0.0)
        arow[3 * s + 2] = jnp.where(low, half_turn(a[:, 128:256])[0:1], 0.0)
    ones = jnp.where((lane == 64) | (lane == 65), 1.0, 0.0)
    for r, n_ref in ((0, n_own), (1, n_oth)):
        start = pl.multiple_of((x if r == 0 else 1 - x) * 256, 256)
        rows = pl.ds(start, 256)
        n = n_ref[...]
        ncat[rows, :] = n
        for s in range(2):
            proj = (nt(n, wx[s]) + biases[s]).astype(bf16)
            u[rows, 512 * s : 512 * s + 512] = proj[:, 0:512]
            for k, feats in ((0, fq), (1, fk)):
                both = nn(proj[:, 256 * k : 256 * k + 128], wfe[s, :, 0:256])
                third = nn(proj[:, 256 * k + 128 : 256 * k + 256], wfe[s, :, 256:384])
                for h, part in ((0, both[:, 0:128]), (1, both[:, 128:256]), (2, third)):
                    part = part + flats[s][6 + h : 7 + h, :]
                    top = jnp.max(part, axis=1, keepdims=True)
                    e = jnp.exp(part - top)
                    feats[3 * s + h, rows, :] = (e * (1.0 / jnp.sum(e, axis=1, keepdims=True))).astype(bf16)
            v01 = proj[:, 512:640].astype(f32)
            v12 = proj[:, 640:768].astype(f32)
            for h, v in ((0, v01), (1, v12), (2, half_turn(v12))):
                va[3 * s + h, rows, :] = jnp.where(low, v - arow[3 * s + h], ones).astype(bf16)
    last = seg[y * 512 + 511].astype(f32)
    keep = (segc[...] == last).astype(f32)
    tops, norms = [], []
    for g in range(6):
        st = tn(va[g], (fk[g].astype(f32) * keep).astype(bf16))
        tops.append(st[0:64])
        norms.append(st[64:65])
    encode(pay, tops, norms)
    encode(pay_far, tops, norms, far_scale(True, seg, y))


def inner_kernel(segc, segr, fq, fk, va, numden):
    for it in range(2):
        wide = 256 * (it + 1)
        i = lax.broadcasted_iota(jnp.int32, (256, wide), 0) + 256 * it
        j = lax.broadcasted_iota(jnp.int32, (256, wide), 1)
        mask = ((j <= i) & (segc[256 * it : 256 * it + 256, :] == segr[:, 0:wide])).astype(f32)

        for g in range(6):
            scores = nt(fq[g, 256 * it : 256 * it + 256, :], fk[g, 0:wide, :])
            weights = (scores * mask).astype(bf16)
            numden[g, 256 * it : 256 * it + 256, :] = nn(weights, va[g, 0:wide, :])


def flag(test):
    return jnp.where(test, 1.0, 0.0).astype(f32)


def far_scale(forward, seg, y):
    if forward:
        return jnp.where(y == 0, flag(seg[511] == seg[1023]), 1.0)
    return jnp.where(y == 0, 1.0, flag(seg[512] == seg[0]))


def send_state_kernel(forward, idx, seg, mine, theirs, one, one_theirs, out):
    y = idx[1]
    scale = far_scale(forward, seg, 1 - y)
    parts = [(1.0, decode(mine)), (scale, decode(theirs, True)), (1.0, decode(one)), (1.0, decode(one_theirs, True))]
    encode(out, *combine(parts))


def carry_state(forward, idx, seg, theirs, one, one_theirs, two):
    y, z = idx[1], idx[2]
    near = flag(seg[511] == seg[512])
    if forward:
        near = jnp.where(y == 1, near, 0.0)
        far = jnp.where(y == 1, flag(seg[0] == seg[512]), 1.0)
        within, across = flag((z & 1) == 1), flag(z >= 2)
    else:
        near = jnp.where(y == 0, near, 0.0)
        far = jnp.where(y == 0, flag(seg[511] == seg[1023]), 1.0)
        within, across = flag((z & 1) == 0), flag(z < 2)
    parts = [(near, decode(theirs, True)), (far * within, decode(one)), (far * within, decode(one_theirs, True))]
    return combine(parts + [(far * across, decode(two))])


def augmented(top, norm, third):
    row = lax.broadcasted_iota(jnp.int32, (64, 128), 0)
    high = norm.astype(bf16).astype(f32)
    rest = norm - high
    if third:
        low = jnp.where(row < 2, high, jnp.where(row == 2, rest, 0.0))
    else:
        low = jnp.where(row == 0, high, jnp.where(row == 1, rest, 0.0))
    return jnp.concatenate([top, low], axis=0).astype(bf16)


def out_kernel(
    idx, seg, theirs, one, one_theirs, two, numden, fq, arow, segc, w_own, w_mine, w_sib,
    att, mixed, paug, part_own, part_a, part_b, w_oth,
):
    x, y = idx[0], idx[1]
    for core, part in ((idx[3], w_mine), (1 - idx[3], w_sib)):
        w_oth[pl.ds(pl.multiple_of(core * 96, 32), 96), :] = part[0:96, :]
    tops, norms = carry_state(True, idx, seg, theirs, one, one_theirs, two)
    low = lanes() < 64
    first = seg[y * 512].astype(f32)
    open_rows = (segc[...] == first).astype(f32)
    for s in range(2):
        heads = []
        for h in range(3):
            g = 3 * s + h
            paug[g] = augmented(tops[g], norms[g], True)
            nd = numden[g] + open_rows * nt(fq[g], paug[g])
            inv = 1.0 / (nd[:, 64:65] + nd[:, 66:67])
            a = jnp.where(low, nd * inv, 0.0)
            att[g] = jnp.where(low, a, inv)
            heads.append(a + arow[g])
        mixed[:, 256 * s : 256 * s + 128] = (heads[0] + half_turn(heads[1])).astype(bf16)
        mixed[:, 256 * s + 128 : 256 * s + 256] = half_turn(heads[2]).astype(bf16)

    def term(start):
        rows = pl.ds(pl.multiple_of(start * 256, 256), 256)
        total = nn(mixed[rows, 0:128], w_own[0:128, :]) + nn(mixed[rows, 128:256], w_own[64:192, :])
        total += nn(mixed[rows, 256:384], w_oth[0:128, :])
        return total + nn(mixed[rows, 384:512], w_oth[64:192, :])

    oth = term(1 - x).astype(bf16)
    part_a[...] = oth[0:128]
    part_b[...] = oth[128:256]
    part_own[...] = term(x)


def ln_two_kernel(k, tok, own, recv, par, mid, normed):
    rows = slice(128 * k, 128 * k + 128)
    v = tok[rows, :].astype(f32) + (own[rows, :] + recv[...].astype(f32) + par[2:3, :])
    mid[...] = v
    hat, _ = norm_stats(v)
    normed[...] = (hat * par[3:4, :] + par[4:5, :]).astype(bf16)


def stack(*refs, cols=slice(None)):
    return jnp.concatenate([r[:, cols] for r in refs], axis=0)


def mlp_own_kernel(
    idx, n2_a, n2_b, cot, up_own, down_own, first, first_sib, second, second_sib,
    b_up, hid, gpre, gn2, up_oth, down_oth,
):
    for core, one, two in ((idx[3], first, second), (1 - idx[3], first_sib, second_sib)):
        start = core * 384
        up_oth[pl.ds(pl.multiple_of(start, 128), 128), :] = one[96:224, :]
        up_oth[pl.ds(pl.multiple_of(start + 128, 128), 256), :] = two[0:256, :]
        down_oth[pl.ds(pl.multiple_of(start, 128), 384), :] = two[256:640, :]
    mlp(stack(n2_a, n2_b), cot[...], up_own, up_oth, down_own, down_oth, b_up, hid, gpre, gn2)


def mlp_kernel(k, n2, cot, up_own, up_oth, down_own, down_oth, b_up, hid, gpre, gn2):
    mlp(n2[...], cot[128 * k : 128 * k + 128, :], up_own, up_oth, down_own, down_oth, b_up, hid, gpre, gn2)


def mlp(rows, cots, up_own, up_oth, down_own, down_oth, b_up, hid, gpre, gn2):
    total = jnp.zeros(rows.shape, f32)
    bias = [jnp.concatenate([b_up[s, 9 + t : 10 + t, :] for t in range(6)], axis=1) for s in range(2)]
    for s, up, down in ((0, up_own, down_own), (1, up_oth, down_oth)):
        for t in range(3):
            cols = slice(256 * t, 256 * t + 256)
            at = slice(768 * s + 256 * t, 768 * s + 256 * t + 256)
            pre = nn(rows, up[:, cols]) + bias[s][:, cols]
            grad = nt(cots, down[cols, :])
            square = pre * pre
            th = jnp.tanh(ROOT * (pre + 0.044715 * (square * pre)))
            half = 0.5 * (1.0 + th)
            hid[:, at] = (pre * half).astype(bf16)
            slope = half + 0.5 * pre * (1.0 - th * th) * (ROOT * (1.0 + 3 * 0.044715 * square))
            g = (grad * slope).astype(bf16)
            gpre[:, at] = g
            total += nt(g, up[:, cols])
    gn2[...] = total.astype(gn2.dtype)


def down_kernel(hid_own, hid_a, hid_b, down_own, down_oth, own, oth):
    hid = stack(hid_a, hid_b)
    oth[...] = (nn(hid[:, 0:768], down_own[...]) + nn(hid[:, 768:1536], down_oth[...])).astype(bf16)
    own[...] = nn(hid_own[:, 0:768], down_own[...]) + nn(hid_own[:, 768:1536], down_oth[...])


def final_kernel(mid_a, mid_b, own, recv, par, out):
    for k, mid in enumerate((mid_a, mid_b)):
        rows = slice(128 * k, 128 * k + 128)
        out[rows, :] = (mid[...] + (own[rows, :] + recv[rows, :].astype(f32)) + par[5:6, :]).astype(bf16)


def norm_grad(v, gain, grad):
    hat, inv = norm_stats(v)
    e = grad * gain
    back = inv * (e - jnp.mean(e, axis=-1, keepdims=True) - hat * jnp.mean(e * hat, axis=-1, keepdims=True))
    return back, jnp.sum(grad * hat, axis=0, keepdims=True), jnp.sum(grad, axis=0, keepdims=True)


def put_vector(ref, row, vec):
    for t in range(vec.shape[1] // 128):
        ref[row + t : row + t + 1, :] = vec[:, 128 * t : 128 * t + 128]


def ln_two_back_kernel(k, mid, own, recv, par, cot, *more):
    *before, gmid, branch, vecs = more
    rows = slice(128 * k, 128 * k + 128)
    cots = cot[rows, :].astype(f32)
    back, dgain, dbias = norm_grad(mid[...], par[3:4, :], own[rows, :] + recv[...].astype(f32))
    g = cots + back
    gmid[...] = g
    low = g.astype(bf16)
    branch[...] = low
    put_vector(vecs, 0, jnp.sum(low.astype(f32), axis=0, keepdims=True))
    put_vector(vecs, 6, dgain)
    put_vector(vecs, 12, dbias)
    put_vector(vecs, 18, jnp.sum(cots, axis=0, keepdims=True))
    for earlier in before:
        vecs[...] += earlier[...]


def ln_one_back_kernel(tok, own, recv, par, gmid_a, gmid_b, vecs_two, out, vecs):
    back, dgain, dbias = norm_grad(tok[...].astype(f32), par[0:1, :], own[...] + recv[...].astype(f32))
    out[...] = stack(gmid_a, gmid_b) + back
    vecs[0:24, :] = vecs_two[...]
    put_vector(vecs, 24, dgain)
    put_vector(vecs, 30, dbias)
    vecs[36:40, :] = jnp.zeros((4, 128), f32)


def down_grad(idx, half, s, hid_own, hid_a, hid_b, cot_own, cot_oth):
    at = pl.ds(pl.multiple_of(half * 384 + 768 * s, 384), 384)
    return tn(hid_own[:, at], cot_own[...]) + tn(stack(hid_a, hid_b, cols=at), cot_oth[...])


def up_grad(idx, half, s, own_a, own_b, oth_a, oth_b, gpre_own, gpre_a, gpre_b):
    at = pl.ds(pl.multiple_of(half * 384, 384), 384)
    cols = slice(768 * s, 768 * s + 768)
    total = tn(stack(own_a, own_b, cols=at), gpre_own[:, cols])
    return total + tn(stack(oth_a, oth_b, cols=at), stack(gpre_a, gpre_b, cols=cols))


def mlp_send_kernel(grad, idx, *args):
    *args, send = args
    for s in range(2):
        send[s] = grad(idx, 1 - idx[3], s, *args).astype(bf16)


def mlp_keep_kernel(grad, idx, *args):
    *args, recv, keep, send = args
    send[...] = (grad(idx, idx[3], 1, *args) + recv[1].astype(f32)).astype(bf16)
    keep[...] = grad(idx, idx[3], 0, *args) + recv[0].astype(f32)


def grad_mixed_kernel(idx, seg, own_a, own_b, oth_a, oth_b, w_own, w_oth, att, fq, segc, gbcat, gna, pay, pay_far):
    x, y = idx[0], idx[1]
    lane = lanes()
    low = lane < 64
    for start, a, b in ((x, own_a, own_b), (1 - x, oth_a, oth_b)):
        gbcat[pl.ds(pl.multiple_of(start * 256, 128), 128), :] = a[...]
        gbcat[pl.ds(pl.multiple_of(start * 256 + 128, 128), 128), :] = b[...]
    first = seg[y * 512].astype(f32)
    open_rows = (segc[...] == first).astype(f32)
    tops, norms = [], []
    for s, w in ((0, w_own), (1, w_oth)):
        g01 = nt(gbcat[...], w[0:128, :]).astype(bf16).astype(f32)
        g12 = nt(gbcat[...], w[64:192, :]).astype(bf16).astype(f32)
        for h, gm in ((0, g01), (1, g12), (2, half_turn(g12))):
            g = 3 * s + h
            a = att[g]
            gn = jnp.where(low, gm * a[:, 64:65], 0.0).astype(bf16).astype(f32)
            gd = -jnp.sum(gn * a, axis=1, keepdims=True)
            high = gd.astype(bf16).astype(f32)
            tail = jnp.where((lane == 64) | (lane == 66), high, jnp.where(lane == 65, gd - high, 0.0))
            gna[g] = jnp.where(low, gn, tail).astype(bf16)
            st = tn(gna[g], (fq[g].astype(f32) * open_rows).astype(bf16))
            tops.append(st[0:64])
            norms.append(st[64:65] + st[65:66])
    encode(pay, tops, norms)
    encode(pay_far, tops, norms, far_scale(False, seg, y))


def soft_grad(soft, grad):
    s = soft.astype(f32)
    return (s * (grad - jnp.sum(grad * s, axis=1, keepdims=True))).astype(bf16)


def query_back_kernel(idx, seg, segc, segr, fq, fk, va, gna, paug, wfe, gq, gpq):
    y = idx[1]
    first = seg[y * 512].astype(f32)
    for it in range(2):
        rows = slice(256 * it, 256 * it + 256)
        wide = 256 * (it + 1)
        i = lax.broadcasted_iota(jnp.int32, (256, wide), 0) + 256 * it
        j = lax.broadcasted_iota(jnp.int32, (256, wide), 1)
        mask = ((j <= i) & (segc[rows, :] == segr[:, 0:wide])).astype(f32)
        open_rows = (segc[rows, :] == first).astype(f32)
        for g in range(6):
            gw = (nt(gna[g, rows, :], va[g, 0:wide, :]) * mask).astype(bf16)
            grad = nn(gw, fk[g, 0:wide, :]) + open_rows * nn(gna[g, rows, :], paug[g])
            gq[g, rows, :] = soft_grad(fq[g, rows, :], grad)
        for s in range(2):
            pair = jnp.concatenate([gq[3 * s, rows, :], gq[3 * s + 1, rows, :]], axis=1)
            gpq[rows, 256 * s : 256 * s + 128] = nt(pair, wfe[s, :, 0:256]).astype(bf16)
            gpq[rows, 256 * s + 128 : 256 * s + 256] = nt(gq[3 * s + 2, rows, :], wfe[s, :, 256:384]).astype(bf16)


def key_back_kernel(segc, segr, fq, fk, va, gna, gkf, gv):
    for it in range(2):
        rows = slice(256 * it, 256 * it + 256)
        late = slice(256 * it, 512)
        tall = 512 - 256 * it
        j = lax.broadcasted_iota(jnp.int32, (256, tall), 0)
        i = lax.broadcasted_iota(jnp.int32, (256, tall), 1)
        mask = ((j <= i) & (segc[rows, :] == segr[:, 256 * it : 512])).astype(f32)
        for g in range(6):
            w = (nt(fk[g, rows, :], fq[g, late, :]) * mask).astype(bf16)
            gv[g, rows, :] = nn(w, gna[g, late, :])
            gw = (nt(va[g, rows, :], gna[g, late, :]) * mask).astype(bf16)
            gkf[g, rows, :] = nn(gw, fq[g, late, :])


def qkv_back_kernel(
    idx, seg, theirs, one, one_theirs, two, segc, fk, va, gkf, gv, gpq, wfe, wx,
    gk, gpkv, part_own, part_oth,
):
    x, y = idx[0], idx[1]
    tops, norms = carry_state(False, idx, seg, theirs, one, one_theirs, two)
    low = lanes() < 64
    last = seg[y * 512 + 511].astype(f32)
    open_rows = (segc[...] == last).astype(f32)
    for s in range(2):
        base = 512 * s
        values = []
        for h in range(3):
            g = 3 * s + h
            aug = augmented(tops[g], norms[g], False)
            gk[g] = soft_grad(fk[g], gkf[g] + open_rows * nn(va[g], aug))
            values.append(jnp.where(low, gv[g] + open_rows * nt(fk[g], aug), 0.0))
        gpkv[:, base + 256 : base + 384] = (values[0] + half_turn(values[1])).astype(bf16)
        gpkv[:, base + 384 : base + 512] = half_turn(values[2]).astype(bf16)
        pair = jnp.concatenate([gk[3 * s], gk[3 * s + 1]], axis=1)
        gpkv[:, base : base + 128] = nt(pair, wfe[s, :, 0:256]).astype(bf16)
        gpkv[:, base + 128 : base + 256] = nt(gk[3 * s + 2], wfe[s, :, 256:384]).astype(bf16)

    def term(start):
        rows = pl.ds(pl.multiple_of(start * 256, 256), 256)
        total = nn(gpq[rows, 0:256], wx[0, 0:256, :]) + nn(gpkv[rows, 0:512], wx[0, 256:768, :])
        return total + (nn(gpq[rows, 256:512], wx[1, 0:256, :]) + nn(gpkv[rows, 512:1024], wx[1, 256:768, :]))

    part_oth[...] = term(1 - x).astype(bf16)
    part_own[...] = term(x)


def split_rows(c, scr, base, rows, at, keep, send, s):
    half = rows // 2
    keep[s, at : at + half, :] = scr[pl.ds(pl.multiple_of(base + half * c, 32), half), :]
    send[s, at : at + half, :] = scr[pl.ds(pl.multiple_of(base + half * (1 - c), 32), half), :].astype(bf16)


def early_weights_kernel(idx, n, gpq, mixed, gb, keep, send, scr):
    for s in range(2):
        cols = slice(256 * s, 256 * s + 256)
        for k, (a, b) in enumerate(((gpq, n), (mixed, gb))):
            grad = tn(a[:, cols], b[...])
            scr[192 * k : 192 * k + 128, :] = grad[0:128]
            scr[192 * k + 128 : 192 * k + 192, :] = grad[192:256]
            split_rows(idx[3], scr, 192 * k, 192, 96 * k, keep, send, s)


def late_weights_kernel(idx, n, gpq, gpkv, u, gq, gk, gpre_own, gpre_a, gpre_b, keep, send, scr):
    row = lax.broadcasted_iota(jnp.int32, (16, 128), 0)
    for s in range(2):
        grad = tn(gpkv[:, 512 * s : 512 * s + 512], n[...])
        for k in range(2):
            scr[192 * k : 192 * k + 128, :] = grad[256 * k : 256 * k + 128]
            scr[192 * k + 128 : 192 * k + 192, :] = grad[256 * k + 192 : 256 * k + 256]
        first = jnp.zeros((128, 256), f32)
        third = jnp.zeros((128, 128), f32)
        sums = []
        for k, g in ((0, gq), (1, gk)):
            at = 512 * s + 256 * k
            pair = jnp.concatenate([g[3 * s], g[3 * s + 1]], axis=1)
            first += tn(u[:, at : at + 128], pair)
            third += tn(u[:, at + 128 : at + 256], g[3 * s + 2])
            sums.append([jnp.sum(g[3 * s + h].astype(f32), axis=0, keepdims=True) for h in range(3)])
        low = lanes() < 64
        block = first[0:64, 0:128]
        zero = block - half_turn(block)
        block = first[64:128, 128:256]
        one = block - half_turn(block)
        block = third[64:128]
        two = block - half_turn(block)
        scr[384:448, 0:128] = jnp.where(low, zero, half_turn(one))
        scr[384:448, 128:256] = jnp.where(low, two, 0.0)
        scr[384:448, 256:768] = jnp.zeros((64, 512), f32)
        rows = []
        for t in range(6):
            tile = gpq[:, 256 * s + 128 * t : 256 * s + 128 * t + 128] if t < 2 else (
                gpkv[:, 512 * s + 128 * t - 256 : 512 * s + 128 * t - 128])
            rows.append(jnp.sum(tile.astype(f32), axis=0, keepdims=True))
        for h in range(3):
            total = jnp.broadcast_to(sums[0][h] + sums[1][h], (8, 128))
            rows.append((total - half_turn(total))[0:1])
        block = jnp.zeros((16, 128), f32)
        for t, value in enumerate(rows):
            block = jnp.where(row == t, value, block)
        scr[384:400, 256:384] = block
        cols = slice(768 * s, 768 * s + 768)
        bias = jnp.sum(gpre_own[:, cols].astype(f32), axis=0, keepdims=True)
        for part in (gpre_a, gpre_b):
            bias += jnp.sum(part[:, cols].astype(f32), axis=0, keepdims=True)
        block = jnp.zeros((16, 128), f32)
        for t in range(6):
            block = jnp.where(row == t, bias[:, 128 * t : 128 * t + 128], block)
        scr[384:400, 384:512] = block
        split_rows(idx[3], scr, 0, 192, 0, keep, send, s)
        split_rows(idx[3], scr, 192, 192, 96, keep, send, s)
        split_rows(idx[3], scr, 384, 64, 192, keep, send, s)


def pair_kernel(keep, recv, mine, across):
    mine[...] = keep[0] + recv[0].astype(f32)
    across[...] = (keep[1] + recv[1].astype(f32)).astype(bf16)


def cp_split_kernel(idx, keep, recv, mine, sent):
    rows = mine.shape[0]
    low = pl.multiple_of((idx[2] & 1) * rows, 16)
    high = pl.multiple_of((1 - (idx[2] & 1)) * rows, 16)
    sent[...] = (keep[pl.ds(high, rows), :] + recv[pl.ds(high, rows), :].astype(f32)).astype(bf16)
    mine[...] = keep[pl.ds(low, rows), :] + recv[pl.ds(low, rows), :].astype(f32)


def add_kernel(mine, recv, out):
    out[...] = (mine[...].astype(f32) + recv[...].astype(f32)).astype(out.dtype)


def place(idx, whole, pieces):
    half, pair, sib, sib_pair = pieces
    rows = half.shape[0]
    low, c = idx[2] & 1, idx[3]
    for core, zlow, piece in ((c, low, half), (c, 1 - low, pair), (1 - c, low, sib), (1 - c, 1 - low, sib_pair)):
        whole[pl.ds(pl.multiple_of((core * 2 + zlow) * rows, 16), rows), :] = piece[...].astype(whole.dtype)


def send_out(pairs, sems):
    copies = [pltpu.make_async_copy(a, b, sems.at[k]) for k, (a, b) in enumerate(pairs)]
    for copy in copies:
        copy.start()
    for copy in copies:
        copy.wait()


def join_kernel(idx, half, pair, out):
    join_halves(idx[2] & 1, out, half, pair)


def spread_kernel(idx, mine, sibling, out, whole, sems):
    for core, rows in ((idx[3], mine), (1 - idx[3], sibling)):
        whole[pl.ds(pl.multiple_of(core * 384, 384), 384), :] = rows[...].astype(f32)
    send_out([(whole, out)], sems)


def spread_attention_kernel(idx, *refs):
    early, late = refs[0:4], refs[4:8]
    outs, (first, second, w_qkv, w_out, feat, b_qkv, b_feat, b_up, sems) = refs[8:14], refs[14:]
    place(idx, first, early)
    place(idx, second, late)
    for c in range(2):
        w_qkv[96 * c : 96 * c + 96, :] = first[192 * c : 192 * c + 96, :]
        w_out[96 * c : 96 * c + 96, :] = first[192 * c + 96 : 192 * c + 192, :]
        w_qkv[192 + 96 * c : 288 + 96 * c, :] = second[224 * c : 224 * c + 96, :]
        w_qkv[384 + 96 * c : 480 + 96 * c, :] = second[224 * c + 96 : 224 * c + 192, :]
    more = jnp.concatenate([second[192:224, :], second[416:448, :]], axis=0)
    feat[0] = more[:, 0:64]
    feat[1] = half_turn(more[:, 0:128])[:, 0:64]
    feat[2] = more[:, 128:192]
    sums = more[0:16, 256:384]
    turned = half_turn(sums)
    for k in range(3):
        b_qkv[k : k + 1, 0:128] = sums[2 * k : 2 * k + 1]
        b_qkv[k : k + 1, 128:192] = turned[2 * k + 1 : 2 * k + 2, 0:64]
    b_feat[...] = sums[6:9, 0:64]
    for t in range(6):
        b_up[128 * t : 128 * t + 128] = more[t : t + 1, 384:512].reshape(128)
    send_out(list(zip((w_qkv, w_out, feat, b_qkv, b_feat, b_up), outs)), sems)


def after(value, *deps):
    return lax.optimization_barrier((value,) + deps)[0]


def swap(value, axis, bit):
    count = lax.axis_size(axis)
    return jax.tree.map(
        lambda v: lax.ppermute(v, axis, [(i, i ^ bit) for i in range(count)]), value
    )


def diagonal(value):
    tp, cp = lax.axis_size("tp"), lax.axis_size("cp")
    pairs = [(t * cp + z, (t ^ 2) * cp + (z ^ 1)) for t in range(tp) for z in range(cp)]
    return lax.ppermute(value, ("tp", "cp"), pairs)


def rest_of_dp(value):
    bit = 2
    while bit < lax.axis_size("dp"):
        value = value + swap(value.astype(bf16), "dp", bit).astype(f32)
        bit *= 2
    return value


def shards(
    tokens, segment_ids, ln1_gain, ln1_bias, w_qkv, b_qkv, w_feat, b_feat, output_weight, b_out,
    ln2_gain, ln2_bias, w_up, b_up, w_down, b_down, cotangent,
):
    t = lax.axis_index("tp")
    z = lax.axis_index("cp")
    c = lax.axis_index("dp") & 1
    x, y = t & 1, t >> 1
    idx = jnp.stack([x, y, z, c, c, c, c, c]).astype(jnp.int32)
    tok = tokens.reshape(256, 768)
    cot_own = cotangent.reshape(256, 768)
    seg = segment_ids.reshape(1024)

    wq = jnp.transpose(w_qkv, (1, 2, 0)).reshape(576, 768)
    done = []

    def run(kernel, outs, args, needs=(), **options):
        args = list(args)
        args[-1] = after(args[-1], *needs, *done)
        result = call(kernel, outs, args, **options)
        done[:] = [result[0]]
        return result

    def array(*shape, kind=bf16):
        return (shape, kind)

    rows_b, rows_f = array(256, 768), array(256, 768, kind=f32)
    part_b, part_f = array(128, 768), array(128, 768, kind=f32)
    head_rows, head_rows_f = array(6, 512, 128), array(6, 512, 128, kind=f32)

    n_own, buf, signed, flat, par, segc, segr, first_part, second_part = run(
        prep_kernel,
        [
            rows_b, array(336, 768), array(192, 128), array(16, 128, kind=f32), array(8, 768, kind=f32),
            array(512, 1, kind=f32), array(1, 512, kind=f32), array(224, 768), array(640, 768),
        ],
        [
            idx, tok, ln1_gain, ln1_bias, b_out, ln2_gain, ln2_bias, b_down, wq, w_feat, b_qkv, b_feat, b_up,
            segment_ids.reshape(1, 1024), output_weight, w_up, w_down,
        ],
        smem=1, hbm=16, name="prep",
        scratch=[
            pltpu.VMEM((256, 768), bf16), [pltpu.VMEM((768,), f32)] * 7, pltpu.VMEM((3, 64, 64), bf16),
            pltpu.VMEM((3, 192), f32), pltpu.VMEM((3, 64), f32), pltpu.VMEM((1, 1024), jnp.int32),
            pltpu.SemaphoreType.DMA((17,)),
        ],
    )
    n_oth = swap(n_own, "tp", 1)
    buf_y = swap(buf, "tp", 2)
    buf_sib = swap(after(buf_y, n_oth), "dp", 1)
    first_mine = swap(after(first_part, buf_y), "tp", 2)
    ncat, u, fq, fk, va, arow, pay, pay_far, wx, wfe, bup = run(
        qkv_kernel,
        [
            array(512, 768), array(512, 1024), head_rows, head_rows, head_rows, array(6, 1, 128, kind=f32),
            PAY_OUT, PAY_OUT, array(2, 768, 768), array(2, 128, 384), array(2, 16, 128, kind=f32),
        ],
        [idx, seg, n_own, n_oth, wq, buf_y, buf_sib, signed, flat, par, segc],
        smem=2, scratch=[pltpu.VMEM((576, 768), bf16)], name="qkv",
    )
    around = [swap(pay, "tp", 2), swap(pay_far, "cp", 1), diagonal(pay_far)]
    first_pair = (first_mine, swap(after(first_mine, pay), "dp", 1))
    second_mine = swap(after(second_part, around[0]), "tp", 2)
    cot_oth = swap(after(cot_own, pay), "tp", 1)
    (numden,) = run(inner_kernel, [head_rows_f], [segc, segr, fq, fk, va], name="inner")
    (state,) = run(
        functools.partial(send_state_kernel, True), [PAY_OUT], [idx, seg, pay_far, *around], smem=2, weight=1, name="state"
    )
    carried = [*around, swap(state, "cp", 2)]
    att, mixed, paug, part_own, send_a, send_b, wo_oth = run(
        out_kernel,
        [head_rows_f, array(512, 512), array(6, 128, 128), rows_f, part_b, part_b, array(192, 768)],
        [idx, seg, *carried, numden, fq, arow, segc, output_weight, *first_pair],
        needs=(cot_oth,), smem=2, weight=0, name="out",
    )
    part_in = [swap(send_a, "tp", 1), swap(send_b, "tp", 1)]

    mid, n2_own = [None, None], [None, None]
    for k in range(2):
        mid[k], n2_own[k] = run(
            functools.partial(ln_two_kernel, k), [part_f, part_b], [tok, part_own, part_in[k], par],
            needs=(second_mine,), weight=4, name="ln_two",
        )
    second_pair = (second_mine, swap(after(second_mine, n2_own[0]), "dp", 1))
    n2_oth = [swap(v, "tp", 1) for v in n2_own]
    units = array(128, 1536)
    v = {}
    tasks = {}

    def task(fn):
        tasks[fn.__name__] = fn
        return fn

    def weight(name):
        return WEIGHTS.get(name, 1)

    def go(name, kernel, outs, args, **options):
        return run(kernel, outs, args, weight=weight(name), name=name, **options)

    @task
    def mlp_own():
        v["hid"], v["gpre"], v["gn2"], v["up"], v["down"] = go(
            "mlp_own", mlp_own_kernel,
            [array(256, 1536), array(256, 1536), rows_f, array(768, 768), array(768, 768)],
            [idx, *n2_own, cot_own, w_up, w_down, *first_pair, *second_pair, bup], smem=1,
        )

    def mlp_part(k):
        name = f"mlp_{k}"
        v["hid", k], v["gpre", k], out = go(
            name, functools.partial(mlp_kernel, k), [units, units, part_b],
            [n2_oth[k], cot_oth, w_up, v["up"], w_down, v["down"], bup],
        )
        v["gn2", k] = swap(out, "tp", 1)

    tasks["mlp_0"] = lambda: mlp_part(0)
    tasks["mlp_1"] = lambda: mlp_part(1)

    def down_args():
        return [idx, v["hid"], v["hid", 0], v["hid", 1], cot_own, cot_oth]

    def up_args():
        return [idx, *n2_own, *n2_oth, v["gpre"], v["gpre", 0], v["gpre", 1]]

    def grad_send(name, grad, args):
        (send,) = go(
            name + "_send", functools.partial(mlp_send_kernel, grad), [array(2, 384, 768)], args, smem=1
        )
        v[name, "dp"] = swap(send, "dp", 1)

    def grad_keep(name, grad, args):
        keep, across = go(
            name + "_keep", functools.partial(mlp_keep_kernel, grad), [array(384, 768, kind=f32), array(384, 768)],
            args + [v[name, "dp"]], smem=1,
        )
        v[name, "y"] = keep, swap(across, "tp", 2)

    tasks["down_send"] = lambda: grad_send("down", down_grad, down_args())
    tasks["up_send"] = lambda: grad_send("up", up_grad, up_args())
    tasks["down_keep"] = lambda: grad_keep("down", down_grad, down_args())
    tasks["up_keep"] = lambda: grad_keep("up", up_grad, up_args())

    def ln_two_back(k):
        before = [v["vecs_two", 0]] if k else []
        v["gmid", k], branch, v["vecs_two", k] = go(
            f"ln_two_back_{k}", functools.partial(ln_two_back_kernel, k), [part_f, part_b, array(24, 128, kind=f32)],
            [mid[k], v["gn2"], v["gn2", k], par, cot_own, *before],
        )
        v["gb", k] = branch, swap(branch, "tp", 1)

    tasks["ln_two_back_0"] = lambda: ln_two_back(0)
    tasks["ln_two_back_1"] = lambda: ln_two_back(1)

    @task
    def down():
        v["down_own"], part = go(
            "down", down_kernel, [rows_f, rows_b], [v["hid"], v["hid", 0], v["hid", 1], w_down, v["down"]]
        )
        v["down_in"] = swap(part, "tp", 1)

    @task
    def grad_mixed():
        own, oth = zip(v["gb", 0], v["gb", 1])
        v["gbcat"], v["gna"], pay_near, far = go(
            "grad_mixed", grad_mixed_kernel, [array(512, 768), head_rows, PAY_OUT, PAY_OUT],
            [idx, seg, *own, *oth, output_weight, wo_oth, att, fq, segc], smem=2,
        )
        v["around"] = [swap(pay_near, "tp", 2), swap(far, "cp", 1), diagonal(far)]
        v["far"] = far

    @task
    def key_back():
        v["gkf"], v["gv"] = go(
            "key_back", key_back_kernel, [head_rows_f, head_rows_f], [segc, segr, fq, fk, va, v["gna"]]
        )

    @task
    def gstate():
        (state,) = go(
            "gstate", functools.partial(send_state_kernel, False), [PAY_OUT], [idx, seg, v["far"], *v["around"]],
            smem=2,
        )
        v["coming"] = [*v["around"], swap(state, "cp", 2)]

    @task
    def query_back():
        v["gq"], v["gpq"] = go(
            "query_back", query_back_kernel, [head_rows, array(512, 512)],
            [idx, seg, segc, segr, fq, fk, va, v["gna"], paug, wfe], smem=2,
        )

    @task
    def early_weights():
        keep, send = go(
            "early_weights", early_weights_kernel, [array(2, 192, 768, kind=f32), array(2, 192, 768)],
            [idx, ncat, v["gpq"], mixed, v["gbcat"]], smem=1, scratch=[pltpu.VMEM((384, 768), f32)],
        )
        v["early", "dp"] = keep, swap(send, "dp", 1)

    @task
    def qkv_back():
        v["gk"], v["gpkv"], v["gn1"], oth = go(
            "qkv_back", qkv_back_kernel, [head_rows, array(512, 1024), rows_f, rows_b],
            [idx, seg, *v["coming"], segc, fk, va, v["gkf"], v["gv"], v["gpq"], wfe, wx], smem=2,
        )
        v["gn1_in"] = swap(oth, "tp", 1)

    @task
    def late_weights():
        keep, send = go(
            "late_weights", late_weights_kernel, [array(2, 224, 768, kind=f32), array(2, 224, 768)],
            [idx, ncat, v["gpq"], v["gpkv"], u, v["gq"], v["gk"], v["gpre"], v["gpre", 0], v["gpre", 1]],
            smem=1, scratch=[pltpu.VMEM((448, 768), f32)],
        )
        v["late", "dp"] = keep, swap(send, "dp", 1)

    @task
    def ln_one_back():
        v["d_tok"], v["vecs"] = go(
            "ln_one_back", ln_one_back_kernel, [rows_f, array(40, 128, kind=f32)],
            [tok, v["gn1"], v["gn1_in"], par, v["gmid", 0], v["gmid", 1], v["vecs_two", 1]],
        )

    @task
    def final():
        (v["out"],) = go("final", final_kernel, [rows_b], [*mid, v["down_own"], v["down_in"], par])

    def pair(name):
        keep, recv = v[name, "dp"]
        rows = keep.shape[1]
        mine, across = go(
            name + "_pair", pair_kernel, [array(rows, 768, kind=f32), array(rows, 768)], [keep, recv]
        )
        v[name, "y"] = mine, swap(across, "tp", 2)

    def split(name):
        keep, recv = v[name, "y"]
        rows = keep.shape[0] // 2
        if lax.axis_size("dp") > 2:
            keep, recv = rest_of_dp(keep + recv.astype(f32)), jnp.zeros_like(recv)
        mine, sent = go(
            name + "_split", cp_split_kernel, [array(rows, 768, kind=f32), array(rows, 768)], [idx, keep, recv],
            smem=1,
        )
        v[name, "z"] = mine, swap(sent, "cp", 1)

    def add(name):
        mine, recv = v[name, "z"]
        (half,) = go(name + "_add", add_kernel, [(mine.shape, bf16)], [mine, recv])
        v[name, "zz"] = half, swap(half, "cp", 2)

    def last(name):
        mine, recv = v[name, "zz"]
        (half,) = go(name + "_last", add_kernel, [(mine.shape, bf16)], [mine, recv])
        v[name, "half"] = half, swap(half, "cp", 1)

    def join(name):
        rows = v[name, "half"][0].shape[0] * 2
        (mine,) = go(name + "_join", join_kernel, [array(rows, 768)], [idx, *v[name, "half"]], smem=1)
        v[name, "rows"] = mine, swap(mine, "dp", 1)

    def spread(name):
        (v[name, "sum"],) = go(
            name + "_spread", spread_kernel, [array(768, 768, kind=f32)], [idx, *v[name, "rows"]],
            smem=1, hbm_out=True, scratch=[pltpu.VMEM((768, 768), f32), pltpu.SemaphoreType.DMA((1,))],
        )

    def pieces(name):
        half, other = v[name, "half"]
        return half, other, swap(half, "dp", 1), swap(other, "dp", 1)

    for step in (pair, split, add, last, join, spread):
        for name in ("down", "up", "early", "late"):
            tasks[f"{name}_{step.__name__}"] = functools.partial(step, name)

    hops = [(axis, 1 << k) for axis in ("tp", "dp", "cp") for k in range(lax.axis_size(axis).bit_length() - 1)]

    @task
    def vec():
        if hops:
            pending = swap(v["vecs"], *hops.pop(0))
            (v["vecs"],) = go("vec", add_kernel, [array(40, 128, kind=f32)], [v["vecs"], pending])

    given = [(576, 768), (192, 768), (3, 64, 64), (3, 192), (3, 64), (768,)]

    @task
    def attention():
        while hops:
            vec()
        v["attention"] = go(
            "attention", spread_attention_kernel, [array(*shape, kind=f32) for shape in given],
            [idx, *pieces("early"), *pieces("late")], smem=1, hbm_out=True,
            scratch=[pltpu.VMEM((384, 768), f32), pltpu.VMEM((448, 768), f32)]
            + [pltpu.VMEM(shape, f32) for shape in given] + [pltpu.SemaphoreType.DMA((6,))],
        )

    for name in ORDER:
        tasks[name]()

    d_wq, d_w_out, d_feat, d_b_qkv, d_b_feat, d_b_up = v["attention"]
    vec_rows = v["vecs"][:36].reshape(6, 768)
    return (
        v["out"].reshape(tokens.shape),
        v["d_tok"].reshape(tokens.shape),
        vec_rows[4],
        vec_rows[5],
        jnp.transpose(d_wq.reshape(3, 192, 768), (2, 0, 1)),
        d_b_qkv,
        d_feat,
        d_b_feat,
        d_w_out,
        vec_rows[0],
        vec_rows[1],
        vec_rows[2],
        v["up", "sum"],
        d_b_up,
        v["down", "sum"],
        vec_rows[3],
    )


def solution(mesh):
    rows = P(("cp", "tp"), "dp", None)
    placed = (
        rows, P("cp", "dp"), P(), P(), P(None, None, "tp"), P(None, "tp"), P("tp", None, None),
        P("tp", None), P("tp", None), P(), P(), P(), P(None, "tp"), P("tp"), P("tp", None), P(), rows,
    )
    given = (
        rows, rows, P(), P(), P(None, None, "tp"), P(None, "tp"), P("tp", None, None), P("tp", None),
        P("tp", None), P(), P(), P(), P(None, "tp"), P("tp"), P("tp", None), P(),
    )
    return jax.shard_map(shards, mesh=mesh, in_specs=placed, out_specs=given, check_vma=False)
```

```python
import functools
import math
import types

import jax
import jax.numpy as jnp
from jax import lax
from jax.experimental import pallas as pl
from jax.experimental.pallas import tpu as pltpu
from jax.sharding import PartitionSpec as P

f32 = jnp.float32
bf16 = jnp.bfloat16
EPS = 1e-05
ROOT = math.sqrt(2.0 / math.pi)
VMEM_LIMIT = 12 * 1024 * 1024


def nn(a, b):
    return jnp.dot(a, b, preferred_element_type=f32)


def nt(a, b):
    return lax.dot_general(a, b, (((1,), (1,)), ((), ())), preferred_element_type=f32)


def tn(a, b):
    return lax.dot_general(a, b, (((0,), (0,)), ((), ())), preferred_element_type=f32)


def call(kernel, outs, args, smem=0, hbm=0, hbm_out=False, scratch=(), weight=1):
    args = [
        pltpu.with_memory_space_constraint(a, pltpu.HBM) if smem <= k < smem + hbm else a for k, a in enumerate(args)
    ]
    specs = [pl.BlockSpec(memory_space=pltpu.SMEM)] * smem
    specs += [pl.BlockSpec(memory_space=pltpu.HBM)] * hbm
    specs += [pl.BlockSpec(memory_space=pltpu.VMEM)] * (len(args) - smem - hbm)
    out_shape = [jax.ShapeDtypeStruct(shape, kind) for shape, kind in outs]
    return pl.pallas_call(
        kernel,
        out_shape=out_shape,
        in_specs=specs,
        out_specs=[pl.BlockSpec(memory_space=pltpu.HBM if hbm_out else pltpu.VMEM)] * len(outs),
        scratch_shapes=list(scratch),
        compiler_params=pltpu.CompilerParams(vmem_limit_bytes=VMEM_LIMIT),
        cost_estimate=pl.CostEstimate(flops=max(1, weight * 10**10), bytes_accessed=10**8, transcendentals=0),
    )(*args)


def lanes():
    return lax.broadcasted_iota(jnp.int32, (1, 128), 1)


def half_turn(v):
    return pltpu.roll(v, 64, 1)


def norm_stats(v):
    centred = v - jnp.mean(v, axis=-1, keepdims=True)
    inv = lax.rsqrt(jnp.mean(centred * centred, axis=-1, keepdims=True) + EPS)
    return centred * inv, inv


def encode(pay, tops, norms, scale=None):
    if scale is not None:
        tops, norms = [scale * t for t in tops], [scale * n for n in norms]
    for g in range(6):
        pay[g * 64 : g * 64 + 64, :] = tops[g].astype(bf16)
    row = lax.broadcasted_iota(jnp.int32, (16, 128), 0)
    for s in range(2):
        block = jnp.zeros((16, 128), f32)
        for h in range(3):
            n = norms[3 * s + h]
            high = n.astype(bf16).astype(f32)
            block = jnp.where(row == h, high, block)
            block = jnp.where(row == 3 + h, n - high, block)
        pay[384 + 16 * s : 400 + 16 * s, :] = block.astype(bf16)


def decode(pay, swap=False):
    tops, norms = [], []
    blocks = [pay[384 + 16 * s : 400 + 16 * s, :].astype(f32) for s in range(2)]
    for s in range(2):
        t = 1 - s if swap else s
        for h in range(3):
            g = 3 * t + h
            tops.append(pay[g * 64 : g * 64 + 64, :].astype(f32))
            norms.append(blocks[t][h : h + 1, :] + blocks[t][3 + h : 4 + h, :])
    return tops, norms


PAY = (416, 128)
PAY_OUT = (PAY, bf16)


def combine(parts):
    tops = [sum(f * p[0][g] for f, p in parts) for g in range(6)]
    norms = [sum(f * p[1][g] for f, p in parts) for g in range(6)]
    return tops, norms


def prep_kernel(
    idx, tok, gain, bias, b_out, gain2, bias2, b_down, w_qkv, w_feat, b_qkv, b_feat, b_up, seg, w_out, w_up, w_down,
    out, buf, signed, flat, par, segc, segr, first_part, second_part,
    tok_v, vecs, feat_v, bq_v, bf_v, seg_v, sems,
):
    half = w_qkv.at[pl.ds(pl.multiple_of(idx[3] * 288, 32), 288), :]
    pairs = [(tok, tok_v), (w_feat, feat_v), (b_qkv, bq_v), (b_feat, bf_v), (seg, seg_v), (half, buf.at[0:288, :])]
    pairs += [(v, vecs[k]) for k, v in enumerate((gain, bias, b_out, gain2, bias2, b_down, b_up))]
    copies = [pltpu.make_async_copy(a, b, sems.at[k]) for k, (a, b) in enumerate(pairs)]
    for copy in copies:
        copy.start()
    halves = []
    for k, (w, skip, part) in enumerate(
        (
            (w_out, 0, first_part.at[0:96, :]),
            (w_up, 0, first_part.at[96:224, :]),
            (w_up, 128, second_part.at[0:256, :]),
            (w_down, 0, second_part.at[256:640, :]),
        )
    ):
        start = pl.multiple_of(idx[3] * (w.shape[0] // 2) + skip, 32)
        source = w.at[pl.ds(start, part.shape[0]), :]
        halves.append(pltpu.make_async_copy(source, part, sems.at[13 + k]))
        halves[k].start()
    for copy in copies:
        copy.wait()
    hat, _ = norm_stats(tok_v[...].astype(f32))
    rows = [v[...].reshape(1, 768) for v in vecs]
    out[...] = (hat * rows[0] + rows[1]).astype(bf16)
    for k in range(6):
        par[k : k + 1, :] = rows[k]
    par[6:8, :] = jnp.zeros((2, 768), f32)
    block = seg_v[:, pl.ds(pl.multiple_of(idx[1] * 512, 512), 512)].astype(f32)
    segr[...] = block
    segc[...] = jnp.transpose(jnp.broadcast_to(block, (8, 512)))[:, 0:1]
    for h in range(3):
        w = feat_v[h]
        signed[64 * h : 64 * h + 64, :] = jnp.concatenate([w, -w], axis=1)
        b = bf_v[h : h + 1, :]
        flat[6 + h : 7 + h, :] = jnp.concatenate([b, -b], axis=1)
        flat[2 * h : 2 * h + 1, :] = bq_v[h : h + 1, 0:128]
        flat[2 * h + 1 : 2 * h + 2, :] = bq_v[h : h + 1, 64:192]
    for t in range(6):
        flat[9 + t : 10 + t, :] = rows[6][:, 128 * t : 128 * t + 128]
    flat[15:16, :] = jnp.zeros((1, 128), f32)
    for t in range(6):
        buf[288:320, 128 * t : 128 * t + 128] = signed[32 * t : 32 * t + 32, :]
    rest = flat[...]
    for t in range(3):
        limb = rest.astype(bf16)
        buf[320:336, 128 * t : 128 * t + 128] = limb
        rest = rest - limb.astype(f32)
    buf[320:336, 384:768] = jnp.zeros((16, 384), bf16)
    for copy in halves:
        copy.wait()


def join_halves(c, whole, mine, sibling):
    rows = mine.shape[0]
    whole[pl.ds(pl.multiple_of(c * rows, 32), rows), :] = mine[...]
    whole[pl.ds(pl.multiple_of((1 - c) * rows, 32), rows), :] = sibling[...]


def qkv_kernel(
    idx, seg, n_own, n_oth, w_own, buf, buf_sib, signed, flat, par, segc,
    ncat, u, fq, fk, va, arow, pay, pay_far, wx, wfe, bup, w_oth,
):
    x, y, c = idx[0], idx[1], idx[3]
    lane = lanes()
    low = lane < 64
    w_oth[pl.ds(pl.multiple_of(c * 288, 32), 288), :] = buf[0:288, :]
    w_oth[pl.ds(pl.multiple_of((1 - c) * 288, 32), 288), :] = buf_sib[0:288, :]
    flats = [flat[...], sum(buf[320:336, 128 * t : 128 * t + 128].astype(f32) for t in range(3))]
    biases = []
    for s, w in ((0, w_own), (1, w_oth)):
        for k in range(3):
            wx[s, 256 * k : 256 * k + 128, :] = w[192 * k : 192 * k + 128, :]
            wx[s, 256 * k + 128 : 256 * k + 256, :] = w[192 * k + 64 : 192 * k + 192, :]
        if s == 0:
            parts = [signed[64 * h : 64 * h + 64, :] for h in range(3)]
        else:
            tiles = [buf[288:320, 128 * t : 128 * t + 128] for t in range(6)]
            parts = [jnp.concatenate([tiles[2 * h], tiles[2 * h + 1]], axis=0) for h in range(3)]
        none = jnp.zeros((64, 128), bf16)
        wfe[s, 0:64, 0:128] = parts[0]
        wfe[s, 64:128, 0:128] = none
        wfe[s, 0:64, 128:256] = none
        wfe[s, 64:128, 128:256] = parts[1]
        wfe[s, 0:64, 256:384] = none
        wfe[s, 64:128, 256:384] = parts[2]
        f = flats[s]
        bup[s] = f
        biases.append(jnp.concatenate([f[t : t + 1, :] for t in range(6)], axis=1))
        centre = jnp.broadcast_to(par[1:2, :], (16, 768)).astype(bf16)
        a = nt(centre, wx[s, 512:768, :])[0:8] + biases[s][:, 512:768]
        arow[3 * s] = jnp.where(low, a[0:1, 0:128], 0.0)
        arow[3 * s + 1] = jnp.where(low, a[0:1, 128:256], 0.0)
        arow[3 * s + 2] = jnp.where(low, half_turn(a[:, 128:256])[0:1], 0.0)
    ones = jnp.where((lane == 64) | (lane == 65), 1.0, 0.0)
    for r, n_ref in ((0, n_own), (1, n_oth)):
        start = pl.multiple_of((x if r == 0 else 1 - x) * 256, 256)
        rows = pl.ds(start, 256)
        n = n_ref[...]
        ncat[rows, :] = n
        for s in range(2):
            proj = (nt(n, wx[s]) + biases[s]).astype(bf16)
            u[rows, 512 * s : 512 * s + 512] = proj[:, 0:512]
            for k, feats in ((0, fq), (1, fk)):
                both = nn(proj[:, 256 * k : 256 * k + 128], wfe[s, :, 0:256])
                third = nn(proj[:, 256 * k + 128 : 256 * k + 256], wfe[s, :, 256:384])
                for h, part in ((0, both[:, 0:128]), (1, both[:, 128:256]), (2, third)):
                    part = part + flats[s][6 + h : 7 + h, :]
                    top = jnp.max(part, axis=1, keepdims=True)
                    e = jnp.exp(part - top)
                    feats[3 * s + h, rows, :] = (e * (1.0 / jnp.sum(e, axis=1, keepdims=True))).astype(bf16)
            v01 = proj[:, 512:640].astype(f32)
            v12 = proj[:, 640:768].astype(f32)
            for h, v in ((0, v01), (1, v12), (2, half_turn(v12))):
                va[3 * s + h, rows, :] = jnp.where(low, v - arow[3 * s + h], ones).astype(bf16)
    last = seg[y * 512 + 511].astype(f32)
    keep = (segc[...] == last).astype(f32)
    tops, norms = [], []
    for g in range(6):
        st = tn(va[g], (fk[g].astype(f32) * keep).astype(bf16))
        tops.append(st[0:64])
        norms.append(st[64:65])
    encode(pay, tops, norms)
    encode(pay_far, tops, norms, far_scale(True, seg, y))


def inner_kernel(segc, segr, fq, fk, va, numden):
    for it in range(2):
        wide = 256 * (it + 1)
        i = lax.broadcasted_iota(jnp.int32, (256, wide), 0) + 256 * it
        j = lax.broadcasted_iota(jnp.int32, (256, wide), 1)
        mask = ((j <= i) & (segc[256 * it : 256 * it + 256, :] == segr[:, 0:wide])).astype(f32)

        for g in range(6):
            scores = nt(fq[g, 256 * it : 256 * it + 256, :], fk[g, 0:wide, :])
            weights = (scores * mask).astype(bf16)
            numden[g, 256 * it : 256 * it + 256, :] = nn(weights, va[g, 0:wide, :])


def flag(test):
    return jnp.where(test, 1.0, 0.0).astype(f32)


def far_scale(forward, seg, y):
    if forward:
        return jnp.where(y == 0, flag(seg[511] == seg[1023]), 1.0)
    return jnp.where(y == 0, 1.0, flag(seg[512] == seg[0]))


def send_state_kernel(forward, idx, seg, mine, theirs, one, one_theirs, out):
    y = idx[1]
    scale = far_scale(forward, seg, 1 - y)
    parts = [(1.0, decode(mine)), (scale, decode(theirs, True)), (1.0, decode(one)), (1.0, decode(one_theirs, True))]
    encode(out, *combine(parts))


def carry_state(forward, idx, seg, theirs, one, one_theirs, two):
    y, z = idx[1], idx[2]
    near = flag(seg[511] == seg[512])
    if forward:
        near = jnp.where(y == 1, near, 0.0)
        far = jnp.where(y == 1, flag(seg[0] == seg[512]), 1.0)
        within, across = flag((z & 1) == 1), flag(z >= 2)
    else:
        near = jnp.where(y == 0, near, 0.0)
        far = jnp.where(y == 0, flag(seg[511] == seg[1023]), 1.0)
        within, across = flag((z & 1) == 0), flag(z < 2)
    parts = [(near, decode(theirs, True)), (far * within, decode(one)), (far * within, decode(one_theirs, True))]
    return combine(parts + [(far * across, decode(two))])


def augmented(top, norm, third):
    row = lax.broadcasted_iota(jnp.int32, (64, 128), 0)
    high = norm.astype(bf16).astype(f32)
    rest = norm - high
    if third:
        low = jnp.where(row < 2, high, jnp.where(row == 2, rest, 0.0))
    else:
        low = jnp.where(row == 0, high, jnp.where(row == 1, rest, 0.0))
    return jnp.concatenate([top, low], axis=0).astype(bf16)


def out_kernel(
    idx, seg, theirs, one, one_theirs, two, numden, fq, arow, segc, w_own, w_mine, w_sib,
    att, mixed, paug, part_own, part_a, part_b, w_oth,
):
    x, y = idx[0], idx[1]
    for core, part in ((idx[3], w_mine), (1 - idx[3], w_sib)):
        w_oth[pl.ds(pl.multiple_of(core * 96, 32), 96), :] = part[0:96, :]
    tops, norms = carry_state(True, idx, seg, theirs, one, one_theirs, two)
    low = lanes() < 64
    first = seg[y * 512].astype(f32)
    open_rows = (segc[...] == first).astype(f32)
    for s in range(2):
        heads = []
        for h in range(3):
            g = 3 * s + h
            paug[g] = augmented(tops[g], norms[g], True)
            nd = numden[g] + open_rows * nt(fq[g], paug[g])
            inv = 1.0 / (nd[:, 64:65] + nd[:, 66:67])
            a = jnp.where(low, nd * inv, 0.0)
            att[g] = jnp.where(low, a, inv)
            heads.append(a + arow[g])
        mixed[:, 256 * s : 256 * s + 128] = (heads[0] + half_turn(heads[1])).astype(bf16)
        mixed[:, 256 * s + 128 : 256 * s + 256] = half_turn(heads[2]).astype(bf16)

    def term(start):
        rows = pl.ds(pl.multiple_of(start * 256, 256), 256)
        total = nn(mixed[rows, 0:128], w_own[0:128, :]) + nn(mixed[rows, 128:256], w_own[64:192, :])
        total += nn(mixed[rows, 256:384], w_oth[0:128, :])
        return total + nn(mixed[rows, 384:512], w_oth[64:192, :])

    oth = term(1 - x).astype(bf16)
    part_a[...] = oth[0:128]
    part_b[...] = oth[128:256]
    part_own[...] = term(x)


def ln_two_kernel(k, tok, own, recv, par, mid, normed):
    rows = slice(128 * k, 128 * k + 128)
    v = tok[rows, :].astype(f32) + (own[rows, :] + recv[...].astype(f32) + par[2:3, :])
    mid[...] = v
    hat, _ = norm_stats(v)
    normed[...] = (hat * par[3:4, :] + par[4:5, :]).astype(bf16)


def stack(*refs, cols=slice(None)):
    return jnp.concatenate([r[:, cols] for r in refs], axis=0)


def mlp_own_kernel(
    idx, n2_a, n2_b, cot, up_own, down_own, first, first_sib, second, second_sib,
    b_up, hid, gpre, gn2, up_oth, down_oth,
):
    for core, one, two in ((idx[3], first, second), (1 - idx[3], first_sib, second_sib)):
        start = core * 384
        up_oth[pl.ds(pl.multiple_of(start, 128), 128), :] = one[96:224, :]
        up_oth[pl.ds(pl.multiple_of(start + 128, 128), 256), :] = two[0:256, :]
        down_oth[pl.ds(pl.multiple_of(start, 128), 384), :] = two[256:640, :]
    mlp(stack(n2_a, n2_b), cot[...], up_own, up_oth, down_own, down_oth, b_up, hid, gpre, gn2)


def mlp_kernel(k, n2, cot, up_own, up_oth, down_own, down_oth, b_up, hid, gpre, gn2):
    mlp(n2[...], cot[128 * k : 128 * k + 128, :], up_own, up_oth, down_own, down_oth, b_up, hid, gpre, gn2)


def mlp(rows, cots, up_own, up_oth, down_own, down_oth, b_up, hid, gpre, gn2):
    total = jnp.zeros(rows.shape, f32)
    bias = [jnp.concatenate([b_up[s, 9 + t : 10 + t, :] for t in range(6)], axis=1) for s in range(2)]
    for s, up, down in ((0, up_own, down_own), (1, up_oth, down_oth)):
        for t in range(3):
            cols = slice(256 * t, 256 * t + 256)
            at = slice(768 * s + 256 * t, 768 * s + 256 * t + 256)
            pre = nn(rows, up[:, cols]) + bias[s][:, cols]
            grad = nt(cots, down[cols, :])
            square = pre * pre
            th = jnp.tanh(ROOT * (pre + 0.044715 * (square * pre)))
            half = 0.5 * (1.0 + th)
            hid[:, at] = (pre * half).astype(bf16)
            slope = half + 0.5 * pre * (1.0 - th * th) * (ROOT * (1.0 + 3 * 0.044715 * square))
            g = (grad * slope).astype(bf16)
            gpre[:, at] = g
            total += nt(g, up[:, cols])
    gn2[...] = total.astype(gn2.dtype)


def down_kernel(hid_own, hid_a, hid_b, down_own, down_oth, own, oth):
    hid = stack(hid_a, hid_b)
    oth[...] = (nn(hid[:, 0:768], down_own[...]) + nn(hid[:, 768:1536], down_oth[...])).astype(bf16)
    own[...] = nn(hid_own[:, 0:768], down_own[...]) + nn(hid_own[:, 768:1536], down_oth[...])


def final_kernel(mid_a, mid_b, own, recv, par, out):
    for k, mid in enumerate((mid_a, mid_b)):
        rows = slice(128 * k, 128 * k + 128)
        out[rows, :] = (mid[...] + (own[rows, :] + recv[rows, :].astype(f32)) + par[5:6, :]).astype(bf16)


def norm_grad(v, gain, grad):
    hat, inv = norm_stats(v)
    e = grad * gain
    back = inv * (e - jnp.mean(e, axis=-1, keepdims=True) - hat * jnp.mean(e * hat, axis=-1, keepdims=True))
    return back, jnp.sum(grad * hat, axis=0, keepdims=True), jnp.sum(grad, axis=0, keepdims=True)


def put_vector(ref, row, vec):
    for t in range(vec.shape[1] // 128):
        ref[row + t : row + t + 1, :] = vec[:, 128 * t : 128 * t + 128]


def ln_two_back_kernel(k, mid, own, recv, par, cot, *more):
    *before, gmid, branch, vecs = more
    rows = slice(128 * k, 128 * k + 128)
    cots = cot[rows, :].astype(f32)
    back, dgain, dbias = norm_grad(mid[...], par[3:4, :], own[rows, :] + recv[...].astype(f32))
    g = cots + back
    gmid[...] = g
    low = g.astype(bf16)
    branch[...] = low
    put_vector(vecs, 0, jnp.sum(low.astype(f32), axis=0, keepdims=True))
    put_vector(vecs, 6, dgain)
    put_vector(vecs, 12, dbias)
    put_vector(vecs, 18, jnp.sum(cots, axis=0, keepdims=True))
    for earlier in before:
        vecs[...] += earlier[...]


def ln_one_back_kernel(tok, own, recv, par, gmid_a, gmid_b, vecs_two, out, vecs):
    back, dgain, dbias = norm_grad(tok[...].astype(f32), par[0:1, :], own[...] + recv[...].astype(f32))
    out[...] = stack(gmid_a, gmid_b) + back
    vecs[0:24, :] = vecs_two[...]
    put_vector(vecs, 24, dgain)
    put_vector(vecs, 30, dbias)
    vecs[36:40, :] = jnp.zeros((4, 128), f32)


def down_grad(idx, half, s, hid_own, hid_a, hid_b, cot_own, cot_oth):
    at = pl.ds(pl.multiple_of(half * 384 + 768 * s, 384), 384)
    return tn(hid_own[:, at], cot_own[...]) + tn(stack(hid_a, hid_b, cols=at), cot_oth[...])


def up_grad(idx, half, s, own_a, own_b, oth_a, oth_b, gpre_own, gpre_a, gpre_b):
    at = pl.ds(pl.multiple_of(half * 384, 384), 384)
    cols = slice(768 * s, 768 * s + 768)
    total = tn(stack(own_a, own_b, cols=at), gpre_own[:, cols])
    return total + tn(stack(oth_a, oth_b, cols=at), stack(gpre_a, gpre_b, cols=cols))


def mlp_send_kernel(grad, idx, *args):
    *args, send = args
    for s in range(2):
        send[s] = grad(idx, 1 - idx[3], s, *args).astype(bf16)


def mlp_keep_kernel(grad, idx, *args):
    *args, recv, keep, send = args
    send[...] = (grad(idx, idx[3], 1, *args) + recv[1].astype(f32)).astype(bf16)
    keep[...] = grad(idx, idx[3], 0, *args) + recv[0].astype(f32)


def grad_mixed_kernel(idx, seg, own_a, own_b, oth_a, oth_b, w_own, w_oth, att, fq, segc, gbcat, gna, pay, pay_far):
    x, y = idx[0], idx[1]
    lane = lanes()
    low = lane < 64
    for start, a, b in ((x, own_a, own_b), (1 - x, oth_a, oth_b)):
        gbcat[pl.ds(pl.multiple_of(start * 256, 128), 128), :] = a[...]
        gbcat[pl.ds(pl.multiple_of(start * 256 + 128, 128), 128), :] = b[...]
    first = seg[y * 512].astype(f32)
    open_rows = (segc[...] == first).astype(f32)
    tops, norms = [], []
    for s, w in ((0, w_own), (1, w_oth)):
        g01 = nt(gbcat[...], w[0:128, :]).astype(bf16).astype(f32)
        g12 = nt(gbcat[...], w[64:192, :]).astype(bf16).astype(f32)
        for h, gm in ((0, g01), (1, g12), (2, half_turn(g12))):
            g = 3 * s + h
            a = att[g]
            gn = jnp.where(low, gm * a[:, 64:65], 0.0).astype(bf16).astype(f32)
            gd = -jnp.sum(gn * a, axis=1, keepdims=True)
            high = gd.astype(bf16).astype(f32)
            tail = jnp.where((lane == 64) | (lane == 66), high, jnp.where(lane == 65, gd - high, 0.0))
            gna[g] = jnp.where(low, gn, tail).astype(bf16)
            st = tn(gna[g], (fq[g].astype(f32) * open_rows).astype(bf16))
            tops.append(st[0:64])
            norms.append(st[64:65] + st[65:66])
    encode(pay, tops, norms)
    encode(pay_far, tops, norms, far_scale(False, seg, y))


def soft_grad(soft, grad):
    s = soft.astype(f32)
    return (s * (grad - jnp.sum(grad * s, axis=1, keepdims=True))).astype(bf16)


def query_back_kernel(idx, seg, segc, segr, fq, fk, va, gna, paug, wfe, gq, gpq):
    y = idx[1]
    first = seg[y * 512].astype(f32)
    for it in range(2):
        rows = slice(256 * it, 256 * it + 256)
        wide = 256 * (it + 1)
        i = lax.broadcasted_iota(jnp.int32, (256, wide), 0) + 256 * it
        j = lax.broadcasted_iota(jnp.int32, (256, wide), 1)
        mask = ((j <= i) & (segc[rows, :] == segr[:, 0:wide])).astype(f32)
        open_rows = (segc[rows, :] == first).astype(f32)
        for g in range(6):
            gw = (nt(gna[g, rows, :], va[g, 0:wide, :]) * mask).astype(bf16)
            grad = nn(gw, fk[g, 0:wide, :]) + open_rows * nn(gna[g, rows, :], paug[g])
            gq[g, rows, :] = soft_grad(fq[g, rows, :], grad)
        for s in range(2):
            pair = jnp.concatenate([gq[3 * s, rows, :], gq[3 * s + 1, rows, :]], axis=1)
            gpq[rows, 256 * s : 256 * s + 128] = nt(pair, wfe[s, :, 0:256]).astype(bf16)
            gpq[rows, 256 * s + 128 : 256 * s + 256] = nt(gq[3 * s + 2, rows, :], wfe[s, :, 256:384]).astype(bf16)


def key_back_kernel(segc, segr, fq, fk, va, gna, gkf, gv):
    for it in range(2):
        rows = slice(256 * it, 256 * it + 256)
        late = slice(256 * it, 512)
        tall = 512 - 256 * it
        j = lax.broadcasted_iota(jnp.int32, (256, tall), 0)
        i = lax.broadcasted_iota(jnp.int32, (256, tall), 1)
        mask = ((j <= i) & (segc[rows, :] == segr[:, 256 * it : 512])).astype(f32)
        for g in range(6):
            w = (nt(fk[g, rows, :], fq[g, late, :]) * mask).astype(bf16)
            gv[g, rows, :] = nn(w, gna[g, late, :])
            gw = (nt(va[g, rows, :], gna[g, late, :]) * mask).astype(bf16)
            gkf[g, rows, :] = nn(gw, fq[g, late, :])


def qkv_back_kernel(
    idx, seg, theirs, one, one_theirs, two, segc, fk, va, gkf, gv, gpq, wfe, wx,
    gk, gpkv, part_own, part_oth,
):
    x, y = idx[0], idx[1]
    tops, norms = carry_state(False, idx, seg, theirs, one, one_theirs, two)
    low = lanes() < 64
    last = seg[y * 512 + 511].astype(f32)
    open_rows = (segc[...] == last).astype(f32)
    for s in range(2):
        base = 512 * s
        values = []
        for h in range(3):
            g = 3 * s + h
            aug = augmented(tops[g], norms[g], False)
            gk[g] = soft_grad(fk[g], gkf[g] + open_rows * nn(va[g], aug))
            values.append(jnp.where(low, gv[g] + open_rows * nt(fk[g], aug), 0.0))
        gpkv[:, base + 256 : base + 384] = (values[0] + half_turn(values[1])).astype(bf16)
        gpkv[:, base + 384 : base + 512] = half_turn(values[2]).astype(bf16)
        pair = jnp.concatenate([gk[3 * s], gk[3 * s + 1]], axis=1)
        gpkv[:, base : base + 128] = nt(pair, wfe[s, :, 0:256]).astype(bf16)
        gpkv[:, base + 128 : base + 256] = nt(gk[3 * s + 2], wfe[s, :, 256:384]).astype(bf16)

    def term(start):
        rows = pl.ds(pl.multiple_of(start * 256, 256), 256)
        total = nn(gpq[rows, 0:256], wx[0, 0:256, :]) + nn(gpkv[rows, 0:512], wx[0, 256:768, :])
        return total + (nn(gpq[rows, 256:512], wx[1, 0:256, :]) + nn(gpkv[rows, 512:1024], wx[1, 256:768, :]))

    part_oth[...] = term(1 - x).astype(bf16)
    part_own[...] = term(x)


def split_rows(c, scr, base, rows, at, keep, send, s):
    half = rows // 2
    keep[s, at : at + half, :] = scr[pl.ds(pl.multiple_of(base + half * c, 32), half), :]
    send[s, at : at + half, :] = scr[pl.ds(pl.multiple_of(base + half * (1 - c), 32), half), :].astype(bf16)


def early_weights_kernel(idx, n, gpq, mixed, gb, keep, send, scr):
    for s in range(2):
        cols = slice(256 * s, 256 * s + 256)
        for k, (a, b) in enumerate(((gpq, n), (mixed, gb))):
            grad = tn(a[:, cols], b[...])
            scr[192 * k : 192 * k + 128, :] = grad[0:128]
            scr[192 * k + 128 : 192 * k + 192, :] = grad[192:256]
            split_rows(idx[3], scr, 192 * k, 192, 96 * k, keep, send, s)


def late_weights_kernel(idx, n, gpq, gpkv, u, gq, gk, gpre_own, gpre_a, gpre_b, keep, send, scr):
    row = lax.broadcasted_iota(jnp.int32, (16, 128), 0)
    for s in range(2):
        grad = tn(gpkv[:, 512 * s : 512 * s + 512], n[...])
        for k in range(2):
            scr[192 * k : 192 * k + 128, :] = grad[256 * k : 256 * k + 128]
            scr[192 * k + 128 : 192 * k + 192, :] = grad[256 * k + 192 : 256 * k + 256]
        first = jnp.zeros((128, 256), f32)
        third = jnp.zeros((128, 128), f32)
        sums = []
        for k, g in ((0, gq), (1, gk)):
            at = 512 * s + 256 * k
            pair = jnp.concatenate([g[3 * s], g[3 * s + 1]], axis=1)
            first += tn(u[:, at : at + 128], pair)
            third += tn(u[:, at + 128 : at + 256], g[3 * s + 2])
            sums.append([jnp.sum(g[3 * s + h].astype(f32), axis=0, keepdims=True) for h in range(3)])
        low = lanes() < 64
        block = first[0:64, 0:128]
        zero = block - half_turn(block)
        block = first[64:128, 128:256]
        one = block - half_turn(block)
        block = third[64:128]
        two = block - half_turn(block)
        scr[384:448, 0:128] = jnp.where(low, zero, half_turn(one))
        scr[384:448, 128:256] = jnp.where(low, two, 0.0)
        scr[384:448, 256:768] = jnp.zeros((64, 512), f32)
        rows = []
        for t in range(6):
            tile = gpq[:, 256 * s + 128 * t : 256 * s + 128 * t + 128] if t < 2 else (
                gpkv[:, 512 * s + 128 * t - 256 : 512 * s + 128 * t - 128])
            rows.append(jnp.sum(tile.astype(f32), axis=0, keepdims=True))
        for h in range(3):
            total = jnp.broadcast_to(sums[0][h] + sums[1][h], (8, 128))
            rows.append((total - half_turn(total))[0:1])
        block = jnp.zeros((16, 128), f32)
        for t, value in enumerate(rows):
            block = jnp.where(row == t, value, block)
        scr[384:400, 256:384] = block
        cols = slice(768 * s, 768 * s + 768)
        bias = jnp.sum(gpre_own[:, cols].astype(f32), axis=0, keepdims=True)
        for part in (gpre_a, gpre_b):
            bias += jnp.sum(part[:, cols].astype(f32), axis=0, keepdims=True)
        block = jnp.zeros((16, 128), f32)
        for t in range(6):
            block = jnp.where(row == t, bias[:, 128 * t : 128 * t + 128], block)
        scr[384:400, 384:512] = block
        split_rows(idx[3], scr, 0, 192, 0, keep, send, s)
        split_rows(idx[3], scr, 192, 192, 96, keep, send, s)
        split_rows(idx[3], scr, 384, 64, 192, keep, send, s)


def pair_kernel(keep, recv, mine, across):
    mine[...] = keep[0] + recv[0].astype(f32)
    across[...] = (keep[1] + recv[1].astype(f32)).astype(bf16)


def cp_split_kernel(idx, keep, recv, mine, sent):
    rows = mine.shape[0]
    low = pl.multiple_of((idx[2] & 1) * rows, 16)
    high = pl.multiple_of((1 - (idx[2] & 1)) * rows, 16)
    sent[...] = (keep[pl.ds(high, rows), :] + recv[pl.ds(high, rows), :].astype(f32)).astype(bf16)
    mine[...] = keep[pl.ds(low, rows), :] + recv[pl.ds(low, rows), :].astype(f32)


def add_kernel(mine, recv, out):
    out[...] = (mine[...].astype(f32) + recv[...].astype(f32)).astype(out.dtype)


def place(idx, whole, pieces):
    half, pair, sib, sib_pair = pieces
    rows = half.shape[0]
    low, c = idx[2] & 1, idx[3]
    for core, zlow, piece in ((c, low, half), (c, 1 - low, pair), (1 - c, low, sib), (1 - c, 1 - low, sib_pair)):
        whole[pl.ds(pl.multiple_of((core * 2 + zlow) * rows, 16), rows), :] = piece[...].astype(whole.dtype)


def send_out(pairs, sems):
    copies = [pltpu.make_async_copy(a, b, sems.at[k]) for k, (a, b) in enumerate(pairs)]
    for copy in copies:
        copy.start()
    for copy in copies:
        copy.wait()


def join_kernel(idx, half, pair, out):
    join_halves(idx[2] & 1, out, half, pair)


def spread_kernel(idx, mine, sibling, out, whole, sems):
    for core, rows in ((idx[3], mine), (1 - idx[3], sibling)):
        whole[pl.ds(pl.multiple_of(core * 384, 384), 384), :] = rows[...].astype(f32)
    send_out([(whole, out)], sems)


def spread_attention_kernel(idx, *refs):
    early, late = refs[0:4], refs[4:8]
    outs, (first, second, w_qkv, w_out, feat, b_qkv, b_feat, b_up, sems) = refs[8:14], refs[14:]
    place(idx, first, early)
    place(idx, second, late)
    for c in range(2):
        w_qkv[96 * c : 96 * c + 96, :] = first[192 * c : 192 * c + 96, :]
        w_out[96 * c : 96 * c + 96, :] = first[192 * c + 96 : 192 * c + 192, :]
        w_qkv[192 + 96 * c : 288 + 96 * c, :] = second[224 * c : 224 * c + 96, :]
        w_qkv[384 + 96 * c : 480 + 96 * c, :] = second[224 * c + 96 : 224 * c + 192, :]
    more = jnp.concatenate([second[192:224, :], second[416:448, :]], axis=0)
    feat[0] = more[:, 0:64]
    feat[1] = half_turn(more[:, 0:128])[:, 0:64]
    feat[2] = more[:, 128:192]
    sums = more[0:16, 256:384]
    turned = half_turn(sums)
    for k in range(3):
        b_qkv[k : k + 1, 0:128] = sums[2 * k : 2 * k + 1]
        b_qkv[k : k + 1, 128:192] = turned[2 * k + 1 : 2 * k + 2, 0:64]
    b_feat[...] = sums[6:9, 0:64]
    for t in range(6):
        b_up[128 * t : 128 * t + 128] = more[t : t + 1, 384:512].reshape(128)
    send_out(list(zip((w_qkv, w_out, feat, b_qkv, b_feat, b_up), outs)), sems)


def after(value, *deps):
    return lax.optimization_barrier((value,) + deps)[0]


def swap(value, axis, bit):
    count = lax.axis_size(axis)
    return jax.tree.map(
        lambda v: lax.ppermute(v, axis, [(i, i ^ bit) for i in range(count)]), value
    )


def diagonal(value):
    tp, cp = lax.axis_size("tp"), lax.axis_size("cp")
    pairs = [(t * cp + z, (t ^ 2) * cp + (z ^ 1)) for t in range(tp) for z in range(cp)]
    return lax.ppermute(value, ("tp", "cp"), pairs)


def rest_of_dp(value):
    bit = 2
    while bit < lax.axis_size("dp"):
        value = value + swap(value.astype(bf16), "dp", bit).astype(f32)
        bit *= 2
    return value


def shards(
    tokens, segment_ids, ln1_gain, ln1_bias, w_qkv, b_qkv, w_feat, b_feat, output_weight, b_out,
    ln2_gain, ln2_bias, w_up, b_up, w_down, b_down, cotangent,
):
    t = lax.axis_index("tp")
    z = lax.axis_index("cp")
    c = lax.axis_index("dp") & 1
    x, y = t & 1, t >> 1
    idx = jnp.stack([x, y, z, c, c, c, c, c]).astype(jnp.int32)
    tok = tokens.reshape(256, 768)
    cot_own = cotangent.reshape(256, 768)
    seg = segment_ids.reshape(1024)

    wq = jnp.transpose(w_qkv, (1, 2, 0)).reshape(576, 768)
    done, first_wait = [], []

    def run(kernel, outs, args, needs=(), **options):
        args = list(args)
        args[-1] = after(args[-1], *needs, *done, *first_wait)
        first_wait.clear()
        result = call(kernel, outs, args, **options)
        done[:] = [result[0]]
        return result

    def array(*shape, kind=bf16):
        return (shape, kind)

    rows_b, rows_f = array(256, 768), array(256, 768, kind=f32)
    part_b, part_f = array(128, 768), array(128, 768, kind=f32)
    head_rows, head_rows_f = array(6, 512, 128), array(6, 512, 128, kind=f32)

    n_own, buf, signed, flat, par, segc, segr, first_part, second_part = run(
        prep_kernel,
        [
            rows_b, array(336, 768), array(192, 128), array(16, 128, kind=f32), array(8, 768, kind=f32),
            array(512, 1, kind=f32), array(1, 512, kind=f32), array(224, 768), array(640, 768),
        ],
        [
            idx, tok, ln1_gain, ln1_bias, b_out, ln2_gain, ln2_bias, b_down, wq, w_feat, b_qkv, b_feat, b_up,
            segment_ids.reshape(1, 1024), output_weight, w_up, w_down,
        ],
        smem=1, hbm=16,
        scratch=[
            pltpu.VMEM((256, 768), bf16), [pltpu.VMEM((768,), f32)] * 7, pltpu.VMEM((3, 64, 64), bf16),
            pltpu.VMEM((3, 192), f32), pltpu.VMEM((3, 64), f32), pltpu.VMEM((1, 1024), jnp.int32),
            pltpu.SemaphoreType.DMA((17,)),
        ],
    )
    n_oth = swap(n_own, "tp", 1)
    buf_y = swap(buf, "tp", 2)
    buf_sib = swap(after(buf_y, n_oth), "dp", 1)
    first_mine = swap(after(first_part, buf_y), "tp", 2)
    ncat, u, fq, fk, va, arow, pay, pay_far, wx, wfe, bup = run(
        qkv_kernel,
        [
            array(512, 768), array(512, 1024), head_rows, head_rows, head_rows, array(6, 1, 128, kind=f32),
            PAY_OUT, PAY_OUT, array(2, 768, 768), array(2, 128, 384), array(2, 16, 128, kind=f32),
        ],
        [idx, seg, n_own, n_oth, wq, buf_y, buf_sib, signed, flat, par, segc],
        smem=2, scratch=[pltpu.VMEM((576, 768), bf16)],
    )
    around = [swap(pay, "tp", 2), swap(pay_far, "cp", 1), diagonal(pay_far)]
    first_pair = (first_mine, swap(after(first_mine, pay), "dp", 1))
    second_mine = swap(after(second_part, around[0]), "tp", 2)
    cot_oth = swap(after(cot_own, pay), "tp", 1)
    (numden,) = run(inner_kernel, [head_rows_f], [segc, segr, fq, fk, va])
    (state,) = run(
        functools.partial(send_state_kernel, True), [PAY_OUT], [idx, seg, pay_far, *around], smem=2, weight=1
    )
    carried = [*around, swap(state, "cp", 2)]
    att, mixed, paug, part_own, send_a, send_b, wo_oth = run(
        out_kernel,
        [head_rows_f, array(512, 512), array(6, 128, 128), rows_f, part_b, part_b, array(192, 768)],
        [idx, seg, *carried, numden, fq, arow, segc, output_weight, *first_pair],
        needs=(cot_oth,), smem=2, weight=0,
    )
    part_in = [swap(send_a, "tp", 1), swap(send_b, "tp", 1)]

    mid, n2_own = [None, None], [None, None]
    for k in range(2):
        mid[k], n2_own[k] = run(
            functools.partial(ln_two_kernel, k), [part_f, part_b], [tok, part_own, part_in[k], par],
            needs=(second_mine,), weight=4,
        )
    second_pair = (second_mine, swap(after(second_mine, n2_own[0]), "dp", 1))
    n2_oth = [swap(v, "tp", 1) for v in n2_own]
    units = array(128, 1536)
    v = types.SimpleNamespace(hid={}, gpre={}, gn2={}, gmid={}, vecs_two={}, gb={})
    sums = {n: types.SimpleNamespace() for n in range(4)}
    DOWN, UP, EARLY, LATE = range(4)

    def mlp_own():
        v.hid[2], v.gpre[2], v.gn2[2], v.up, v.down = run(mlp_own_kernel,
            [array(256, 1536), array(256, 1536), rows_f, array(768, 768), array(768, 768)],
            [idx, *n2_own, cot_own, w_up, w_down, *first_pair, *second_pair, bup], smem=1,
        )

    def mlp_part(k):
        v.hid[k], v.gpre[k], out = run(
            functools.partial(mlp_kernel, k), [units, units, part_b],
            [n2_oth[k], cot_oth, w_up, v.up, w_down, v.down, bup],
        )
        v.gn2[k] = swap(out, "tp", 1)


    def down_args():
        return [idx, v.hid[2], v.hid[0], v.hid[1], cot_own, cot_oth]

    def up_args():
        return [idx, *n2_own, *n2_oth, v.gpre[2], v.gpre[0], v.gpre[1]]

    def grad_send(name, grad, args):
        (send,) = run(functools.partial(mlp_send_kernel, grad), [array(2, 384, 768)], args, smem=1, weight=0)
        sums[name].dp = swap(send, "dp", 1)

    def grad_keep(name, grad, args):
        keep, across = run(functools.partial(mlp_keep_kernel, grad), [array(384, 768, kind=f32), array(384, 768)],
            args + [sums[name].dp], smem=1,
        )
        sums[name].y = keep, swap(across, "tp", 2)


    def ln_two_back(k):
        before = [v.vecs_two[0]] if k else []
        v.gmid[k], branch, v.vecs_two[k] = run(functools.partial(ln_two_back_kernel, k), [part_f, part_b, array(24, 128, kind=f32)],
            [mid[k], v.gn2[2], v.gn2[k], par, cot_own, *before], weight=4,
        )
        v.gb[k] = branch, swap(branch, "tp", 1)


    def down():
        v.down_own, part = run(down_kernel, [rows_f, rows_b], [v.hid[2], v.hid[0], v.hid[1], w_down, v.down]
        )
        v.down_in = swap(part, "tp", 1)

    def grad_mixed():
        own, oth = zip(v.gb[0], v.gb[1])
        v.gbcat, v.gna, pay_near, far = run(grad_mixed_kernel, [array(512, 768), head_rows, PAY_OUT, PAY_OUT],
            [idx, seg, *own, *oth, output_weight, wo_oth, att, fq, segc], smem=2,
        )
        v.around = [swap(pay_near, "tp", 2), swap(far, "cp", 1), diagonal(far)]
        v.far = far

    def key_back():
        v.gkf, v.gv = run(key_back_kernel, [head_rows_f, head_rows_f], [segc, segr, fq, fk, va, v.gna]
        )

    def gstate():
        (state,) = run(functools.partial(send_state_kernel, False), [PAY_OUT], [idx, seg, v.far, *v.around],
            smem=2, weight=4,
        )
        v.coming = [*v.around, swap(state, "cp", 2)]

    def query_back():
        v.gq, v.gpq = run(query_back_kernel, [head_rows, array(512, 512)],
            [idx, seg, segc, segr, fq, fk, va, v.gna, paug, wfe], smem=2,
        )

    def early_weights():
        keep, send = run(early_weights_kernel, [array(2, 192, 768, kind=f32), array(2, 192, 768)],
            [idx, ncat, v.gpq, mixed, v.gbcat], smem=1, scratch=[pltpu.VMEM((384, 768), f32)],
        )
        sums[EARLY].dp = keep, swap(send, "dp", 1)

    def qkv_back():
        v.gk, v.gpkv, v.gn1, oth = run(qkv_back_kernel, [head_rows, array(512, 1024), rows_f, rows_b],
            [idx, seg, *v.coming, segc, fk, va, v.gkf, v.gv, v.gpq, wfe, wx], smem=2,
        )
        v.gn1_in = swap(oth, "tp", 1)

    def late_weights():
        keep, send = run(late_weights_kernel, [array(2, 224, 768, kind=f32), array(2, 224, 768)],
            [idx, ncat, v.gpq, v.gpkv, u, v.gq, v.gk, v.gpre[2], v.gpre[0], v.gpre[1]],
            smem=1, scratch=[pltpu.VMEM((448, 768), f32)],
        )
        sums[LATE].dp = keep, swap(send, "dp", 1)

    def ln_one_back():
        v.d_tok, v.vecs = run(ln_one_back_kernel, [rows_f, array(40, 128, kind=f32)],
            [tok, v.gn1, v.gn1_in, par, v.gmid[0], v.gmid[1], v.vecs_two[1]],
        )

    def final():
        (v.out,) = run(final_kernel, [rows_b], [*mid, v.down_own, v.down_in, par])

    def pair(name):
        keep, recv = sums[name].dp
        rows = keep.shape[1]
        mine, across = run(pair_kernel, [array(rows, 768, kind=f32), array(rows, 768)], [keep, recv]
        )
        sums[name].y = mine, swap(across, "tp", 2)

    def split(name):
        keep, recv = sums[name].y
        rows = keep.shape[0] // 2
        if lax.axis_size("dp") > 2:
            keep, recv = rest_of_dp(keep + recv.astype(f32)), jnp.zeros_like(recv)
        mine, sent = run(cp_split_kernel, [array(rows, 768, kind=f32), array(rows, 768)], [idx, keep, recv],
            smem=1,
        )
        sums[name].z = mine, swap(sent, "cp", 1)

    def add(name):
        mine, recv = sums[name].z
        (half,) = run(add_kernel, [(mine.shape, bf16)], [mine, recv])
        sums[name].zz = half, swap(half, "cp", 2)

    def last(name):
        mine, recv = sums[name].zz
        (half,) = run(add_kernel, [(mine.shape, bf16)], [mine, recv])
        sums[name].half = half, swap(half, "cp", 1)

    def join(name):
        rows = sums[name].half[0].shape[0] * 2
        (mine,) = run(join_kernel, [array(rows, 768)], [idx, *sums[name].half], smem=1)
        sums[name].rows = mine, swap(mine, "dp", 1)

    def spread(name):
        (sums[name].sum,) = run(spread_kernel, [array(768, 768, kind=f32)], [idx, *sums[name].rows],
            smem=1, hbm_out=True, scratch=[pltpu.VMEM((768, 768), f32), pltpu.SemaphoreType.DMA((1,))],
        )

    def pieces(name):
        half, other = sums[name].half
        return half, other, swap(half, "dp", 1), swap(other, "dp", 1)

    hops = [(axis, 1 << k) for axis in ("tp", "dp", "cp") for k in range(lax.axis_size(axis).bit_length() - 1)]

    def vec():
        if hops:
            pending = swap(v.vecs, *hops.pop(0))
            (v.vecs,) = run(add_kernel, [array(40, 128, kind=f32)], [v.vecs, pending])

    given = [(576, 768), (192, 768), (3, 64, 64), (3, 192), (3, 64), (768,)]

    def attention():
        while hops:
            vec()
        v.attention = run(spread_attention_kernel, [array(*shape, kind=f32) for shape in given],
            [idx, *pieces(EARLY), *pieces(LATE)], smem=1, hbm_out=True,
            scratch=[pltpu.VMEM((384, 768), f32), pltpu.VMEM((448, 768), f32)]
            + [pltpu.VMEM(shape, f32) for shape in given] + [pltpu.SemaphoreType.DMA((6,))],
        )

    mlp_own()
    mlp_part(0)
    mlp_part(1)
    grad_send(DOWN, down_grad, down_args())
    ln_two_back(0)
    grad_keep(DOWN, down_grad, down_args())
    grad_send(UP, up_grad, up_args())
    ln_two_back(1)
    grad_keep(UP, up_grad, up_args())
    grad_mixed()
    split(DOWN)
    key_back()
    gstate()
    query_back()
    add(DOWN)
    split(UP)
    qkv_back()
    early_weights()
    late_weights()
    pair(EARLY)
    pair(LATE)
    last(DOWN)
    add(UP)
    ln_one_back()
    split(EARLY)
    split(LATE)
    down()
    vec()
    join(DOWN)
    vec()
    add(EARLY)
    add(LATE)
    vec()
    last(UP)
    spread(DOWN)
    vec()
    last(EARLY)
    final()
    join(UP)
    last(LATE)
    spread(UP)
    attention()

    d_wq, d_w_out, d_feat, d_b_qkv, d_b_feat, d_b_up = v.attention
    vec_rows = v.vecs[:36].reshape(6, 768)
    return (
        v.out.reshape(tokens.shape),
        v.d_tok.reshape(tokens.shape),
        vec_rows[4],
        vec_rows[5],
        jnp.transpose(d_wq.reshape(3, 192, 768), (2, 0, 1)),
        d_b_qkv,
        d_feat,
        d_b_feat,
        d_w_out,
        vec_rows[0],
        vec_rows[1],
        vec_rows[2],
        sums[UP].sum,
        d_b_up,
        sums[DOWN].sum,
        vec_rows[3],
    )


def solution(mesh):
    rows = P(("cp", "tp"), "dp", None)
    placed = (
        rows, P("cp", "dp"), P(), P(), P(None, None, "tp"), P(None, "tp"), P("tp", None, None),
        P("tp", None), P("tp", None), P(), P(), P(), P(None, "tp"), P("tp"), P("tp", None), P(), rows,
    )
    given = (
        rows, rows, P(), P(), P(None, None, "tp"), P(None, "tp"), P("tp", None, None), P("tp", None),
        P("tp", None), P(), P(), P(), P(None, "tp"), P("tp"), P("tp", None), P(),
    )
    return jax.shard_map(shards, mesh=mesh, in_specs=placed, out_specs=given, check_vma=False)
```

```python
import functools
import math
import types

import jax
import jax.numpy as jnp
from jax import lax
from jax.experimental import pallas as pl
from jax.experimental.pallas import tpu as pltpu
from jax.sharding import PartitionSpec as P

f32 = jnp.float32
bf16 = jnp.bfloat16
EPS = 1e-05
ROOT = math.sqrt(2.0 / math.pi)
VMEM_LIMIT = 12 * 1024 * 1024


def nn(a, b):
    return jnp.dot(a, b, preferred_element_type=f32)


def nt(a, b):
    return lax.dot_general(a, b, (((1,), (1,)), ((), ())), preferred_element_type=f32)


def tn(a, b):
    return lax.dot_general(a, b, (((0,), (0,)), ((), ())), preferred_element_type=f32)


def call(kernel, outs, args, smem=0, hbm=0, hbm_out=False, scratch=(), weight=1):
    args = [
        pltpu.with_memory_space_constraint(a, pltpu.HBM) if smem <= k < smem + hbm else a for k, a in enumerate(args)
    ]
    specs = [pl.BlockSpec(memory_space=pltpu.SMEM)] * smem
    specs += [pl.BlockSpec(memory_space=pltpu.HBM)] * hbm
    specs += [pl.BlockSpec(memory_space=pltpu.VMEM)] * (len(args) - smem - hbm)
    out_shape = [jax.ShapeDtypeStruct(shape, kind) for shape, kind in outs]
    return pl.pallas_call(
        kernel,
        out_shape=out_shape,
        in_specs=specs,
        out_specs=[pl.BlockSpec(memory_space=pltpu.HBM if hbm_out else pltpu.VMEM)] * len(outs),
        scratch_shapes=list(scratch),
        compiler_params=pltpu.CompilerParams(vmem_limit_bytes=VMEM_LIMIT),
        cost_estimate=pl.CostEstimate(flops=max(1, weight * 10**10), bytes_accessed=10**8, transcendentals=0),
    )(*args)


def lanes():
    return lax.broadcasted_iota(jnp.int32, (1, 128), 1)


def half_turn(v):
    return pltpu.roll(v, 64, 1)


def norm_stats(v):
    centred = v - jnp.mean(v, axis=-1, keepdims=True)
    inv = lax.rsqrt(jnp.mean(centred * centred, axis=-1, keepdims=True) + EPS)
    return centred * inv, inv


def encode(pay, tops, norms, scale=None):
    if scale is not None:
        tops, norms = [scale * t for t in tops], [scale * n for n in norms]
    for g in range(6):
        pay[g * 64 : g * 64 + 64, :] = tops[g].astype(bf16)
    row = lax.broadcasted_iota(jnp.int32, (16, 128), 0)
    for s in range(2):
        block = jnp.zeros((16, 128), f32)
        for h in range(3):
            n = norms[3 * s + h]
            high = n.astype(bf16).astype(f32)
            block = jnp.where(row == h, high, block)
            block = jnp.where(row == 3 + h, n - high, block)
        pay[384 + 16 * s : 400 + 16 * s, :] = block.astype(bf16)


def decode(pay, swap=False):
    tops, norms = [], []
    blocks = [pay[384 + 16 * s : 400 + 16 * s, :].astype(f32) for s in range(2)]
    for s in range(2):
        t = 1 - s if swap else s
        for h in range(3):
            g = 3 * t + h
            tops.append(pay[g * 64 : g * 64 + 64, :].astype(f32))
            norms.append(blocks[t][h : h + 1, :] + blocks[t][3 + h : 4 + h, :])
    return tops, norms


PAY = (416, 128)
PAY_OUT = (PAY, bf16)


def combine(parts):
    tops = [sum(f * p[0][g] for f, p in parts) for g in range(6)]
    norms = [sum(f * p[1][g] for f, p in parts) for g in range(6)]
    return tops, norms


def prep_kernel(
    idx, tok, gain, bias, b_out, gain2, bias2, b_down, w_qkv, w_feat, b_qkv, b_feat, b_up, seg, w_out, w_up, w_down,
    out, buf, signed, flat, par, segc, segr, first_part, second_part,
    tok_v, vecs, feat_v, bq_v, bf_v, seg_v, sems,
):
    half = w_qkv.at[pl.ds(pl.multiple_of(idx[3] * 288, 32), 288), :]
    pairs = [(tok, tok_v), (w_feat, feat_v), (b_qkv, bq_v), (b_feat, bf_v), (seg, seg_v), (half, buf.at[0:288, :])]
    pairs += [(v, vecs[k]) for k, v in enumerate((gain, bias, b_out, gain2, bias2, b_down, b_up))]
    copies = [pltpu.make_async_copy(a, b, sems.at[k]) for k, (a, b) in enumerate(pairs)]
    for copy in copies:
        copy.start()
    halves = []
    for k, (w, skip, part) in enumerate(
        (
            (w_out, 0, first_part.at[0:96, :]),
            (w_up, 0, first_part.at[96:224, :]),
            (w_up, 128, second_part.at[0:256, :]),
            (w_down, 0, second_part.at[256:640, :]),
        )
    ):
        start = pl.multiple_of(idx[3] * (w.shape[0] // 2) + skip, 32)
        source = w.at[pl.ds(start, part.shape[0]), :]
        halves.append(pltpu.make_async_copy(source, part, sems.at[13 + k]))
        halves[k].start()
    for copy in copies:
        copy.wait()
    hat, _ = norm_stats(tok_v[...].astype(f32))
    rows = [v[...].reshape(1, 768) for v in vecs]
    out[...] = (hat * rows[0] + rows[1]).astype(bf16)
    for k in range(6):
        par[k : k + 1, :] = rows[k]
    par[6:8, :] = jnp.zeros((2, 768), f32)
    block = seg_v[:, pl.ds(pl.multiple_of(idx[1] * 512, 512), 512)].astype(f32)
    segr[...] = block
    segc[...] = jnp.transpose(jnp.broadcast_to(block, (8, 512)))[:, 0:1]
    for h in range(3):
        w = feat_v[h]
        signed[64 * h : 64 * h + 64, :] = jnp.concatenate([w, -w], axis=1)
        b = bf_v[h : h + 1, :]
        flat[6 + h : 7 + h, :] = jnp.concatenate([b, -b], axis=1)
        flat[2 * h : 2 * h + 1, :] = bq_v[h : h + 1, 0:128]
        flat[2 * h + 1 : 2 * h + 2, :] = bq_v[h : h + 1, 64:192]
    for t in range(6):
        flat[9 + t : 10 + t, :] = rows[6][:, 128 * t : 128 * t + 128]
    flat[15:16, :] = jnp.zeros((1, 128), f32)
    for t in range(6):
        buf[288:320, 128 * t : 128 * t + 128] = signed[32 * t : 32 * t + 32, :]
    rest = flat[...]
    for t in range(3):
        limb = rest.astype(bf16)
        buf[320:336, 128 * t : 128 * t + 128] = limb
        rest = rest - limb.astype(f32)
    buf[320:336, 384:768] = jnp.zeros((16, 384), bf16)
    for copy in halves:
        copy.wait()


def join_halves(c, whole, mine, sibling):
    rows = mine.shape[0]
    whole[pl.ds(pl.multiple_of(c * rows, 32), rows), :] = mine[...]
    whole[pl.ds(pl.multiple_of((1 - c) * rows, 32), rows), :] = sibling[...]


def qkv_kernel(
    idx, seg, n_own, n_oth, w_own, buf, buf_sib, signed, flat, par, segc,
    ncat, u, fq, fk, va, arow, pay, pay_far, wx, wfe, bup, w_oth,
):
    x, y, c = idx[0], idx[1], idx[3]
    lane = lanes()
    low = lane < 64
    w_oth[pl.ds(pl.multiple_of(c * 288, 32), 288), :] = buf[0:288, :]
    w_oth[pl.ds(pl.multiple_of((1 - c) * 288, 32), 288), :] = buf_sib[0:288, :]
    flats = [flat[...], sum(buf[320:336, 128 * t : 128 * t + 128].astype(f32) for t in range(3))]
    biases = []
    for s, w in ((0, w_own), (1, w_oth)):
        for k in range(3):
            wx[s, 256 * k : 256 * k + 128, :] = w[192 * k : 192 * k + 128, :]
            wx[s, 256 * k + 128 : 256 * k + 256, :] = w[192 * k + 64 : 192 * k + 192, :]
        if s == 0:
            parts = [signed[64 * h : 64 * h + 64, :] for h in range(3)]
        else:
            tiles = [buf[288:320, 128 * t : 128 * t + 128] for t in range(6)]
            parts = [jnp.concatenate([tiles[2 * h], tiles[2 * h + 1]], axis=0) for h in range(3)]
        none = jnp.zeros((64, 128), bf16)
        wfe[s, 0:64, 0:128] = parts[0]
        wfe[s, 64:128, 0:128] = none
        wfe[s, 0:64, 128:256] = none
        wfe[s, 64:128, 128:256] = parts[1]
        wfe[s, 0:64, 256:384] = none
        wfe[s, 64:128, 256:384] = parts[2]
        f = flats[s]
        bup[s] = f
        biases.append(jnp.concatenate([f[t : t + 1, :] for t in range(6)], axis=1))
        centre = jnp.broadcast_to(par[1:2, :], (16, 768)).astype(bf16)
        a = nt(centre, wx[s, 512:768, :])[0:8] + biases[s][:, 512:768]
        arow[3 * s] = jnp.where(low, a[0:1, 0:128], 0.0)
        arow[3 * s + 1] = jnp.where(low, a[0:1, 128:256], 0.0)
        arow[3 * s + 2] = jnp.where(low, half_turn(a[:, 128:256])[0:1], 0.0)
    ones = jnp.where((lane == 64) | (lane == 65), 1.0, 0.0)
    for r, n_ref in ((0, n_own), (1, n_oth)):
        start = pl.multiple_of((x if r == 0 else 1 - x) * 256, 256)
        rows = pl.ds(start, 256)
        n = n_ref[...]
        ncat[rows, :] = n
        for s in range(2):
            proj = (nt(n, wx[s]) + biases[s]).astype(bf16)
            u[rows, 512 * s : 512 * s + 512] = proj[:, 0:512]
            for k, feats in ((0, fq), (1, fk)):
                both = nn(proj[:, 256 * k : 256 * k + 128], wfe[s, :, 0:256])
                third = nn(proj[:, 256 * k + 128 : 256 * k + 256], wfe[s, :, 256:384])
                for h, part in ((0, both[:, 0:128]), (1, both[:, 128:256]), (2, third)):
                    part = part + flats[s][6 + h : 7 + h, :]
                    top = jnp.max(part, axis=1, keepdims=True)
                    e = jnp.exp(part - top)
                    feats[3 * s + h, rows, :] = (e * (1.0 / jnp.sum(e, axis=1, keepdims=True))).astype(bf16)
            v01 = proj[:, 512:640].astype(f32)
            v12 = proj[:, 640:768].astype(f32)
            for h, v in ((0, v01), (1, v12), (2, half_turn(v12))):
                va[3 * s + h, rows, :] = jnp.where(low, v - arow[3 * s + h], ones).astype(bf16)
    last = seg[y * 512 + 511].astype(f32)
    keep = (segc[...] == last).astype(f32)
    tops, norms = [], []
    for g in range(6):
        st = tn(va[g], (fk[g].astype(f32) * keep).astype(bf16))
        tops.append(st[0:64])
        norms.append(st[64:65])
    encode(pay, tops, norms)
    encode(pay_far, tops, norms, far_scale(True, seg, y))


def inner_kernel(segc, segr, fq, fk, va, numden):
    for it in range(2):
        wide = 256 * (it + 1)
        i = lax.broadcasted_iota(jnp.int32, (256, wide), 0) + 256 * it
        j = lax.broadcasted_iota(jnp.int32, (256, wide), 1)
        mask = ((j <= i) & (segc[256 * it : 256 * it + 256, :] == segr[:, 0:wide])).astype(f32)

        for g in range(6):
            scores = nt(fq[g, 256 * it : 256 * it + 256, :], fk[g, 0:wide, :])
            weights = (scores * mask).astype(bf16)
            numden[g, 256 * it : 256 * it + 256, :] = nn(weights, va[g, 0:wide, :])


def flag(test):
    return jnp.where(test, 1.0, 0.0).astype(f32)


def far_scale(forward, seg, y):
    if forward:
        return jnp.where(y == 0, flag(seg[511] == seg[1023]), 1.0)
    return jnp.where(y == 0, 1.0, flag(seg[512] == seg[0]))


def send_state_kernel(forward, idx, seg, mine, theirs, one, one_theirs, out):
    y = idx[1]
    scale = far_scale(forward, seg, 1 - y)
    parts = [(1.0, decode(mine)), (scale, decode(theirs, True)), (1.0, decode(one)), (1.0, decode(one_theirs, True))]
    encode(out, *combine(parts))


def carry_state(forward, idx, seg, theirs, one, one_theirs, two):
    y, z = idx[1], idx[2]
    near = flag(seg[511] == seg[512])
    if forward:
        near = jnp.where(y == 1, near, 0.0)
        far = jnp.where(y == 1, flag(seg[0] == seg[512]), 1.0)
        within, across = flag((z & 1) == 1), flag(z >= 2)
    else:
        near = jnp.where(y == 0, near, 0.0)
        far = jnp.where(y == 0, flag(seg[511] == seg[1023]), 1.0)
        within, across = flag((z & 1) == 0), flag(z < 2)
    parts = [(near, decode(theirs, True)), (far * within, decode(one)), (far * within, decode(one_theirs, True))]
    return combine(parts + [(far * across, decode(two))])


def augmented(top, norm, third):
    row = lax.broadcasted_iota(jnp.int32, (64, 128), 0)
    high = norm.astype(bf16).astype(f32)
    rest = norm - high
    if third:
        low = jnp.where(row < 2, high, jnp.where(row == 2, rest, 0.0))
    else:
        low = jnp.where(row == 0, high, jnp.where(row == 1, rest, 0.0))
    return jnp.concatenate([top, low], axis=0).astype(bf16)


def out_kernel(
    idx, seg, theirs, one, one_theirs, two, numden, fq, arow, segc, w_own, w_mine, w_sib,
    att, mixed, paug, part_own, part_a, part_b, w_oth,
):
    x, y = idx[0], idx[1]
    for core, part in ((idx[3], w_mine), (1 - idx[3], w_sib)):
        w_oth[pl.ds(pl.multiple_of(core * 96, 32), 96), :] = part[0:96, :]
    tops, norms = carry_state(True, idx, seg, theirs, one, one_theirs, two)
    low = lanes() < 64
    first = seg[y * 512].astype(f32)
    open_rows = (segc[...] == first).astype(f32)
    for s in range(2):
        heads = []
        for h in range(3):
            g = 3 * s + h
            paug[g] = augmented(tops[g], norms[g], True)
            nd = numden[g] + open_rows * nt(fq[g], paug[g])
            inv = 1.0 / (nd[:, 64:65] + nd[:, 66:67])
            a = jnp.where(low, nd * inv, 0.0)
            att[g] = jnp.where(low, a, inv)
            heads.append(a + arow[g])
        mixed[:, 256 * s : 256 * s + 128] = (heads[0] + half_turn(heads[1])).astype(bf16)
        mixed[:, 256 * s + 128 : 256 * s + 256] = half_turn(heads[2]).astype(bf16)

    def term(start):
        rows = pl.ds(pl.multiple_of(start * 256, 256), 256)
        total = nn(mixed[rows, 0:128], w_own[0:128, :]) + nn(mixed[rows, 128:256], w_own[64:192, :])
        total += nn(mixed[rows, 256:384], w_oth[0:128, :])
        return total + nn(mixed[rows, 384:512], w_oth[64:192, :])

    oth = term(1 - x).astype(bf16)
    part_a[...] = oth[0:128]
    part_b[...] = oth[128:256]
    part_own[...] = term(x)


def ln_two_kernel(k, tok, own, recv, par, mid, normed):
    rows = slice(128 * k, 128 * k + 128)
    v = tok[rows, :].astype(f32) + (own[rows, :] + recv[...].astype(f32) + par[2:3, :])
    mid[...] = v
    hat, _ = norm_stats(v)
    normed[...] = (hat * par[3:4, :] + par[4:5, :]).astype(bf16)


def stack(*refs, cols=slice(None)):
    return jnp.concatenate([r[:, cols] for r in refs], axis=0)


def mlp_own_kernel(
    idx, n2_a, n2_b, cot, up_own, down_own, first, first_sib, second, second_sib,
    b_up, hid, gpre, gn2, up_oth, down_oth,
):
    for core, one, two in ((idx[3], first, second), (1 - idx[3], first_sib, second_sib)):
        start = core * 384
        up_oth[pl.ds(pl.multiple_of(start, 128), 128), :] = one[96:224, :]
        up_oth[pl.ds(pl.multiple_of(start + 128, 128), 256), :] = two[0:256, :]
        down_oth[pl.ds(pl.multiple_of(start, 128), 384), :] = two[256:640, :]
    mlp(stack(n2_a, n2_b), cot[...], up_own, up_oth, down_own, down_oth, b_up, hid, gpre, gn2)


def mlp_kernel(k, n2, cot, up_own, up_oth, down_own, down_oth, b_up, hid, gpre, gn2):
    mlp(n2[...], cot[128 * k : 128 * k + 128, :], up_own, up_oth, down_own, down_oth, b_up, hid, gpre, gn2)


def mlp(rows, cots, up_own, up_oth, down_own, down_oth, b_up, hid, gpre, gn2):
    total = jnp.zeros(rows.shape, f32)
    bias = [jnp.concatenate([b_up[s, 9 + t : 10 + t, :] for t in range(6)], axis=1) for s in range(2)]
    for s, up, down in ((0, up_own, down_own), (1, up_oth, down_oth)):
        for t in range(3):
            cols = slice(256 * t, 256 * t + 256)
            at = slice(768 * s + 256 * t, 768 * s + 256 * t + 256)
            pre = nn(rows, up[:, cols]) + bias[s][:, cols]
            grad = nt(cots, down[cols, :])
            square = pre * pre
            th = jnp.tanh(ROOT * (pre + 0.044715 * (square * pre)))
            half = 0.5 * (1.0 + th)
            hid[:, at] = (pre * half).astype(bf16)
            slope = half + 0.5 * pre * (1.0 - th * th) * (ROOT * (1.0 + 3 * 0.044715 * square))
            g = (grad * slope).astype(bf16)
            gpre[:, at] = g
            total += nt(g, up[:, cols])
    gn2[...] = total.astype(gn2.dtype)


def down_kernel(hid_own, hid_a, hid_b, down_own, down_oth, own, oth):
    hid = stack(hid_a, hid_b)
    oth[...] = (nn(hid[:, 0:768], down_own[...]) + nn(hid[:, 768:1536], down_oth[...])).astype(bf16)
    own[...] = nn(hid_own[:, 0:768], down_own[...]) + nn(hid_own[:, 768:1536], down_oth[...])


def final_kernel(mid_a, mid_b, own, recv, par, out):
    for k, mid in enumerate((mid_a, mid_b)):
        rows = slice(128 * k, 128 * k + 128)
        out[rows, :] = (mid[...] + (own[rows, :] + recv[rows, :].astype(f32)) + par[5:6, :]).astype(bf16)


def norm_grad(v, gain, grad):
    hat, inv = norm_stats(v)
    e = grad * gain
    back = inv * (e - jnp.mean(e, axis=-1, keepdims=True) - hat * jnp.mean(e * hat, axis=-1, keepdims=True))
    return back, jnp.sum(grad * hat, axis=0, keepdims=True), jnp.sum(grad, axis=0, keepdims=True)


def put_vector(ref, row, vec):
    for t in range(vec.shape[1] // 128):
        ref[row + t : row + t + 1, :] = vec[:, 128 * t : 128 * t + 128]


def ln_two_back_kernel(k, mid, own, recv, par, cot, *more):
    *before, gmid, branch, vecs = more
    rows = slice(128 * k, 128 * k + 128)
    cots = cot[rows, :].astype(f32)
    back, dgain, dbias = norm_grad(mid[...], par[3:4, :], own[rows, :] + recv[...].astype(f32))
    g = cots + back
    gmid[...] = g
    low = g.astype(bf16)
    branch[...] = low
    put_vector(vecs, 0, jnp.sum(low.astype(f32), axis=0, keepdims=True))
    put_vector(vecs, 6, dgain)
    put_vector(vecs, 12, dbias)
    put_vector(vecs, 18, jnp.sum(cots, axis=0, keepdims=True))
    for earlier in before:
        vecs[...] += earlier[...]


def ln_one_back_kernel(tok, own, recv, par, gmid_a, gmid_b, vecs_two, out, vecs):
    back, dgain, dbias = norm_grad(tok[...].astype(f32), par[0:1, :], own[...] + recv[...].astype(f32))
    out[...] = stack(gmid_a, gmid_b) + back
    vecs[0:24, :] = vecs_two[...]
    put_vector(vecs, 24, dgain)
    put_vector(vecs, 30, dbias)
    vecs[36:40, :] = jnp.zeros((4, 128), f32)


def down_grad(idx, half, s, hid_own, hid_a, hid_b, cot_own, cot_oth):
    at = pl.ds(pl.multiple_of(half * 384 + 768 * s, 384), 384)
    return tn(hid_own[:, at], cot_own[...]) + tn(stack(hid_a, hid_b, cols=at), cot_oth[...])


def up_grad(idx, half, s, own_a, own_b, oth_a, oth_b, gpre_own, gpre_a, gpre_b):
    at = pl.ds(pl.multiple_of(half * 384, 384), 384)
    cols = slice(768 * s, 768 * s + 768)
    total = tn(stack(own_a, own_b, cols=at), gpre_own[:, cols])
    return total + tn(stack(oth_a, oth_b, cols=at), stack(gpre_a, gpre_b, cols=cols))


def mlp_send_kernel(grad, idx, *args):
    *args, send = args
    for s in range(2):
        send[s] = grad(idx, 1 - idx[3], s, *args).astype(bf16)


def mlp_keep_kernel(grad, idx, *args):
    *args, recv, keep, send = args
    send[...] = (grad(idx, idx[3], 1, *args) + recv[1].astype(f32)).astype(bf16)
    keep[...] = grad(idx, idx[3], 0, *args) + recv[0].astype(f32)


def grad_mixed_kernel(idx, seg, own_a, own_b, oth_a, oth_b, w_own, w_oth, att, fq, segc, gbcat, gna, pay, pay_far):
    x, y = idx[0], idx[1]
    lane = lanes()
    low = lane < 64
    for start, a, b in ((x, own_a, own_b), (1 - x, oth_a, oth_b)):
        gbcat[pl.ds(pl.multiple_of(start * 256, 128), 128), :] = a[...]
        gbcat[pl.ds(pl.multiple_of(start * 256 + 128, 128), 128), :] = b[...]
    first = seg[y * 512].astype(f32)
    open_rows = (segc[...] == first).astype(f32)
    tops, norms = [], []
    for s, w in ((0, w_own), (1, w_oth)):
        g01 = nt(gbcat[...], w[0:128, :]).astype(bf16).astype(f32)
        g12 = nt(gbcat[...], w[64:192, :]).astype(bf16).astype(f32)
        for h, gm in ((0, g01), (1, g12), (2, half_turn(g12))):
            g = 3 * s + h
            a = att[g]
            gn = jnp.where(low, gm * a[:, 64:65], 0.0).astype(bf16).astype(f32)
            gd = -jnp.sum(gn * a, axis=1, keepdims=True)
            high = gd.astype(bf16).astype(f32)
            tail = jnp.where((lane == 64) | (lane == 66), high, jnp.where(lane == 65, gd - high, 0.0))
            gna[g] = jnp.where(low, gn, tail).astype(bf16)
            st = tn(gna[g], (fq[g].astype(f32) * open_rows).astype(bf16))
            tops.append(st[0:64])
            norms.append(st[64:65] + st[65:66])
    encode(pay, tops, norms)
    encode(pay_far, tops, norms, far_scale(False, seg, y))


def soft_grad(soft, grad):
    s = soft.astype(f32)
    return (s * (grad - jnp.sum(grad * s, axis=1, keepdims=True))).astype(bf16)


def query_back_kernel(idx, seg, segc, segr, fq, fk, va, gna, paug, wfe, gq, gpq):
    y = idx[1]
    first = seg[y * 512].astype(f32)
    for it in range(2):
        rows = slice(256 * it, 256 * it + 256)
        wide = 256 * (it + 1)
        i = lax.broadcasted_iota(jnp.int32, (256, wide), 0) + 256 * it
        j = lax.broadcasted_iota(jnp.int32, (256, wide), 1)
        mask = ((j <= i) & (segc[rows, :] == segr[:, 0:wide])).astype(f32)
        open_rows = (segc[rows, :] == first).astype(f32)
        for g in range(6):
            gw = (nt(gna[g, rows, :], va[g, 0:wide, :]) * mask).astype(bf16)
            grad = nn(gw, fk[g, 0:wide, :]) + open_rows * nn(gna[g, rows, :], paug[g])
            gq[g, rows, :] = soft_grad(fq[g, rows, :], grad)
        for s in range(2):
            pair = jnp.concatenate([gq[3 * s, rows, :], gq[3 * s + 1, rows, :]], axis=1)
            gpq[rows, 256 * s : 256 * s + 128] = nt(pair, wfe[s, :, 0:256]).astype(bf16)
            gpq[rows, 256 * s + 128 : 256 * s + 256] = nt(gq[3 * s + 2, rows, :], wfe[s, :, 256:384]).astype(bf16)


def key_back_kernel(segc, segr, fq, fk, va, gna, gkf, gv):
    for it in range(2):
        rows = slice(256 * it, 256 * it + 256)
        late = slice(256 * it, 512)
        tall = 512 - 256 * it
        j = lax.broadcasted_iota(jnp.int32, (256, tall), 0)
        i = lax.broadcasted_iota(jnp.int32, (256, tall), 1)
        mask = ((j <= i) & (segc[rows, :] == segr[:, 256 * it : 512])).astype(f32)
        for g in range(6):
            w = (nt(fk[g, rows, :], fq[g, late, :]) * mask).astype(bf16)
            gv[g, rows, :] = nn(w, gna[g, late, :])
            gw = (nt(va[g, rows, :], gna[g, late, :]) * mask).astype(bf16)
            gkf[g, rows, :] = nn(gw, fq[g, late, :])


def qkv_back_kernel(
    idx, seg, theirs, one, one_theirs, two, segc, fk, va, gkf, gv, gpq, wfe, wx,
    gk, gpkv, part_own, part_oth,
):
    x, y = idx[0], idx[1]
    tops, norms = carry_state(False, idx, seg, theirs, one, one_theirs, two)
    low = lanes() < 64
    last = seg[y * 512 + 511].astype(f32)
    open_rows = (segc[...] == last).astype(f32)
    for s in range(2):
        base = 512 * s
        values = []
        for h in range(3):
            g = 3 * s + h
            aug = augmented(tops[g], norms[g], False)
            gk[g] = soft_grad(fk[g], gkf[g] + open_rows * nn(va[g], aug))
            values.append(jnp.where(low, gv[g] + open_rows * nt(fk[g], aug), 0.0))
        gpkv[:, base + 256 : base + 384] = (values[0] + half_turn(values[1])).astype(bf16)
        gpkv[:, base + 384 : base + 512] = half_turn(values[2]).astype(bf16)
        pair = jnp.concatenate([gk[3 * s], gk[3 * s + 1]], axis=1)
        gpkv[:, base : base + 128] = nt(pair, wfe[s, :, 0:256]).astype(bf16)
        gpkv[:, base + 128 : base + 256] = nt(gk[3 * s + 2], wfe[s, :, 256:384]).astype(bf16)

    def term(start):
        rows = pl.ds(pl.multiple_of(start * 256, 256), 256)
        total = nn(gpq[rows, 0:256], wx[0, 0:256, :]) + nn(gpkv[rows, 0:512], wx[0, 256:768, :])
        return total + (nn(gpq[rows, 256:512], wx[1, 0:256, :]) + nn(gpkv[rows, 512:1024], wx[1, 256:768, :]))

    part_oth[...] = term(1 - x).astype(bf16)
    part_own[...] = term(x)


def split_rows(c, scr, base, rows, at, keep, send, s):
    half = rows // 2
    keep[s, at : at + half, :] = scr[pl.ds(pl.multiple_of(base + half * c, 32), half), :]
    send[s, at : at + half, :] = scr[pl.ds(pl.multiple_of(base + half * (1 - c), 32), half), :].astype(bf16)


def early_weights_kernel(idx, n, gpq, mixed, gb, keep, send, scr):
    for s in range(2):
        cols = slice(256 * s, 256 * s + 256)
        for k, (a, b) in enumerate(((gpq, n), (mixed, gb))):
            grad = tn(a[:, cols], b[...])
            scr[192 * k : 192 * k + 128, :] = grad[0:128]
            scr[192 * k + 128 : 192 * k + 192, :] = grad[192:256]
            split_rows(idx[3], scr, 192 * k, 192, 96 * k, keep, send, s)


def late_weights_kernel(idx, n, gpq, gpkv, u, gq, gk, gpre_own, gpre_a, gpre_b, keep, send, scr):
    row = lax.broadcasted_iota(jnp.int32, (16, 128), 0)
    for s in range(2):
        grad = tn(gpkv[:, 512 * s : 512 * s + 512], n[...])
        for k in range(2):
            scr[192 * k : 192 * k + 128, :] = grad[256 * k : 256 * k + 128]
            scr[192 * k + 128 : 192 * k + 192, :] = grad[256 * k + 192 : 256 * k + 256]
        first = jnp.zeros((128, 256), f32)
        third = jnp.zeros((128, 128), f32)
        sums = []
        for k, g in ((0, gq), (1, gk)):
            at = 512 * s + 256 * k
            pair = jnp.concatenate([g[3 * s], g[3 * s + 1]], axis=1)
            first += tn(u[:, at : at + 128], pair)
            third += tn(u[:, at + 128 : at + 256], g[3 * s + 2])
            sums.append([jnp.sum(g[3 * s + h].astype(f32), axis=0, keepdims=True) for h in range(3)])
        low = lanes() < 64
        block = first[0:64, 0:128]
        zero = block - half_turn(block)
        block = first[64:128, 128:256]
        one = block - half_turn(block)
        block = third[64:128]
        two = block - half_turn(block)
        scr[384:448, 0:128] = jnp.where(low, zero, half_turn(one))
        scr[384:448, 128:256] = jnp.where(low, two, 0.0)
        scr[384:448, 256:768] = jnp.zeros((64, 512), f32)
        rows = []
        for t in range(6):
            tile = gpq[:, 256 * s + 128 * t : 256 * s + 128 * t + 128] if t < 2 else (
                gpkv[:, 512 * s + 128 * t - 256 : 512 * s + 128 * t - 128])
            rows.append(jnp.sum(tile.astype(f32), axis=0, keepdims=True))
        for h in range(3):
            total = jnp.broadcast_to(sums[0][h] + sums[1][h], (8, 128))
            rows.append((total - half_turn(total))[0:1])
        block = jnp.zeros((16, 128), f32)
        for t, value in enumerate(rows):
            block = jnp.where(row == t, value, block)
        scr[384:400, 256:384] = block
        cols = slice(768 * s, 768 * s + 768)
        bias = jnp.sum(gpre_own[:, cols].astype(f32), axis=0, keepdims=True)
        for part in (gpre_a, gpre_b):
            bias += jnp.sum(part[:, cols].astype(f32), axis=0, keepdims=True)
        block = jnp.zeros((16, 128), f32)
        for t in range(6):
            block = jnp.where(row == t, bias[:, 128 * t : 128 * t + 128], block)
        scr[384:400, 384:512] = block
        split_rows(idx[3], scr, 0, 192, 0, keep, send, s)
        split_rows(idx[3], scr, 192, 192, 96, keep, send, s)
        split_rows(idx[3], scr, 384, 64, 192, keep, send, s)


def pair_kernel(keep, recv, mine, across):
    mine[...] = keep[0] + recv[0].astype(f32)
    across[...] = (keep[1] + recv[1].astype(f32)).astype(bf16)


def cp_split_kernel(idx, keep, recv, mine, sent):
    rows = mine.shape[0]
    low = pl.multiple_of((idx[2] & 1) * rows, 16)
    high = pl.multiple_of((1 - (idx[2] & 1)) * rows, 16)
    sent[...] = (keep[pl.ds(high, rows), :] + recv[pl.ds(high, rows), :].astype(f32)).astype(bf16)
    mine[...] = keep[pl.ds(low, rows), :] + recv[pl.ds(low, rows), :].astype(f32)


def add_kernel(mine, recv, out):
    out[...] = (mine[...].astype(f32) + recv[...].astype(f32)).astype(out.dtype)


def place(idx, whole, pieces):
    half, pair, sib, sib_pair = pieces
    rows = half.shape[0]
    low, c = idx[2] & 1, idx[3]
    for core, zlow, piece in ((c, low, half), (c, 1 - low, pair), (1 - c, low, sib), (1 - c, 1 - low, sib_pair)):
        whole[pl.ds(pl.multiple_of((core * 2 + zlow) * rows, 16), rows), :] = piece[...].astype(whole.dtype)


def send_out(pairs, sems):
    copies = [pltpu.make_async_copy(a, b, sems.at[k]) for k, (a, b) in enumerate(pairs)]
    for copy in copies:
        copy.start()
    for copy in copies:
        copy.wait()


def join_kernel(idx, half, pair, out):
    join_halves(idx[2] & 1, out, half, pair)


def spread_kernel(idx, mine, sibling, out, whole, sems):
    for core, rows in ((idx[3], mine), (1 - idx[3], sibling)):
        whole[pl.ds(pl.multiple_of(core * 384, 384), 384), :] = rows[...].astype(f32)
    send_out([(whole, out)], sems)


def spread_attention_kernel(idx, *refs):
    early, late = refs[0:4], refs[4:8]
    outs, (first, second, w_qkv, w_out, feat, b_qkv, b_feat, b_up, sems) = refs[8:14], refs[14:]
    place(idx, first, early)
    place(idx, second, late)
    for c in range(2):
        w_qkv[96 * c : 96 * c + 96, :] = first[192 * c : 192 * c + 96, :]
        w_out[96 * c : 96 * c + 96, :] = first[192 * c + 96 : 192 * c + 192, :]
        w_qkv[192 + 96 * c : 288 + 96 * c, :] = second[224 * c : 224 * c + 96, :]
        w_qkv[384 + 96 * c : 480 + 96 * c, :] = second[224 * c + 96 : 224 * c + 192, :]
    more = jnp.concatenate([second[192:224, :], second[416:448, :]], axis=0)
    feat[0] = more[:, 0:64]
    feat[1] = half_turn(more[:, 0:128])[:, 0:64]
    feat[2] = more[:, 128:192]
    sums = more[0:16, 256:384]
    turned = half_turn(sums)
    for k in range(3):
        b_qkv[k : k + 1, 0:128] = sums[2 * k : 2 * k + 1]
        b_qkv[k : k + 1, 128:192] = turned[2 * k + 1 : 2 * k + 2, 0:64]
    b_feat[...] = sums[6:9, 0:64]
    for t in range(6):
        b_up[128 * t : 128 * t + 128] = more[t : t + 1, 384:512].reshape(128)
    send_out(list(zip((w_qkv, w_out, feat, b_qkv, b_feat, b_up), outs)), sems)


def after(value, *deps):
    return lax.optimization_barrier((value,) + deps)[0]


def swap(value, axis, bit):
    count = lax.axis_size(axis)
    return jax.tree.map(
        lambda v: lax.ppermute(v, axis, [(i, i ^ bit) for i in range(count)]), value
    )


def diagonal(value):
    tp, cp = lax.axis_size("tp"), lax.axis_size("cp")
    pairs = [(t * cp + z, (t ^ 2) * cp + (z ^ 1)) for t in range(tp) for z in range(cp)]
    return lax.ppermute(value, ("tp", "cp"), pairs)


def rest_of_dp(value):
    bit = 2
    while bit < lax.axis_size("dp"):
        value = value + swap(value.astype(bf16), "dp", bit).astype(f32)
        bit *= 2
    return value


def shards(
    tokens, segment_ids, ln1_gain, ln1_bias, w_qkv, b_qkv, w_feat, b_feat, output_weight, b_out,
    ln2_gain, ln2_bias, w_up, b_up, w_down, b_down, cotangent,
):
    t = lax.axis_index("tp")
    z = lax.axis_index("cp")
    c = lax.axis_index("dp") & 1
    x, y = t & 1, t >> 1
    idx = jnp.stack([x, y, z, c, c, c, c, c]).astype(jnp.int32)
    tok = tokens.reshape(256, 768)
    cot_own = cotangent.reshape(256, 768)
    seg = segment_ids.reshape(1024)

    wq = jnp.transpose(w_qkv, (1, 2, 0)).reshape(576, 768)
    done, first_wait = [], []

    def run(kernel, outs, args, needs=(), **options):
        args = list(args)
        args[-1] = after(args[-1], *needs, *done, *first_wait)
        first_wait.clear()
        result = call(kernel, outs, args, **options)
        done[:] = [result[0]]
        return result

    def array(*shape, kind=bf16):
        return (shape, kind)

    rows_b, rows_f = array(256, 768), array(256, 768, kind=f32)
    part_b, part_f = array(128, 768), array(128, 768, kind=f32)
    head_rows, head_rows_f = array(6, 512, 128), array(6, 512, 128, kind=f32)

    n_own, buf, signed, flat, par, segc, segr, first_part, second_part = run(
        prep_kernel,
        [
            rows_b, array(336, 768), array(192, 128), array(16, 128, kind=f32), array(8, 768, kind=f32),
            array(512, 1, kind=f32), array(1, 512, kind=f32), array(224, 768), array(640, 768),
        ],
        [
            idx, tok, ln1_gain, ln1_bias, b_out, ln2_gain, ln2_bias, b_down, wq, w_feat, b_qkv, b_feat, b_up,
            segment_ids.reshape(1, 1024), output_weight, w_up, w_down,
        ],
        smem=1, hbm=16,
        scratch=[
            pltpu.VMEM((256, 768), bf16), [pltpu.VMEM((768,), f32)] * 7, pltpu.VMEM((3, 64, 64), bf16),
            pltpu.VMEM((3, 192), f32), pltpu.VMEM((3, 64), f32), pltpu.VMEM((1, 1024), jnp.int32),
            pltpu.SemaphoreType.DMA((17,)),
        ],
    )
    n_oth = swap(n_own, "tp", 1)
    buf_y = swap(buf, "tp", 2)
    buf_sib = swap(after(buf_y, n_oth), "dp", 1)
    first_mine = swap(after(first_part, buf_y), "tp", 2)
    ncat, u, fq, fk, va, arow, pay, pay_far, wx, wfe, bup = run(
        qkv_kernel,
        [
            array(512, 768), array(512, 1024), head_rows, head_rows, head_rows, array(6, 1, 128, kind=f32),
            PAY_OUT, PAY_OUT, array(2, 768, 768), array(2, 128, 384), array(2, 16, 128, kind=f32),
        ],
        [idx, seg, n_own, n_oth, wq, buf_y, buf_sib, signed, flat, par, segc],
        smem=2, scratch=[pltpu.VMEM((576, 768), bf16)],
    )
    around = [swap(pay, "tp", 2), swap(pay_far, "cp", 1), diagonal(pay_far)]
    first_pair = (first_mine, swap(after(first_mine, pay), "dp", 1))
    second_mine = swap(after(second_part, around[0]), "tp", 2)
    cot_oth = swap(after(cot_own, pay), "tp", 1)
    (numden,) = run(inner_kernel, [head_rows_f], [segc, segr, fq, fk, va])
    (state,) = run(
        functools.partial(send_state_kernel, True), [PAY_OUT], [idx, seg, pay_far, *around], smem=2, weight=1
    )
    carried = [*around, swap(state, "cp", 2)]
    att, mixed, paug, part_own, send_a, send_b, wo_oth = run(
        out_kernel,
        [head_rows_f, array(512, 512), array(6, 128, 128), rows_f, part_b, part_b, array(192, 768)],
        [idx, seg, *carried, numden, fq, arow, segc, output_weight, *first_pair],
        needs=(cot_oth,), smem=2, weight=0,
    )
    part_in = [swap(send_a, "tp", 1), swap(send_b, "tp", 1)]

    mid, n2_own = [None, None], [None, None]
    for k in range(2):
        mid[k], n2_own[k] = run(
            functools.partial(ln_two_kernel, k), [part_f, part_b], [tok, part_own, part_in[k], par],
            needs=(second_mine,), weight=4,
        )
    second_pair = (second_mine, swap(after(second_mine, n2_own[0]), "dp", 1))
    n2_oth = [swap(v, "tp", 1) for v in n2_own]
    units = array(128, 1536)
    v = types.SimpleNamespace(hid={}, gpre={}, gn2={}, gmid={}, vecs_two={}, gb={})
    sums = {n: types.SimpleNamespace() for n in range(4)}
    DOWN, UP, EARLY, LATE = range(4)

    def mlp_own():
        v.hid[2], v.gpre[2], v.gn2[2], v.up, v.down = run(mlp_own_kernel,
            [array(256, 1536), array(256, 1536), rows_f, array(768, 768), array(768, 768)],
            [idx, *n2_own, cot_own, w_up, w_down, *first_pair, *second_pair, bup], smem=1,
        )

    def mlp_part(k):
        v.hid[k], v.gpre[k], out = run(
            functools.partial(mlp_kernel, k), [units, units, part_b],
            [n2_oth[k], cot_oth, w_up, v.up, w_down, v.down, bup],
        )
        v.gn2[k] = swap(out, "tp", 1)


    def down_args():
        return [idx, v.hid[2], v.hid[0], v.hid[1], cot_own, cot_oth]

    def up_args():
        return [idx, *n2_own, *n2_oth, v.gpre[2], v.gpre[0], v.gpre[1]]

    def grad_send(name, grad, args):
        (send,) = run(functools.partial(mlp_send_kernel, grad), [array(2, 384, 768)], args, smem=1, weight=0)
        sums[name].dp = swap(send, "dp", 1)

    def grad_keep(name, grad, args):
        keep, across = run(functools.partial(mlp_keep_kernel, grad), [array(384, 768, kind=f32), array(384, 768)],
            args + [sums[name].dp], smem=1,
        )
        sums[name].y = keep, swap(across, "tp", 2)


    def ln_two_back(k):
        before = [v.vecs_two[0]] if k else []
        v.gmid[k], branch, v.vecs_two[k] = run(functools.partial(ln_two_back_kernel, k), [part_f, part_b, array(24, 128, kind=f32)],
            [mid[k], v.gn2[2], v.gn2[k], par, cot_own, *before], weight=4,
        )
        v.gb[k] = branch, swap(branch, "tp", 1)


    def down():
        v.down_own, part = run(down_kernel, [rows_f, rows_b], [v.hid[2], v.hid[0], v.hid[1], w_down, v.down]
        )
        v.down_in = swap(part, "tp", 1)

    def grad_mixed():
        own, oth = zip(v.gb[0], v.gb[1])
        v.gbcat, v.gna, pay_near, far = run(grad_mixed_kernel, [array(512, 768), head_rows, PAY_OUT, PAY_OUT],
            [idx, seg, *own, *oth, output_weight, wo_oth, att, fq, segc], smem=2,
        )
        v.around = [swap(pay_near, "tp", 2), swap(far, "cp", 1), diagonal(far)]
        v.far = far

    def key_back():
        v.gkf, v.gv = run(key_back_kernel, [head_rows_f, head_rows_f], [segc, segr, fq, fk, va, v.gna]
        )

    def gstate():
        (state,) = run(functools.partial(send_state_kernel, False), [PAY_OUT], [idx, seg, v.far, *v.around],
            smem=2, weight=4,
        )
        v.coming = [*v.around, swap(state, "cp", 2)]

    def query_back():
        v.gq, v.gpq = run(query_back_kernel, [head_rows, array(512, 512)],
            [idx, seg, segc, segr, fq, fk, va, v.gna, paug, wfe], smem=2,
        )

    def early_weights():
        keep, send = run(early_weights_kernel, [array(2, 192, 768, kind=f32), array(2, 192, 768)],
            [idx, ncat, v.gpq, mixed, v.gbcat], smem=1, scratch=[pltpu.VMEM((384, 768), f32)],
        )
        sums[EARLY].dp = keep, swap(send, "dp", 1)

    def qkv_back():
        v.gk, v.gpkv, v.gn1, oth = run(qkv_back_kernel, [head_rows, array(512, 1024), rows_f, rows_b],
            [idx, seg, *v.coming, segc, fk, va, v.gkf, v.gv, v.gpq, wfe, wx], smem=2,
        )
        v.gn1_in = swap(oth, "tp", 1)

    def late_weights():
        keep, send = run(late_weights_kernel, [array(2, 224, 768, kind=f32), array(2, 224, 768)],
            [idx, ncat, v.gpq, v.gpkv, u, v.gq, v.gk, v.gpre[2], v.gpre[0], v.gpre[1]],
            smem=1, scratch=[pltpu.VMEM((448, 768), f32)],
        )
        sums[LATE].dp = keep, swap(send, "dp", 1)

    def ln_one_back():
        v.d_tok, v.vecs = run(ln_one_back_kernel, [rows_f, array(40, 128, kind=f32)],
            [tok, v.gn1, v.gn1_in, par, v.gmid[0], v.gmid[1], v.vecs_two[1]],
        )

    def final():
        (v.out,) = run(final_kernel, [rows_b], [*mid, v.down_own, v.down_in, par])

    def pair(name):
        keep, recv = sums[name].dp
        rows = keep.shape[1]
        mine, across = run(pair_kernel, [array(rows, 768, kind=f32), array(rows, 768)], [keep, recv]
        )
        sums[name].y = mine, swap(across, "tp", 2)

    def split(name):
        keep, recv = sums[name].y
        rows = keep.shape[0] // 2
        if lax.axis_size("dp") > 2:
            keep, recv = rest_of_dp(keep + recv.astype(f32)), jnp.zeros_like(recv)
        mine, sent = run(cp_split_kernel, [array(rows, 768, kind=f32), array(rows, 768)], [idx, keep, recv],
            smem=1,
        )
        sums[name].z = mine, swap(sent, "cp", 1)

    def add(name):
        mine, recv = sums[name].z
        (half,) = run(add_kernel, [(mine.shape, bf16)], [mine, recv])
        sums[name].zz = half, swap(half, "cp", 2)

    def last(name):
        mine, recv = sums[name].zz
        (half,) = run(add_kernel, [(mine.shape, bf16)], [mine, recv])
        sums[name].half = half, swap(half, "cp", 1)

    def join(name):
        rows = sums[name].half[0].shape[0] * 2
        (mine,) = run(join_kernel, [array(rows, 768)], [idx, *sums[name].half], smem=1)
        sums[name].rows = mine, swap(mine, "dp", 1)

    def spread(name):
        (sums[name].sum,) = run(spread_kernel, [array(768, 768, kind=f32)], [idx, *sums[name].rows],
            smem=1, hbm_out=True, scratch=[pltpu.VMEM((768, 768), f32), pltpu.SemaphoreType.DMA((1,))],
        )

    def pieces(name):
        half, other = sums[name].half
        other = after(other, sums[UP].sum)
        return half, other, swap(half, "dp", 1), swap(other, "dp", 1)

    hops = [(axis, 1 << k) for axis in ("tp", "dp", "cp") for k in range(lax.axis_size(axis).bit_length() - 1)]

    def vec():
        if hops:
            pending = swap(v.vecs, *hops.pop(0))
            (v.vecs,) = run(add_kernel, [array(40, 128, kind=f32)], [v.vecs, pending])

    given = [(576, 768), (192, 768), (3, 64, 64), (3, 192), (3, 64), (768,)]

    def attention():
        while hops:
            vec()
        v.attention = run(spread_attention_kernel, [array(*shape, kind=f32) for shape in given],
            [idx, *pieces(EARLY), *pieces(LATE)], smem=1, hbm_out=True,
            scratch=[pltpu.VMEM((384, 768), f32), pltpu.VMEM((448, 768), f32)]
            + [pltpu.VMEM(shape, f32) for shape in given] + [pltpu.SemaphoreType.DMA((6,))],
        )

    mlp_own()
    mlp_part(0)
    mlp_part(1)
    grad_send(DOWN, down_grad, down_args())
    ln_two_back(0)
    grad_keep(DOWN, down_grad, down_args())
    grad_send(UP, up_grad, up_args())
    ln_two_back(1)
    grad_keep(UP, up_grad, up_args())
    grad_mixed()
    split(DOWN)
    key_back()
    gstate()
    query_back()
    add(DOWN)
    split(UP)
    qkv_back()
    early_weights()
    late_weights()
    pair(EARLY)
    pair(LATE)
    last(DOWN)
    add(UP)
    ln_one_back()
    split(EARLY)
    split(LATE)
    down()
    vec()
    join(DOWN)
    last(UP)
    vec()
    add(EARLY)
    add(LATE)
    vec()
    spread(DOWN)
    vec()
    last(EARLY)
    final()
    join(UP)
    last(LATE)
    spread(UP)
    attention()

    d_wq, d_w_out, d_feat, d_b_qkv, d_b_feat, d_b_up = v.attention
    vec_rows = v.vecs[:36].reshape(6, 768)
    return (
        v.out.reshape(tokens.shape),
        v.d_tok.reshape(tokens.shape),
        vec_rows[4],
        vec_rows[5],
        jnp.transpose(d_wq.reshape(3, 192, 768), (2, 0, 1)),
        d_b_qkv,
        d_feat,
        d_b_feat,
        d_w_out,
        vec_rows[0],
        vec_rows[1],
        vec_rows[2],
        sums[UP].sum,
        d_b_up,
        sums[DOWN].sum,
        vec_rows[3],
    )


def solution(mesh):
    rows = P(("cp", "tp"), "dp", None)
    placed = (
        rows, P("cp", "dp"), P(), P(), P(None, None, "tp"), P(None, "tp"), P("tp", None, None),
        P("tp", None), P("tp", None), P(), P(), P(), P(None, "tp"), P("tp"), P("tp", None), P(), rows,
    )
    given = (
        rows, rows, P(), P(), P(None, None, "tp"), P(None, "tp"), P("tp", None, None), P("tp", None),
        P("tp", None), P(), P(), P(), P(None, "tp"), P("tp"), P("tp", None), P(),
    )
    return jax.shard_map(shards, mesh=mesh, in_specs=placed, out_specs=given, check_vma=False)
```
